32 devices in a mesh: dp: 16 (over z, y, core), mod: 2 (over x).
Axes of the slice: x: 2, y: 2, z: 4, core: 2. Of those that a mesh axis runs over, the one named last changes fastest.
Arguments:
- tokens: bfloat16 [8192, 1152], P(('dp', 'mod')), may hold values from -6 to 6
- condition: bfloat16 [256, 1152], P('dp'), may hold values from -6 to 6
- lengths: int32 [64, 4], P(('dp', 'mod')), may hold values from 1 to 64, 128 in all within a row
- positions: int32 [2, 8192], P(None, ('dp', 'mod')), may hold values from 0 to 31
- query_gain: float32 [72], replicated, may hold values from 0.25 to 1.75
- key_gain: float32 [72], replicated, may hold values from 0.25 to 1.75
- attend_in: bfloat16 [1152, 3456], P('dp', 'mod'), may hold values from -0.1875 to 0.1875
- attend_out: bfloat16 [1152, 1152], P('dp', 'mod'), may hold values from -0.375 to 0.375
- feed_in: bfloat16 [1152, 6144], P('dp', 'mod'), may hold values from -0.1875 to 0.1875
- feed_out: bfloat16 [3072, 1152], P('dp', 'mod'), may hold values from -0.15625 to 0.15625
- modulate_weight: bfloat16 [1152, 6912], P('dp', 'mod'), may hold values from -0.25 to 0.25
- cotangent: bfloat16 [8192, 1152], P(('dp', 'mod')), may hold values from -6 to 6
Outputs:
- block_out: bfloat16 [8192, 1152], P(('dp', 'mod'))
- tokens_grad: float32 [8192, 1152], P(('dp', 'mod'))
- condition_grad: float32 [256, 1152], P('dp', 'mod')
- query_gain_grad: float32 [72], replicated
- key_gain_grad: float32 [72], replicated
- attend_in_grad: float32 [1152, 3456], P('dp', 'mod')
- attend_out_grad: float32 [1152, 1152], P('dp', 'mod')
- feed_in_grad: float32 [1152, 6144], P('dp', 'mod')
- feed_out_grad: float32 [3072, 1152], P('dp', 'mod')
- modulate_grad: float32 [1152, 6912], P('dp', 'mod')
The draws below stay inside these ranges and needn't reach their ends.
Inputs may be any that keep to these rules, and one draw needn't show every extreme that they name: `lengths`: row j lists in order the token counts of the 4 images packed into sequence j, whose conditioning vectors are condition rows j * 4 to j * 4 + 3; each row sums to 128 and holds one image of exactly 64 tokens. `positions`: a 2-D patch position (row, column) of each token on a grid of 32 x 32.
All inputs are finite; a program needn't handle non-finite values.
Results may differ from the reference program's by a relative error of at most 0.018.
Values may be sent and summed in bfloat16 or wider, within the bound.
No kernel may reach another device: no remote copies, remote signals or barrier semaphores. Data moves between devices by JAX's collectives and lax.ppermute only.
A program may use at most 256 MiB of HBM per device.

```python
import math
import jax
import jax.numpy as jnp
import numpy as np
from jax import lax

D = 1152
HEAD = 72
FF = 3072
SEQ = 128
ITEMS_SEQ = 4
GRID = 32
TOKENS = 8192
SEQS = 64
ITEMS = 256


def place_ends(array, stream_key, low, high):
    spot = [jax.random.randint(jax.random.fold_in(stream_key, axis), (), 0, length) for axis, length in enumerate(array.shape)]
    longest = array.shape.index(max(array.shape))
    neighbour = spot[:longest] + [(spot[longest] + 1) % array.shape[longest]] + spot[longest + 1:]
    return array.at[tuple(spot)].set(low).at[tuple(neighbour)].set(high)


def strengthened(entries, stream_key, source, target, parts, factor):
    def block_of(axis_at):
        return (jnp.arange(entries.shape[axis_at]) // (entries.shape[axis_at] // parts)).reshape((-1,) + (1,) * (entries.ndim - 1 - axis_at))

    first = jax.random.permutation(stream_key, parts)[block_of(target)]
    other_side = (block_of(target) + parts // 2) % parts
    return jnp.where((block_of(source) == first) | (block_of(source) == other_side), factor * entries, entries)


def levels(stream_key, extent, shards, smallest, top_value):
    def one(axis_at, parts):
        heights = jax.random.uniform(jax.random.fold_in(jax.random.fold_in(stream_key, 6), axis_at), (parts,), jnp.float32, smallest / len(shards), top_value / len(shards))
        return jnp.repeat(jnp.exp(heights), extent[axis_at] // parts).reshape((-1,) + (1,) * (len(extent) - axis_at - 1))

    factor_of = one(*shards[0])
    for cut in shards[1:]:
        factor_of = factor_of * one(*cut)
    return factor_of


def length_profile(count, total, reach, slope):
    loads = [(1 << 20) // math.isqrt(standing ** slope) + 1 for standing in range(2, count + 1)]
    spare, counts = total - reach - (count - 1), [1] * (count - 1)
    while spare > 0:
        movable = [i for i in range(count - 1) if counts[i] < reach]
        mass, remaining = sum([loads[i] for i in movable]), spare
        for i in movable:
            more = min(reach - counts[i], max(1, remaining * loads[i] // mass), spare)
            counts[i] = counts[i] + more
            spare = spare - more
    return np.array([reach] + counts)


def uneven(stream_key, amount, total, limit, lean):
    if amount == 2:
        one = jax.random.randint(stream_key, (), max(1, total - limit), min(limit, total - 1) + 1)
        return jnp.stack([one, total - one])
    sizes = jnp.asarray(length_profile(amount, total, limit, lean), jnp.int32)
    pairs = (amount - 1) // 2
    donor, taker = sizes[1:1 + 2 * pairs:2], sizes[2:2 + 2 * pairs:2]
    room = jnp.minimum(donor - 1, limit - taker)
    moved = jax.random.randint(jax.random.fold_in(stream_key, 1), (pairs,), 0, 1 << 20) % (room + 1)
    sizes = sizes.at[1:1 + 2 * pairs:2].set(donor - moved).at[2:2 + 2 * pairs:2].set(taker + moved)
    return sizes[jax.random.permutation(jax.random.fold_in(stream_key, 2), amount)]


def noise(own_key, dims, scale, reach, pieces=(), kind=jnp.bfloat16):
    entries = jax.random.normal(own_key, dims, jnp.float32) * scale
    if len(pieces) > 0:
        entries = levels(own_key, dims, pieces, -0.22, 0.18) * entries
    return jnp.clip(entries, min=-reach, max=reach).astype(kind)


def heavy_noise(stream_key, shape, scale, limit, pieces, heavy, held_as=jnp.bfloat16):
    array = scale * jax.random.normal(stream_key, shape, jnp.float32)
    if pieces:
        array = array * levels(stream_key, shape, pieces, -0.22, 0.18)
    return jnp.clip(strengthened(array, jax.random.fold_in(stream_key, 3), *heavy), -limit, limit).astype(held_as)


def setup_inputs(seed: int = 0) -> dict:
    arg_keys = jax.random.split(jax.random.key(seed), 13)
    tokens = heavy_noise(arg_keys[0], (TOKENS, D), 1.0, 6.0, ((0, 32),), (0, 1, 32, 2.75))
    condition = noise(arg_keys[1], (ITEMS, D), 1.0, 6.0, ((0, 16),))
    lengths = jax.vmap(lambda own: uneven(own, ITEMS_SEQ, SEQ, SEQ // 2, 2))(jax.random.split(arg_keys[2], SEQS)).reshape((SEQS, ITEMS_SEQ)).astype(jnp.int32)
    positions = place_ends(jax.random.randint(arg_keys[3], (2, TOKENS), 0, GRID), jax.random.fold_in(arg_keys[3], 1), 0, GRID - 1).astype(jnp.int32)
    query_gain = jnp.clip(1.0 + 0.15 * jax.random.normal(arg_keys[4], (HEAD,), jnp.float32), 0.25, 1.75)
    key_gain = jnp.clip(1.0 + 0.15 * jax.random.normal(arg_keys[5], (HEAD,), jnp.float32), 0.25, 1.75)
    attend_in = noise(arg_keys[6], (D, 3 * D), D ** -0.5, 0.1875, ((0, 16), (1, 2)))
    attend_out = noise(arg_keys[7], (D, D), (D // 4) ** -0.5, 0.375, ((0, 16), (1, 2)))
    feed_in = noise(arg_keys[8], (D, 2 * FF), D ** -0.5, 0.1875, ((0, 16), (1, 2)))
    feed_out = noise(arg_keys[9], (FF, D), (FF // 2) ** -0.5, 0.15625, ((0, 16), (1, 2)))
    modulate_weight = noise(arg_keys[10], (D, 6 * D), (D // 2) ** -0.5, 0.25, ((0, 16), (1, 2)))
    cotangent = noise(arg_keys[11], (TOKENS, D), 1.0, 6.0, ((0, 32),))
    return {"tokens": tokens, "condition": condition, "lengths": lengths, "positions": positions, "query_gain": query_gain, "key_gain": key_gain, "attend_in": attend_in, "attend_out": attend_out, "feed_in": feed_in, "feed_out": feed_out, "modulate_weight": modulate_weight, "cotangent": cotangent}


HIGHEST = lax.Precision.HIGHEST

@jax.custom_vjp
def low(v):
    return lax.optimization_barrier(v.astype(jnp.bfloat16)).astype(jnp.float32)

@jax.custom_vjp
def low_back(v):
    return v

def low_keep(v):
    return (low(v), None)

def low_pass(kept, grad):
    return (grad,)

def back_keep(v):
    return (v, None)

def back_low(kept, grad):
    return (low(grad),)
low.defvjp(low_keep, low_pass)
low_back.defvjp(back_keep, back_low)

def item_index(lengths_row, count):
    ends = jnp.cumsum(lengths_row, dtype=jnp.int32)
    places = jnp.arange(count, dtype=jnp.int32)
    return lax.optimization_barrier(jnp.sum((places[:, None] >= ends[None, :]).astype(jnp.int32), axis=1, dtype=jnp.int32))

def rope_tables(places, head):
    quarter = head // 4
    index = jnp.arange(head, dtype=jnp.int32)
    freq = jnp.power(10000.0, -(index % quarter).astype(jnp.float32) / quarter)
    which = index // (head // 2)
    spot = jnp.where(which[None, :] == 0, places[0][:, None], places[1][:, None]).astype(jnp.float32)
    angle = spot * freq[None, :]
    return (jnp.cos(angle), jnp.sin(angle))

def rotate(values):
    shape = values.shape
    halves = values.reshape(shape[:-1] + (2, 2, shape[-1] // 4))
    turned = jnp.concatenate([-halves[..., 1:2, :], halves[..., 0:1, :]], axis=-2)
    return turned.reshape(shape)

def layer_norm(values):
    average = lax.optimization_barrier(jnp.mean(values, axis=-1, keepdims=True))
    centred = values - average
    spread = lax.optimization_barrier(jnp.mean(centred * centred, axis=-1, keepdims=True))
    return centred * lax.rsqrt(spread + 1e-06)

def rms_gain(values, gain):
    return values * lax.rsqrt(lax.optimization_barrier(jnp.mean(values * values, axis=-1, keepdims=True)) + 1e-06) * gain

def sequence_forward(inputs, mods, lengths_row, places, gain_q, gain_k, weight_in, weight_out, weight_up, weight_down):
    count, width = inputs.shape
    head = gain_q.shape[0]
    heads = width // head
    items = item_index(lengths_row, count)
    onehot = (items[:, None] == jnp.arange(lengths_row.shape[0], dtype=jnp.int32)[None, :]).astype(jnp.float32)
    token_mod = jnp.dot(onehot, mods, precision=HIGHEST)
    shift_attend, scale_attend, gate_attend, shift_feed, scale_feed, gate_feed = jnp.split(token_mod, 6, axis=1)
    modded_one = low(layer_norm(inputs) * (1.0 + scale_attend) + shift_attend)
    projected = low_back(jnp.dot(modded_one, weight_in, precision=HIGHEST)).reshape(count, 3, heads, head)
    cosine, sine = rope_tables(places, head)
    cosine = cosine[:, None, :]
    sine = sine[:, None, :]
    query_norm = rms_gain(projected[:, 0], gain_q)
    key_norm = rms_gain(projected[:, 1], gain_k)
    query_rot = low(query_norm * cosine + rotate(query_norm) * sine)
    key_rot = low(key_norm * cosine + rotate(key_norm) * sine)
    values_low = low(projected[:, 2])
    scores = low_back(jnp.einsum('shd,thd->hst', query_rot, key_rot, precision=HIGHEST) * head ** (-0.5))
    same_item = items[:, None] == items[None, :]
    scores = jnp.where(same_item[None], scores, -1e+30)
    probs = low(jax.nn.softmax(scores, axis=-1))
    mixed = jnp.einsum('hst,thd->shd', probs, values_low, precision=HIGHEST).reshape(count, width)
    mixed = low(low_back(mixed))
    attended = low_back(jnp.dot(mixed, weight_out, precision=HIGHEST))
    resid = inputs + gate_attend * attended
    modded_two = low(layer_norm(resid) * (1.0 + scale_feed) + shift_feed)
    gate_up = low_back(jnp.dot(modded_two, weight_up, precision=HIGHEST))
    gate_part, up_part = jnp.split(gate_up, 2, axis=1)
    hidden = low(jax.nn.silu(gate_part) * up_part)
    fed = low_back(jnp.dot(hidden, weight_down, precision=HIGHEST))
    return resid + gate_feed * fed

def reference(tokens, condition, lengths, positions, query_gain, key_gain, attend_in, attend_out, feed_in, feed_out, modulate_weight, cotangent):
    group = math.gcd(SEQS, max(1, 4096 // SEQ))
    blocks = SEQS // group
    lengths_blocks = lengths.reshape(blocks, group, ITEMS_SEQ)
    places_blocks = jnp.transpose(positions.reshape(2, SEQS, SEQ), (1, 0, 2)).reshape(blocks, group, 2, SEQ)

    def forward(inputs, cond_in, gain_q, gain_k, weight_in, weight_out, weight_up, weight_down, weight_mod):
        mods = low_back(low(jnp.dot(low(jax.nn.silu(cond_in)), weight_mod, precision=HIGHEST)))
        mods_blocks = mods.reshape(blocks, group, ITEMS_SEQ, 6 * D)
        input_blocks = inputs.reshape(blocks, group, SEQ, D)

        def one_block(packed):
            block_in, block_mods, block_lengths, block_places = packed
            return jax.vmap(sequence_forward, in_axes=(0, 0, 0, 0, None, None, None, None, None, None))(block_in, block_mods, block_lengths, block_places, gain_q, gain_k, weight_in, weight_out, weight_up, weight_down)
        result = lax.map(jax.checkpoint(one_block), (input_blocks, mods_blocks, lengths_blocks, places_blocks))
        return result.reshape(TOKENS, D)
    output, pullback = jax.vjp(forward, tokens.astype(jnp.float32), condition.astype(jnp.float32), query_gain, key_gain, attend_in.astype(jnp.float32), attend_out.astype(jnp.float32), feed_in.astype(jnp.float32), feed_out.astype(jnp.float32), modulate_weight.astype(jnp.float32))
    grads = pullback(cotangent.astype(jnp.float32))
    return (output.astype(jnp.bfloat16), grads[0], grads[1], grads[2], grads[3], grads[4], grads[5], grads[6], grads[7], grads[8])
```

```python
import functools

import jax
import jax.numpy as jnp
from jax import lax
from jax.experimental import pallas as pl
from jax.experimental.pallas import tpu as pltpu
from jax.sharding import PartitionSpec as P

HIGHEST = lax.Precision.HIGHEST
BF = jnp.bfloat16
F32 = jnp.float32
VMEM_LIMIT = 48 * 1024 * 1024


def layer_norm(values):
    average = jnp.mean(values, axis=-1, keepdims=True)
    centred = values - average
    spread = jnp.mean(centred * centred, axis=-1, keepdims=True)
    inverse = lax.rsqrt(spread + 1e-06)
    return (centred * inverse, inverse)


def norm_back(upstream, normed, inverse):
    first = jnp.mean(upstream, axis=-1, keepdims=True)
    second = jnp.mean(upstream * normed, axis=-1, keepdims=True)
    return inverse * (upstream - first - normed * second)


def dot(left, right, left_dim=1, right_dim=0):
    return lax.dot_general(
        left, right, (((left_dim,), (right_dim,)), ((), ())), preferred_element_type=F32
    )


def turned(values, first):
    quarter = values.shape[0] // 4
    ahead = pltpu.roll(values, values.shape[0] - quarter, 0)
    behind = pltpu.roll(values, quarter, 0)
    return jnp.where(first, ahead, behind)


def rms(values):
    return lax.rsqrt(jnp.mean(values * values, axis=0, keepdims=True) + 1e-06)


def scores_t(key_rot, query_rot, same, scale):
    raw = dot(key_rot, query_rot, 0, 0) * scale
    return jnp.where(same, raw, -1e30)


def softmax_t(scores):
    peak = jnp.max(scores, axis=0, keepdims=True)
    exponent = jnp.exp(scores - peak)
    return exponent / jnp.sum(exponent, axis=0, keepdims=True)


def first_mask(head, count):
    row = lax.broadcasted_iota(jnp.int32, (head, count), 0)
    return lax.rem(row, head // 2) < head // 4


def attend_forward_kernel(
    heads, head, modded_ref, weight_ref, cos_ref, sin_ref, qg_ref, kg_ref, row_ref, col_ref,
    raw_ref, low_ref, mixed_ref,
):
    count = modded_ref.shape[0]
    own = heads * head
    projected = jnp.dot(modded_ref[...], weight_ref[...], preferred_element_type=F32).T
    raw_ref[0] = projected[: 2 * own]
    values = projected[2 * own :].astype(BF)
    low_ref[0] = values
    same = col_ref[0] == row_ref[0]
    first = first_mask(head, count)
    cosine, sine = cos_ref[0], sin_ref[0]
    scale = head ** (-0.5)

    def rotated(raw, gain):
        normed = raw * rms(raw) * gain
        return (normed * cosine + turned(normed, first) * sine).astype(BF)

    for h in range(heads):
        query_rot = rotated(projected[h * head : (h + 1) * head], qg_ref[...])
        key_rot = rotated(projected[own + h * head : own + (h + 1) * head], kg_ref[...])
        prob = softmax_t(scores_t(key_rot, query_rot, same, scale)).astype(BF)
        mixed = dot(values[h * head : (h + 1) * head], prob)
        mixed_ref[h * head : (h + 1) * head, :] = mixed.astype(BF)


def attend_backward_kernel(
    heads, head, grad_ref, weight_ref, raw_ref, low_ref, cos_ref, sin_ref, qg_ref, kg_ref, row_ref,
    col_ref, out_ref, qgg_ref, kgg_ref, held_ref,
):
    count = grad_ref.shape[0]
    own = heads * head
    mixed_grad = dot(weight_ref[...], grad_ref[...], 1, 1).astype(BF)
    same = col_ref[0] == row_ref[0]
    first = first_mask(head, count)
    cosine, sine = cos_ref[0], sin_ref[0]
    scale = head ** (-0.5)

    @pl.when(pl.program_id(0) == 0)
    def _():
        qgg_ref[...] = jnp.zeros_like(qgg_ref)
        kgg_ref[...] = jnp.zeros_like(kgg_ref)

    def rotated(raw, gain):
        inverse = rms(raw)
        normed = raw * inverse * gain
        return inverse, (normed * cosine + turned(normed, first) * sine).astype(BF)

    def back(rot_grad, raw, inverse, gain):
        norm_grad = rot_grad * cosine + turned(rot_grad * sine, first)
        gain_grad = norm_grad * raw * inverse
        scaled = norm_grad * gain
        inner = jnp.mean(scaled * raw, axis=0, keepdims=True)
        return inverse * scaled - raw * (inverse * inverse * inverse * inner), gain_grad

    query_total = jnp.zeros((head, count), F32)
    key_total = jnp.zeros((head, count), F32)
    for h in range(heads):
        rows = slice(h * head, (h + 1) * head)
        query_raw = raw_ref[0, h * head : (h + 1) * head]
        key_raw = raw_ref[0, own + h * head : own + (h + 1) * head]
        values = low_ref[0, h * head : (h + 1) * head]
        upstream = mixed_grad[rows]
        query_inverse, query_rot = rotated(query_raw, qg_ref[...])
        key_inverse, key_rot = rotated(key_raw, kg_ref[...])
        prob = softmax_t(scores_t(key_rot, query_rot, same, scale))
        prob_grad = dot(values, upstream, 0, 0)
        inner = jnp.sum(prob * prob_grad, axis=0, keepdims=True)
        score_grad = (prob * (prob_grad - inner)).astype(BF)
        query_rot_grad = dot(key_rot, score_grad) * scale
        key_rot_grad = dot(query_rot, score_grad, 1, 1) * scale
        values_grad = dot(upstream, prob.astype(BF), 1, 1)
        query_grad, query_part = back(query_rot_grad, query_raw, query_inverse, qg_ref[...])
        key_grad, key_part = back(key_rot_grad, key_raw, key_inverse, kg_ref[...])
        query_total += query_part
        key_total += key_part
        held_ref[h * head : (h + 1) * head, :] = query_grad
        held_ref[own + h * head : own + (h + 1) * head, :] = key_grad
        held_ref[2 * own + h * head : 2 * own + (h + 1) * head, :] = values_grad
    qgg_ref[...] += query_total
    kgg_ref[...] += key_total
    out_ref[...] = held_ref[...].T.astype(BF)


def whole_spec(shape):
    return pl.BlockSpec(shape, lambda i: (0,) * len(shape))


def lead_spec(shape):
    return pl.BlockSpec((1,) + shape[1:], lambda i: (i,) + (0,) * (len(shape) - 1))


def attend_forward(modded, weight, cosine, sine, qg, kg, row, col, heads):
    seqs, head, count = cosine.shape
    width = modded.shape[1]
    own = heads * head
    flops = 2 * seqs * count * (width * 3 * own + 2 * count * own)
    return pl.pallas_call(
        functools.partial(attend_forward_kernel, heads, head),
        grid=(seqs,),
        in_specs=[
            pl.BlockSpec((count, width), lambda i: (i, 0)),
            whole_spec(weight.shape),
            lead_spec(cosine.shape),
            lead_spec(sine.shape),
            whole_spec(qg.shape),
            whole_spec(kg.shape),
            lead_spec(row.shape),
            lead_spec(col.shape),
        ],
        out_specs=[
            lead_spec((seqs, 2 * own, count)),
            lead_spec((seqs, own, count)),
            pl.BlockSpec((own, count), lambda i: (0, i)),
        ],
        out_shape=[
            jax.ShapeDtypeStruct((seqs, 2 * own, count), F32),
            jax.ShapeDtypeStruct((seqs, own, count), BF),
            jax.ShapeDtypeStruct((own, seqs * count), BF),
        ],
        compiler_params=pltpu.CompilerParams(vmem_limit_bytes=VMEM_LIMIT),
        cost_estimate=pl.CostEstimate(
            flops=flops, bytes_accessed=10 * 2**20, transcendentals=seqs * heads * count * count
        ),
        name="attend_forward",
    )(modded, weight, cosine, sine, qg, kg, row, col)


def attend_backward(grad, weight, raw, low, cosine, sine, qg, kg, row, col, heads):
    seqs, head, count = cosine.shape
    width = grad.shape[1]
    own = heads * head
    flops = 2 * seqs * count * (width * own + 5 * count * own)
    return pl.pallas_call(
        functools.partial(attend_backward_kernel, heads, head),
        grid=(seqs,),
        in_specs=[
            pl.BlockSpec((count, width), lambda i: (i, 0)),
            whole_spec(weight.shape),
            lead_spec(raw.shape),
            lead_spec(low.shape),
            lead_spec(cosine.shape),
            lead_spec(sine.shape),
            whole_spec(qg.shape),
            whole_spec(kg.shape),
            lead_spec(row.shape),
            lead_spec(col.shape),
        ],
        out_specs=[
            pl.BlockSpec((count, 3 * own), lambda i: (i, 0)),
            whole_spec((head, count)),
            whole_spec((head, count)),
        ],
        out_shape=[
            jax.ShapeDtypeStruct((seqs * count, 3 * own), BF),
            jax.ShapeDtypeStruct((head, count), F32),
            jax.ShapeDtypeStruct((head, count), F32),
        ],
        scratch_shapes=[pltpu.VMEM((3 * own, count), F32)],
        compiler_params=pltpu.CompilerParams(vmem_limit_bytes=VMEM_LIMIT),
        cost_estimate=pl.CostEstimate(
            flops=flops, bytes_accessed=10 * 2**20, transcendentals=seqs * heads * count * count
        ),
        name="attend_backward",
    )(grad, weight, raw, low, cosine, sine, qg, kg, row, col)


def body(
    tokens,
    condition,
    lengths,
    positions,
    query_gain,
    key_gain,
    attend_in,
    attend_out,
    feed_in,
    feed_out,
    modulate_weight,
    cotangent,
):
    ndp, nmod = lax.axis_size("dp"), lax.axis_size("mod")
    planes = ndp // 2
    dp, mod = lax.axis_index("dp"), lax.axis_index("mod")
    core, plane, side = dp % 2, dp // 2, mod % 2
    own_seqs, items_seq = lengths.shape
    own_count, width = tokens.shape
    count = own_count // own_seqs
    head = query_gain.shape[0]
    heads_all = width // head
    heads = heads_all // 4
    cls = 2 * side + core
    own_items = own_seqs * items_seq
    dp_items = condition.shape[0]
    ringed = nmod == 2 and attend_out.shape[0] == head
    hid = feed_out.shape[0] // 2

    def swap_core(value):
        return lax.ppermute(value, "dp", [(i, i ^ 1) for i in range(ndp)])

    def swap_side(value):
        return lax.ppermute(value, "mod", [(i, i ^ 1) for i in range(nmod)])

    def pick(which, pair0, pair1):
        return jnp.where(which == 0, pair0, pair1)

    def ordered(which, own, other):
        return pick(which, own, other), pick(which, other, own)

    half = planes // 2

    def plane_of(ring):
        ring = lax.rem(ring + 2 * planes, planes)
        return jnp.where(ring < half, 2 * ring, 2 * (planes - 1 - ring) + 1)

    place = jnp.where(plane % 2 == 0, plane // 2, planes - 1 - plane // 2)

    def static_plane(ring):
        ring %= planes
        return 2 * ring if ring < half else 2 * (planes - 1 - ring) + 1

    def hop(value, step):
        pairs = [
            (2 * static_plane(r) + c, 2 * static_plane(r + step) + c)
            for r in range(planes)
            for c in range(2)
        ]
        return lax.ppermute(value, "dp", pairs)

    def ring_gather(block, slot=lambda index: index):
        out = jnp.zeros((planes,) + block.shape, block.dtype)
        cut = block.shape[0] // 32 * 16

        def put(out, piece, ring, row=0):
            start = (slot(plane_of(ring)), row) + (0,) * (block.ndim - 1)
            return lax.dynamic_update_slice(out, piece[None], start[: block.ndim + 1])

        out = put(out, block, place)
        ahead = behind = block
        for step in range(1, half):
            ahead, behind = hop(ahead, 1), hop(behind, -1)
            out = put(out, ahead, place - step)
            out = put(out, behind, place + step)
        ahead, behind = hop(ahead[:cut], 1), hop(behind[cut:], -1)
        out = put(out, ahead, place - half)
        return put(out, behind, place + half, cut)

    def ring_scatter(blocks, slot=lambda index: index):
        rows = blocks.shape[1]
        cut = rows // 32 * 16

        def take(ring, row, size):
            start = (slot(plane_of(ring)), row) + (0,) * (blocks.ndim - 2)
            return lax.dynamic_slice(blocks, start, (1, size) + blocks.shape[2:])[0]

        def plus(left, right):
            return (left.astype(F32) + right.astype(F32)).astype(BF)

        ahead = hop(take(place + half, 0, cut), 1)
        behind = hop(take(place - half, cut, rows - cut), -1)
        for step in range(half - 1, 0, -1):
            mine_ahead, mine_behind = take(place + step, 0, rows), take(place - step, 0, rows)
            if step == half - 1:
                ahead = jnp.concatenate([plus(mine_ahead[:cut], ahead), mine_ahead[cut:]], 0)
                behind = jnp.concatenate([mine_behind[:cut], plus(mine_behind[cut:], behind)], 0)
            else:
                ahead, behind = plus(mine_ahead, ahead), plus(mine_behind, behind)
            ahead, behind = hop(ahead, 1), hop(behind, -1)
        return take(place, 0, rows).astype(F32) + ahead.astype(F32) + behind.astype(F32)

    def spread_columns(parts):
        keep = pick(side, parts[0], parts[1])
        came = swap_side(pick(side, parts[1], parts[0]))
        both = jnp.concatenate(ordered(side, keep, came), axis=-1)
        keep = pick(core, both[0], both[1])
        came = swap_core(pick(core, both[1], both[0]))
        return jnp.concatenate(ordered(core, keep, came), axis=0)

    def unspread_columns(summed):
        rows, k = summed.shape[0] // 2, summed.shape[1] // 2
        top, low = summed[:rows], summed[rows:]
        came = swap_core(pick(core, low, top))
        both = jnp.stack(ordered(core, pick(core, top, low), came))
        left, right = both[:, :, :k], both[:, :, k:]
        came = swap_side(pick(side, right, left))
        return jnp.stack(ordered(side, pick(side, left, right), came))

    def gather_whole(weight):
        return lax.all_gather(
            lax.all_gather(weight, "mod", axis=1, tiled=True), "dp", axis=0, tiled=True
        )

    def scatter_whole(padded):
        padded = lax.psum_scatter(padded.astype(BF), "mod", scatter_dimension=1, tiled=True)
        return lax.psum_scatter(padded, "dp", scatter_dimension=0, tiled=True).astype(F32)

    def stack_other_core(value):
        return jnp.stack(ordered(core, value, swap_core(value)))

    def group(value):
        first = jnp.stack([value, swap_side(value)])
        return jnp.concatenate([first, swap_core(first)])

    whole_count = lengths.size + positions.size
    small = jnp.concatenate([lengths.reshape(-1), positions.reshape(-1)])
    small = group(small)
    lengths_g = small[:, : lengths.size].reshape(4 * own_seqs, items_seq)
    places_g = small[:, lengths.size : whole_count].reshape(4, 2, own_seqs, count)
    places_g = jnp.swapaxes(places_g, 1, 2).reshape(4 * own_seqs, 2, count)
    seqs = 4 * own_seqs

    cond_float = condition.astype(F32)
    silu_cond = jax.nn.silu(cond_float).astype(BF)
    silu_rows = lax.all_to_all(silu_cond, "dp", split_axis=1, concat_axis=0, tiled=True)
    partial = dot(silu_rows, modulate_weight)
    mod_cols = partial.shape[1]
    if ringed:
        partial = partial.reshape(planes, 2 * dp_items, 2, mod_cols // 2)
        left, right = partial[:, :, 0], partial[:, :, 1]
        came = swap_core(pick(core, right, left).astype(BF))
        kept = (pick(core, left, right) + came.astype(F32)).astype(BF)
        mods = ring_scatter(kept).astype(BF)
        mods = jnp.concatenate(ordered(core, mods, swap_core(mods)), axis=1)
        mods = jnp.concatenate(ordered(side, mods, swap_side(mods)), axis=1)
    else:
        mods = lax.psum_scatter(partial, "dp", scatter_dimension=0, tiled=True).astype(BF)
        mods = lax.all_gather(mods, "mod", axis=1, tiled=True)
        mods = stack_other_core(mods).reshape(2 * dp_items, 6 * width)

    columns_in = attend_in.shape[1]
    if ringed:
        parts = attend_in.reshape(head, columns_in // (4 * head), 4, head)
        parts = jnp.transpose(parts, (2, 0, 1, 3)).reshape(2, 2, head, columns_in // 4)
        w_in = ring_gather(spread_columns(parts)).reshape(width, 3 * heads * head)
        w_out = ring_gather(attend_out, lambda index: (index % 2) * half + index // 2)
        rows = feed_in.shape[0]
        parts = feed_in.reshape(rows, planes, 2, 2, hid)
        parts = jnp.transpose(parts, (3, 2, 0, 1, 4)).reshape(2, 2, rows, planes * hid)
        w_up = ring_gather(spread_columns(parts)).reshape(width, 2 * planes * hid)
        keep = pick(side, feed_out[:hid], feed_out[hid:])
        came = swap_side(pick(side, feed_out[hid:], feed_out[:hid]))
        w_down = jnp.concatenate(ordered(side, keep, came), axis=1)
        w_down = ring_gather(w_down).reshape(planes * hid, width)
        w_out = w_out.reshape(2, half * head, width // 2)
        w_out = jnp.concatenate(ordered(side, w_out, swap_side(w_out)), axis=2)
        w_out = jnp.stack(ordered(core, w_out, swap_core(w_out)), axis=1)
        w_out = w_out.reshape(4, heads * head, width)
    else:
        w_in = gather_whole(attend_in).reshape(width, 3 * heads, 4, head)
        w_in = lax.dynamic_index_in_dim(w_in, cls, 2, False).reshape(width, 3 * heads * head)
        w_out = gather_whole(attend_out).reshape(heads, 4, head, width)
        w_out = jnp.swapaxes(w_out, 0, 1).reshape(4, heads * head, width)
        share = 2 * core + side
        w_up = gather_whole(feed_in).reshape(width, 2 * planes, 4, hid)
        w_up = lax.dynamic_index_in_dim(w_up, share, 2, False).reshape(width, 2 * planes * hid)
        w_down = gather_whole(feed_out).reshape(planes, 4, hid, width)
        w_down = lax.dynamic_index_in_dim(w_down, share, 1, False).reshape(planes * hid, width)
    hidden_units = planes * hid

    inputs = group(tokens).reshape(4 * own_count, width).astype(F32)
    upstream = group(cotangent).reshape(4 * own_count, width).astype(F32)

    ends = jnp.cumsum(lengths_g, axis=1, dtype=jnp.int32)
    spots = jnp.arange(count, dtype=jnp.int32)
    items = jnp.sum(
        (spots[None, :, None] >= ends[:, None, :]).astype(jnp.int32), axis=2, dtype=jnp.int32
    )
    rel = jnp.arange(4, dtype=jnp.int32)
    base = (core ^ (rel // 2)) * dp_items + (mod ^ (rel % 2)) * own_items
    base = base[:, None] + jnp.arange(own_seqs, dtype=jnp.int32)[None, :] * items_seq
    index = (base.reshape(seqs, 1) + items).reshape(-1)
    members = index[:, None] == jnp.arange(2 * dp_items, dtype=jnp.int32)[None, :]
    members = members.astype(BF)
    own_index = jnp.arange(own_seqs, dtype=jnp.int32)[:, None] * items_seq + items[:own_seqs]
    own_members = own_index.reshape(-1)[:, None] == jnp.arange(own_items, dtype=jnp.int32)[None, :]
    own_members = own_members.astype(F32)

    def token_mod(block):
        return dot(members, mods[:, block * width : (block + 1) * width])

    shift_attend, scale_attend, gate_attend, shift_feed, scale_feed, gate_feed = (
        token_mod(block) for block in range(6)
    )

    quarter = head // 4
    entry = jnp.arange(head, dtype=jnp.int32)
    freq = jnp.power(10000.0, -(entry % quarter).astype(F32) / quarter)
    spot = jnp.where(
        (entry // (head // 2))[None, :, None] == 0, places_g[:, 0:1, :], places_g[:, 1:2, :]
    ).astype(F32)
    angle = spot * freq[None, :, None]
    cosine = jnp.cos(angle)
    sine = jnp.sin(angle)
    sine = jnp.where((entry % (head // 2) < quarter)[None, :, None], -sine, sine)
    qg = jnp.broadcast_to(query_gain[:, None], (head, count))
    kg = jnp.broadcast_to(key_gain[:, None], (head, count))
    item_row, item_col = items[:, None, :], items[:, :, None]

    normed_one, inverse_one = layer_norm(inputs)
    modded_one = (normed_one * (1.0 + scale_attend) + shift_attend).astype(BF)
    raw, low, mixed = attend_forward(
        modded_one, w_in, cosine, sine, qg, kg, item_row, item_col, heads
    )
    mixed_all = jnp.zeros((4,) + mixed.shape, BF)
    pair = jnp.stack([mixed, swap_side(mixed)])
    both = jnp.concatenate([pair, swap_core(pair)])
    both = both.reshape(4, heads * head, 4, own_count)
    for other in range(4):
        block = both[other]
        if other & 1:
            block = block.reshape(-1, 2, 2, own_count)[:, :, ::-1]
        if other & 2:
            block = block.reshape(-1, 2, 2, own_count)[:, ::-1]
        mixed_all = lax.dynamic_update_slice(
            mixed_all, block.reshape((1,) + mixed.shape), ((2 * (side ^ (other & 1))) + (core ^ (other >> 1)), 0, 0)
        )
    attended = dot(mixed_all.reshape(width, -1), w_out.reshape(width, width), 0, 0)
    resid = inputs + gate_attend * attended
    normed_two, inverse_two = layer_norm(resid)
    modded_two = (normed_two * (1.0 + scale_feed) + shift_feed).astype(BF)
    gate_up = dot(modded_two, w_up)
    gate_part, up_part = gate_up[:, :hidden_units], gate_up[:, hidden_units:]
    sigma = jax.nn.sigmoid(gate_part)
    silu_gate = gate_part * sigma
    hidden = (silu_gate * up_part).astype(BF)
    fed_part = dot(hidden, w_down).astype(BF)

    def group_sum(part):
        part = part.reshape(2, 2, own_count, width)
        part = (part[0].astype(F32) + swap_core(part[1]).astype(F32)).astype(BF)
        return part[0].astype(F32) + swap_side(part[1]).astype(F32)

    own_resid, own_upstream = resid[:own_count], upstream[:own_count]
    fed = group_sum(fed_part)
    block_out = (own_resid + gate_feed[:own_count] * fed).astype(BF)

    fed_grad = (gate_feed * upstream).astype(BF)
    hidden_grad = dot(fed_grad, w_down, 1, 1)
    slope = sigma * (1.0 + gate_part * (1.0 - sigma))
    gate_up_grad = jnp.concatenate(
        [hidden_grad * up_part * slope, hidden_grad * silu_gate], axis=1
    ).astype(BF)
    down_grad = dot(hidden, fed_grad, 0, 0).astype(BF)
    up_grad = dot(modded_two, gate_up_grad, 0, 0).astype(BF)
    m2 = group_sum(dot(gate_up_grad, w_up, 1, 1).astype(BF))
    own_normed_two = normed_two[:own_count]
    resid_grad = own_upstream + norm_back(
        m2 * (1.0 + scale_feed[:own_count]), own_normed_two, inverse_two[:own_count]
    )
    attended_grad = (gate_attend[:own_count] * resid_grad).astype(BF)
    attended_grad = group(attended_grad).reshape(4 * own_count, width)

    own_w_out = lax.dynamic_index_in_dim(w_out, cls, 0, False)
    projected_grad, query_gain_part, key_gain_part = attend_backward(
        attended_grad, own_w_out, raw, low, cosine, sine, qg, kg, item_row, item_col, heads
    )
    gains = jnp.stack([jnp.sum(query_gain_part, axis=1), jnp.sum(key_gain_part, axis=1)])
    core_mixed = mixed_all.reshape(2, 2, heads * head, -1)
    core_mixed = pick(core, core_mixed[:, 0], core_mixed[:, 1]).reshape(2 * heads * head, -1)
    side_grad = pick(side, attended_grad[:, : width // 2], attended_grad[:, width // 2 :])
    out_grad = dot(core_mixed, side_grad).astype(BF)
    in_grad = dot(modded_one, projected_grad, 0, 0).astype(BF)
    m1 = group_sum(dot(projected_grad, w_in, 1, 1).astype(BF))
    own_normed_one = normed_one[:own_count]
    tokens_grad = resid_grad + norm_back(
        m1 * (1.0 + scale_attend[:own_count]), own_normed_one, inverse_one[:own_count]
    )

    if ringed:
        down_sum = ring_scatter(down_grad.reshape(planes, hid, width)).astype(BF)
        left, right = down_sum[:, : width // 2], down_sum[:, width // 2 :]
        came = swap_side(pick(side, right, left))
        feed_out_grad = jnp.concatenate(
            ordered(side, pick(side, left, right), came), axis=0
        ).astype(F32)
        up_sum = ring_scatter(up_grad.reshape(planes, 2 * feed_in.shape[0], -1)).astype(BF)
        parts = unspread_columns(up_sum).reshape(2, 2, feed_in.shape[0], planes, hid)
        feed_in_grad = jnp.transpose(parts, (2, 3, 1, 0, 4)).reshape(feed_in.shape).astype(F32)
        attend_out_grad = ring_scatter(
            out_grad.reshape(planes, head, width // 2),
            lambda index: (index % 2) * half + index // 2,
        )
        in_sum = ring_scatter(in_grad.reshape(planes, 2 * head, -1)).astype(BF)
        parts = unspread_columns(in_sum).reshape(4, head, columns_in // (4 * head), head)
        attend_in_grad = jnp.transpose(parts, (1, 2, 0, 3)).reshape(attend_in.shape).astype(F32)
    else:

        def padded(shape, value, axis, which):
            zero = jnp.zeros(shape, value.dtype)
            return lax.dynamic_update_index_in_dim(zero, value, which, axis)

        grad = down_grad.reshape(planes, hid, width)
        grad = padded((planes, 4, hid, width), grad, 1, share)
        feed_out_grad = scatter_whole(grad.reshape(4 * hidden_units, width))
        grad = up_grad.reshape(width, 2 * planes, hid)
        grad = padded((width, 2 * planes, 4, hid), grad, 2, share)
        feed_in_grad = scatter_whole(grad.reshape(width, 8 * hidden_units))
        grad = out_grad.reshape(2, heads, head, width // 2)
        grad = jnp.swapaxes(grad, 0, 1)
        grad = padded((heads, 2, head, 2, width // 2), grad, 3, side)
        grad = padded((heads, 2, 2, head, 2, width // 2), grad, 2, core)
        attend_out_grad = scatter_whole(grad.reshape(width, width))
        grad = in_grad.reshape(width, 3 * heads, head)
        grad = padded((width, 3 * heads, 4, head), grad, 2, cls)
        attend_in_grad = scatter_whole(grad.reshape(width, 3 * width))

    terms = (
        m1,
        m1 * own_normed_one,
        resid_grad * attended[:own_count],
        m2,
        m2 * own_normed_two,
        own_upstream * fed,
    )
    mod_grad = jnp.concatenate(
        [
            lax.dot_general(own_members, term, (((0,), (0,)), ((), ())), precision=HIGHEST)
            for term in terms
        ],
        axis=1,
    ).astype(BF)
    if ringed:
        left, right = mod_grad[:, :mod_cols], mod_grad[:, mod_cols:]
        came = swap_side(pick(side, right, left))
        mod_grad = jnp.concatenate(ordered(side, pick(side, left, right), came), axis=0)
        mod_grad = ring_gather(mod_grad)
        mod_grad = jnp.stack(ordered(core, mod_grad, swap_core(mod_grad)), axis=1)
        mod_grad = mod_grad.reshape(ndp * dp_items, mod_cols)
    else:
        mod_grad = lax.all_to_all(mod_grad, "mod", split_axis=1, concat_axis=0, tiled=True)
        mod_grad = lax.all_gather(mod_grad, "dp", axis=0, tiled=True)
    modulate_grad = dot(silu_rows, mod_grad, 0, 0)
    cond_terms = dot(mod_grad, modulate_weight, 1, 1).astype(BF)
    cond_terms = lax.all_to_all(cond_terms, "dp", split_axis=0, concat_axis=1, tiled=True)
    own_width = width // nmod
    if ringed:
        left, right = cond_terms[:, :own_width], cond_terms[:, own_width:]
        came = swap_side(pick(side, right, left))
        cond_share = pick(side, left, right).astype(F32) + came.astype(F32)
    else:
        cond_share = lax.psum_scatter(
            cond_terms, "mod", scatter_dimension=1, tiled=True
        ).astype(F32)
    cond_cols = lax.dynamic_slice_in_dim(cond_float, mod * own_width, own_width, 1)
    cond_sigma = jax.nn.sigmoid(cond_cols)
    condition_grad = cond_share * cond_sigma * (1.0 + cond_cols * (1.0 - cond_sigma))
    gains = lax.psum(gains, ("dp", "mod"))
    return (
        block_out,
        tokens_grad,
        condition_grad,
        gains[0],
        gains[1],
        attend_in_grad,
        attend_out_grad,
        feed_in_grad,
        feed_out_grad,
        modulate_grad,
    )


def solution(mesh):
    rows = P(("dp", "mod"), None)
    both = P("dp", "mod")
    return jax.shard_map(
        body,
        mesh=mesh,
        in_specs=(
            rows,
            P("dp", None),
            rows,
            P(None, ("dp", "mod")),
            P(),
            P(),
            both,
            both,
            both,
            both,
            both,
            rows,
        ),
        out_specs=(rows, rows, both, P(), P(), both, both, both, both, both),
        check_vma=False,
    )
```

```python
import functools

import jax
import jax.numpy as jnp
from jax import lax
from jax.experimental import pallas as pl
from jax.experimental.pallas import tpu as pltpu
from jax.sharding import PartitionSpec as P

HIGHEST = lax.Precision.HIGHEST
BF = jnp.bfloat16
F32 = jnp.float32
I32 = jnp.int32
MIB = 2**20


def layer_norm(values):
    average = jnp.mean(values, axis=-1, keepdims=True)
    centred = values - average
    spread = jnp.mean(centred * centred, axis=-1, keepdims=True)
    inverse = lax.rsqrt(spread + 1e-06)
    return (centred * inverse, inverse)


def norm_back(upstream, normed, inverse):
    first = jnp.mean(upstream, axis=-1, keepdims=True)
    second = jnp.mean(upstream * normed, axis=-1, keepdims=True)
    return inverse * (upstream - first - normed * second)


def dot(left, right, left_dim=1, right_dim=0):
    return lax.dot_general(
        left, right, (((left_dim,), (right_dim,)), ((), ())), preferred_element_type=F32
    )


def fence(*values):
    return lax.optimization_barrier(values)


def kernel_call(kernel, grid, in_specs, out_specs, out_shape, name, scratch=(), alias=None):
    return pl.pallas_call(
        kernel,
        grid_spec=pltpu.PrefetchScalarGridSpec(
            num_scalar_prefetch=1,
            grid=grid,
            in_specs=in_specs,
            out_specs=out_specs,
            scratch_shapes=list(scratch),
        ),
        out_shape=out_shape,
        input_output_aliases=alias or {},
        compiler_params=pltpu.CompilerParams(vmem_limit_bytes=56 * MIB),
        cost_estimate=pl.CostEstimate(flops=1024, bytes_accessed=1024, transcendentals=0),
        name=name,
    )


def whole_spec(shape):
    return pl.BlockSpec(shape, lambda *_: (0,) * len(shape))


def lead_spec(shape):
    return pl.BlockSpec((1,) + shape[1:], lambda i, *_: (i,) + (0,) * (len(shape) - 1))


def shaped(shape, dtype):
    return jax.ShapeDtypeStruct(shape, dtype)


def plane_of(ring, planes):
    ring = lax.rem(ring + 2 * planes, planes)
    return jnp.where(ring < planes // 2, 2 * ring, 2 * (planes - 1 - ring) + 1)


SIDE, CORE, PLACE, CLS, FIRST = 0, 1, 2, 3, 4


def sort_kernel(width, share_of, me_ref, weight_ref, *outs):
    rows, columns = weight_ref.shape
    groups = columns // (4 * width)
    for share in range(4):
        side, core = share_of(share)
        pieces = [
            weight_ref[:, (4 * g + share) * width : (4 * g + share + 1) * width]
            for g in range(groups)
        ]
        value = jnp.concatenate(pieces, axis=1)
        relation = 2 * (me_ref[CORE] ^ core) + (me_ref[SIDE] ^ side)
        for k in range(4):

            @pl.when(relation == k)
            def _(k=k, value=value):
                outs[k][...] = value


def sort_columns(me, weight, width, share_of, name):
    rows, columns = weight.shape
    return kernel_call(
        functools.partial(sort_kernel, width, share_of),
        (1,),
        [whole_spec(weight.shape)],
        [whole_spec((rows, columns // 4))] * 4,
        [shaped((rows, columns // 4), weight.dtype)] * 4,
        name,
    )(me, weight)


def quad(me_ref, refs):
    own, side, core, both = (ref[...].astype(F32) for ref in refs)
    here = me_ref[SIDE] == 0
    near = jnp.concatenate([jnp.where(here, own, side), jnp.where(here, side, own)], axis=1)
    far = jnp.concatenate([jnp.where(here, core, both), jnp.where(here, both, core)], axis=1)
    here = me_ref[CORE] == 0
    return jnp.concatenate([jnp.where(here, near, far), jnp.where(here, far, near)], axis=0)


def unit_kernel(me_ref, a_ref, b_ref, c_ref, d_ref, *rest):
    out_ref = rest[-1]
    value = quad(me_ref, (a_ref, b_ref, c_ref, d_ref)).astype(BF)
    rows, columns = value.shape
    out_ref[:rows, :columns] = value
    if len(rest) == 1:
        return
    extra = rest[0][...].astype(F32)
    half = extra.shape[1] // 2
    extra = jnp.concatenate([extra[:, :half], extra[:, half:]], axis=0).astype(BF)
    out_ref[:rows, columns:] = extra
    keep, came = rest[1][...].astype(F32), rest[2][...].astype(F32)
    here = me_ref[SIDE] == 0
    value = jnp.concatenate([jnp.where(here, keep, came), jnp.where(here, came, keep)], axis=1)
    out_ref[rows:, :] = value.astype(BF)


def make_unit(me, parts, extras, name):
    rows, columns = parts[0].shape
    high, wide = 2 * rows, 2 * columns
    if extras:
        high, wide = high + extras[1].shape[0], wide + extras[0].shape[1] // 2
    operands = list(parts) + list(extras)
    return kernel_call(
        unit_kernel,
        (1,),
        [whole_spec(v.shape) for v in operands],
        whole_spec((high, wide)),
        shaped((high, wide), BF),
        name,
    )(me, *operands)


def gather_steps(planes):
    return [0] + [s * d for d in range(1, planes // 2) for s in (-1, 1)] + [planes // 2]


def assemble_kernel(planes, rows, split, me_ref, *refs):
    pieces = len(gather_steps(planes)) + 1
    outs = refs[pieces:]
    high = refs[0].shape[0]
    for at, step in enumerate(gather_steps(planes)):
        plane = plane_of(me_ref[PLACE] + step, planes)
        if at == pieces - 2:
            value = jnp.concatenate(
                [refs[at][...].astype(F32), refs[at + 1][...].astype(F32)], axis=0
            ).astype(BF)
        else:
            value = refs[at][...]
        outs[0][pl.ds(pl.multiple_of(plane * rows, 16), rows), :] = value[:rows, :split]
        if len(outs) > 1:
            slot = lax.rem(plane, 2) * (planes // 2) + plane // 2
            extra = value[:rows, split:].astype(F32)
            extra = jnp.concatenate([extra[: rows // 2], extra[rows // 2 :]], axis=1)
            outs[1][slot] = extra.astype(BF)
            rest = high - rows
            outs[2][pl.ds(pl.multiple_of(plane * rest, 16), rest), :] = value[rows:]


def assemble(me, pieces, planes, rows, split, name):
    high, columns = pieces[0].shape
    outs = [shaped((planes * rows, split), BF)]
    if split < columns:
        outs.append(shaped((planes, rows // 2, 2 * (columns - split)), BF))
        outs.append(shaped((planes * (high - rows), columns), BF))
    return kernel_call(
        functools.partial(assemble_kernel, planes, rows, split),
        (1,),
        [whole_spec(v.shape) for v in pieces],
        [whole_spec(v.shape) for v in outs],
        outs,
        name,
    )(me, *pieces)


def mod_part_kernel(me_ref, rows_ref, weight_ref, keep_ref, send_ref):
    columns = keep_ref.shape[1]
    product = dot(rows_ref[...], weight_ref[...])
    here = me_ref[CORE] == 0
    left, right = product[:, :columns], product[:, columns:]
    keep_ref[...] = jnp.where(here, left, right)
    send_ref[...] = jnp.where(here, right, left).astype(BF)


def mod_part(me, rows, weight):
    shape = (rows.shape[0], weight.shape[1] // 2)
    return kernel_call(
        mod_part_kernel,
        (1,),
        [whole_spec(rows.shape), whole_spec(weight.shape)],
        [whole_spec(shape)] * 2,
        [shaped(shape, F32), shaped(shape, BF)],
        "mod_part",
    )(me, rows, weight)


def split_kernel(columns, me_ref, own_ref, ahead_ref, behind_ref, *outs):
    total = own_ref[0].astype(F32) + ahead_ref[...].astype(F32) + behind_ref[...].astype(F32)
    rows = total.shape[0] // 2
    for side in range(2):
        for core in range(2):
            value = total[core * rows : (core + 1) * rows, side * columns : (side + 1) * columns]
            relation = 2 * (me_ref[CORE] ^ core) + (me_ref[SIDE] ^ side)
            for k in range(4):

                @pl.when(relation == k)
                def _(k=k, value=value):
                    outs[k][...] = value.astype(BF)

    if len(outs) > 4:
        extra = total[:, 2 * columns :]
        outs[4][...] = jnp.concatenate([extra[:rows], extra[rows:]], axis=1)


def split_sum(me, blocks, ahead, behind, columns, name):
    planes, rows, wide = blocks.shape
    outs = [shaped((rows // 2, columns), BF)] * 4
    if 2 * columns < wide:
        outs.append(shaped((rows // 2, 2 * (wide - 2 * columns)), F32))
    return kernel_call(
        functools.partial(split_kernel, columns),
        (1,),
        [
            pl.BlockSpec((1, rows, wide), lambda i, me: (plane_of(me[PLACE], planes), 0, 0)),
            whole_spec(ahead.shape),
            whole_spec(behind.shape),
        ],
        [whole_spec(v.shape) for v in outs],
        outs,
        name,
    )(me, blocks, ahead, behind)


def unsort_kernel(width, share_of, me_ref, *refs):
    out_ref = refs[-1]
    groups = refs[0].shape[1] // width
    found = [ref[...].astype(F32) for ref in refs[:4]]
    shares = []
    for share in range(4):
        side, core = share_of(share)
        near, far = me_ref[SIDE] == side, me_ref[CORE] == core
        shares.append(
            jnp.where(
                far,
                jnp.where(near, found[0], found[1]),
                jnp.where(near, found[2], found[3]),
            )
        )
    out_ref[...] = jnp.concatenate(
        [shares[s][:, g * width : (g + 1) * width] for g in range(groups) for s in range(4)],
        axis=1,
    )


def unsort_columns(me, parts, width, share_of, name):
    rows, columns = parts[0].shape
    return kernel_call(
        functools.partial(unsort_kernel, width, share_of),
        (1,),
        [whole_spec(v.shape) for v in parts],
        whole_spec((rows, 4 * columns)),
        shaped((rows, 4 * columns), F32),
        name,
    )(me, *parts)


def attend_grads_kernel(
    planes, me_ref, modded_ref, grad_ref, mixed_ref, mixed_side_ref, a_ref, b_ref, c_ref, d_ref,
    out_ref,
):
    rows = out_ref.shape[1]
    columns = grad_ref.shape[1]
    count, width = a_ref.shape
    whole = dot(modded_ref[...], grad_ref[...], 0, 0).astype(BF)
    for plane in range(planes):
        out_ref[plane, :, :columns] = whole[plane * rows : (plane + 1) * rows]
    here = me_ref[SIDE] == 0
    blocks = [
        jnp.where(here, ref[:, : width // 2].astype(F32), ref[:, width // 2 :].astype(F32))
        for ref in (a_ref, b_ref, c_ref, d_ref)
    ]
    head = rows // 2
    half = width // 4
    for flip, ref in enumerate((mixed_ref, mixed_side_ref)):
        order = jnp.concatenate([blocks[k ^ flip] for k in range(4)], axis=0).astype(BF)
        found = dot(ref[...], order)
        for j in range(found.shape[0] // head):
            value = found[j * head : (j + 1) * head]
            value = jnp.concatenate([value[:, :half], value[:, half:]], axis=0).astype(BF)
            out_ref[2 * j + (me_ref[SIDE] ^ flip), :, columns:] = value


def attend_grads(me, modded, grad, mixed, mixed_side, attended_grads, planes):
    width = modded.shape[1]
    rows = width // planes
    out = shaped((planes, rows, grad.shape[1] + width // 4), BF)
    operands = [modded, grad, mixed, mixed_side, *attended_grads]
    return kernel_call(
        functools.partial(attend_grads_kernel, planes),
        (1,),
        [whole_spec(v.shape) for v in operands],
        whole_spec(out.shape),
        out,
        "attend_grads",
    )(me, *operands)


def ring_add_kernel(cut, me_ref, ahead_mine, behind_mine, ahead, behind, ahead_out, behind_out):
    mine = ahead_mine[0].astype(F32)
    came = ahead[...].astype(F32)
    if cut:
        ahead_out[...] = jnp.concatenate([mine[:cut] + came, mine[cut:]], axis=0).astype(BF)
    else:
        ahead_out[...] = (mine + came).astype(BF)
    mine = behind_mine[0].astype(F32)
    came = behind[...].astype(F32)
    if cut:
        behind_out[...] = jnp.concatenate([mine[:cut], mine[cut:] + came], axis=0).astype(BF)
    else:
        behind_out[...] = (mine + came).astype(BF)


def ring_add(me, blocks, ahead, behind, step, slot, cut, name):
    planes, rows, columns = blocks.shape

    def at(sign):
        return lambda i, me: (slot(plane_of(me[PLACE] + sign * step, planes)), 0, 0)

    block = (1, rows, columns)
    return kernel_call(
        functools.partial(ring_add_kernel, cut),
        (1,),
        [
            pl.BlockSpec(block, at(1)),
            pl.BlockSpec(block, at(-1)),
            whole_spec(ahead.shape),
            whole_spec(behind.shape),
        ],
        [whole_spec((rows, columns))] * 2,
        [shaped((rows, columns), BF)] * 2,
        name,
    )(me, blocks, blocks, ahead, behind)


def weight_grad_kernel(me_ref, left_ref, right_ref, out_ref):
    out_ref[...] = dot(left_ref[...], right_ref[...], 0, 0).astype(BF)


def weight_grad(me, left, right, tile, name):
    count, rows = left.shape
    columns = right.shape[1]
    return kernel_call(
        weight_grad_kernel,
        (rows // tile,),
        [pl.BlockSpec((count, tile), lambda i, *_: (0, i)), whole_spec(right.shape)],
        pl.BlockSpec((tile, columns), lambda i, *_: (i, 0)),
        shaped((rows, columns), BF),
        name,
    )(me, left, right)


def turned(values, first):
    quarter = values.shape[0] // 4
    ahead = pltpu.roll(values, values.shape[0] - quarter, 0)
    behind = pltpu.roll(values, quarter, 0)
    return jnp.where(first, ahead, behind)


def rms(values):
    return lax.rsqrt(jnp.mean(values * values, axis=0, keepdims=True) + 1e-06)


def scores_t(key_rot, query_rot, same, scale):
    raw = dot(key_rot, query_rot, 0, 0) * scale
    return jnp.where(same, raw, -1e30)


def softmax_t(scores):
    peak = jnp.max(scores, axis=0, keepdims=True)
    exponent = jnp.exp(scores - peak)
    return exponent / jnp.sum(exponent, axis=0, keepdims=True)


def first_mask(head, count):
    row = lax.broadcasted_iota(I32, (head, count), 0)
    return lax.rem(row, head // 2) < head // 4


def members_of(column, items):
    lane = lax.broadcasted_iota(I32, (column.shape[0], items), 1)
    return (column == lane).astype(BF)


def attend_forward_kernel(
    heads, head, me_ref, tokens_ref, mods_ref, weight_ref, cos_ref, sin_ref, qg_ref, kg_ref,
    row_ref, col_ref, modded_ref, raw_ref, low_ref, mixed_ref, held_ref,
):
    count, width = tokens_ref.shape
    own = heads * head
    members = members_of(col_ref[0], mods_ref.shape[0])
    token_mod = dot(members, mods_ref[:, : 2 * width])
    normed, _ = layer_norm(tokens_ref[...].astype(F32))
    modded = (normed * (1.0 + token_mod[:, width:]) + token_mod[:, :width]).astype(BF)
    modded_ref[...] = modded
    projected = dot(modded, weight_ref[...]).T
    raw_ref[0] = projected[: 2 * own]
    values = projected[2 * own :]
    low_ref[0] = values.astype(BF)
    same = col_ref[0] == row_ref[0]
    first = first_mask(head, count)
    cosine, sine = cos_ref[0], sin_ref[0]
    scale = head ** (-0.5)

    def rotated(raw, gain):
        normed = raw * rms(raw) * gain
        return (normed * cosine + turned(normed, first) * sine).astype(BF)

    for h in range(heads):
        query_rot = rotated(projected[h * head : (h + 1) * head], qg_ref[...])
        key_rot = rotated(projected[own + h * head : own + (h + 1) * head], kg_ref[...])
        prob = softmax_t(scores_t(key_rot, query_rot, same, scale)).astype(BF)
        mixed = dot(values[h * head : (h + 1) * head].astype(BF), prob)
        held_ref[h * head : (h + 1) * head, :] = mixed
    mixed_ref[...] = held_ref[...].astype(BF)


def attend_forward(me, tokens, mods, weight, cosine, sine, qg, kg, row, col, heads):
    seqs, head, count = cosine.shape
    width = tokens.shape[1]
    own = heads * head
    return kernel_call(
        functools.partial(attend_forward_kernel, heads, head),
        (seqs,),
        [
            pl.BlockSpec((count, width), lambda i, *_: (i, 0)),
            whole_spec(mods.shape),
            whole_spec(weight.shape),
            lead_spec(cosine.shape),
            lead_spec(sine.shape),
            whole_spec(qg.shape),
            whole_spec(kg.shape),
            lead_spec(row.shape),
            lead_spec(col.shape),
        ],
        [
            pl.BlockSpec((count, width), lambda i, *_: (i, 0)),
            lead_spec((seqs, 2 * own, count)),
            lead_spec((seqs, own, count)),
            pl.BlockSpec((own, count), lambda i, *_: (0, i)),
        ],
        [
            shaped((seqs * count, width), BF),
            shaped((seqs, 2 * own, count), F32),
            shaped((seqs, own, count), BF),
            shaped((own, seqs * count), BF),
        ],
        "attend_forward",
        [pltpu.VMEM((own, count), F32)],
    )(me, tokens, mods, weight, cosine, sine, qg, kg, row, col)


def attend_backward_kernel(
    heads, head, me_ref, near_ref, far_ref, out_w_ref, in_w_ref, raw_ref, low_ref, cos_ref,
    sin_ref, qg_ref, kg_ref, row_ref, col_ref, tokens_ref, *rest,
):
    out_ref, m1_ref, qgg_ref, kgg_ref, sums_ref, held_ref = rest[-6:]
    own = heads * head
    half = pl.num_programs(0) // 2
    grad = jnp.where(pl.program_id(0) < half, near_ref[...], far_ref[...])
    count = grad.shape[0]
    mixed_grad = dot(out_w_ref[0], grad, 1, 1)
    same = col_ref[0] == row_ref[0]
    first = first_mask(head, count)
    cosine, sine = cos_ref[0], sin_ref[0]
    scale = head ** (-0.5)

    @pl.when(pl.program_id(0) == 0)
    def _():
        qgg_ref[...] = jnp.zeros_like(qgg_ref)
        kgg_ref[...] = jnp.zeros_like(kgg_ref)
        sums_ref[...] = jnp.zeros_like(sums_ref)

    def rotated(raw, gain):
        inverse = rms(raw)
        normed = raw * inverse * gain
        return inverse, (normed * cosine + turned(normed, first) * sine).astype(BF)

    def back(rot_grad, raw, inverse, gain):
        norm_grad = rot_grad * cosine + turned(rot_grad * sine, first)
        gain_grad = norm_grad * raw * inverse
        scaled = norm_grad * gain
        inner = jnp.mean(scaled * raw, axis=0, keepdims=True)
        return inverse * scaled - raw * (inverse * inverse * inverse * inner), gain_grad

    query_total = jnp.zeros((head, count), F32)
    key_total = jnp.zeros((head, count), F32)
    low = low_ref[0].astype(F32)
    for h in range(heads):
        rows = slice(h * head, (h + 1) * head)
        query_raw = raw_ref[0, h * head : (h + 1) * head]
        key_raw = raw_ref[0, own + h * head : own + (h + 1) * head]
        values = low[rows].astype(BF)
        upstream = mixed_grad[rows].astype(BF)
        query_inverse, query_rot = rotated(query_raw, qg_ref[...])
        key_inverse, key_rot = rotated(key_raw, kg_ref[...])
        prob = softmax_t(scores_t(key_rot, query_rot, same, scale))
        prob_grad = dot(values, upstream, 0, 0)
        inner = jnp.sum(prob * prob_grad, axis=0, keepdims=True)
        score_grad = (prob * (prob_grad - inner)).astype(BF)
        query_rot_grad = dot(key_rot, score_grad) * scale
        key_rot_grad = dot(query_rot, score_grad, 1, 1) * scale
        values_grad = dot(upstream, prob.astype(BF), 1, 1)
        query_grad, query_part = back(query_rot_grad, query_raw, query_inverse, qg_ref[...])
        key_grad, key_part = back(key_rot_grad, key_raw, key_inverse, kg_ref[...])
        query_total += query_part
        key_total += key_part
        held_ref[h * head : (h + 1) * head, :] = query_grad
        held_ref[own + h * head : own + (h + 1) * head, :] = key_grad
        held_ref[2 * own + h * head : 2 * own + (h + 1) * head, :] = values_grad
    qgg_ref[...] += query_total
    kgg_ref[...] += key_total
    projected_grad = held_ref[...].T.astype(BF)
    out_ref[...] = projected_grad
    m1 = dot(projected_grad, in_w_ref[...], 1, 1)
    m1_ref[...] = m1.astype(BF)
    normed, _ = layer_norm(tokens_ref[...].astype(F32))
    members = members_of(col_ref[0], sums_ref.shape[0])
    width = m1.shape[1]
    sums_ref[:, :width] += dot(members, m1.astype(BF), 0, 0)
    sums_ref[:, width:] += dot(members, (m1 * normed).astype(BF), 0, 0)


def attend_backward(
    me, near, far, w_out, w_in, raw, low, cosine, sine, qg, kg, row, col, tokens, items, heads,
    at, held,
):
    seqs, head, count = cosine.shape
    width = near.shape[1]
    own = heads * head
    per = seqs // 4

    def seq(i):
        return at * per + i + jnp.where(i < per, 0, per)

    def block(shape):
        return pl.BlockSpec((1,) + shape[1:], lambda i, *_: (seq(i), 0, 0))

    in_specs = [
        pl.BlockSpec((count, width), lambda i, *_: (jnp.minimum(i, per - 1), 0)),
        pl.BlockSpec((count, width), lambda i, *_: (jnp.maximum(i - per, 0), 0)),
        pl.BlockSpec((1,) + w_out.shape[1:], lambda i, me: (me[CLS], 0, 0)),
        whole_spec(w_in.shape),
        block(raw.shape),
        block(low.shape),
        block(cosine.shape),
        block(sine.shape),
        whole_spec(qg.shape),
        whole_spec(kg.shape),
        block(row.shape),
        block(col.shape),
        pl.BlockSpec((count, width), lambda i, *_: (seq(i), 0)),
    ]
    operands = [near, far, w_out, w_in, raw, low, cosine, sine, qg, kg, row, col, tokens]
    alias = {}
    if held is not None:
        alias = {1 + len(operands): 0}
        operands.append(held)
        in_specs.append(pl.BlockSpec(memory_space=pl.ANY))
    return kernel_call(
        functools.partial(attend_backward_kernel, heads, head),
        (2 * per,),
        in_specs,
        [
            pl.BlockSpec((count, 3 * own), lambda i, *_: (seq(i), 0)),
            pl.BlockSpec((count, width), lambda i, *_: (i, 0)),
            whole_spec((head, count)),
            whole_spec((head, count)),
            whole_spec((items, 2 * width)),
        ],
        [
            shaped((seqs * count, 3 * own), BF),
            shaped((2 * per * count, width), BF),
            shaped((head, count), F32),
            shaped((head, count), F32),
            shaped((items, 2 * width), F32),
        ],
        "attend_backward",
        [pltpu.VMEM((3 * own, count), F32)],
        alias,
    )(me, *operands)


def feed_forward_kernel(
    me_ref, tokens_ref, upstream_ref, mods_ref, col_ref, m0_ref, m1_ref, m2_ref, m3_ref,
    w_out_ref, w_up_ref, modded_ref, gate_up_ref, hidden_ref, fed_grad_ref, attended_ref,
    mixed_ref,
):
    width = tokens_ref.shape[1]
    own = m0_ref.shape[0]
    for k, ref in enumerate((m0_ref, m1_ref, m2_ref, m3_ref)):
        cls = 2 * (me_ref[SIDE] ^ (k & 1)) + (me_ref[CORE] ^ (k >> 1))
        mixed_ref[pl.ds(pl.multiple_of(cls * own, 16), own), :] = ref[...]
    attended = dot(mixed_ref[...], w_out_ref[...], 0, 0)

    @pl.when(pl.program_id(0) == 0)
    def _():
        attended_ref[...] = attended

    members = members_of(col_ref[...], mods_ref.shape[0])
    token_mod = dot(members, mods_ref[:, 2 * width :])
    resid = tokens_ref[...].astype(F32) + token_mod[:, :width] * attended
    normed, _ = layer_norm(resid)
    modded = normed * (1.0 + token_mod[:, 2 * width : 3 * width]) + token_mod[:, width : 2 * width]
    modded = modded.astype(BF)
    modded_ref[...] = modded
    gate_up = dot(modded, w_up_ref[...])
    gate_up_ref[...] = gate_up
    units = gate_up.shape[1] // 2
    gate, up = gate_up[:, :units], gate_up[:, units:]
    hidden_ref[...] = (gate * jax.nn.sigmoid(gate) * up).astype(BF)
    fed_grad_ref[...] = (token_mod[:, 3 * width :] * upstream_ref[...].astype(F32)).astype(BF)


def feed_forward(me, tokens, upstream, mods, col, mixed, w_out, w_up):
    total, width = tokens.shape
    count = total // 4
    own = mixed[0].shape[0]
    columns = w_up.shape[1]

    def rows(n):
        return pl.BlockSpec((count, n), lambda j, *_: (j, 0))

    def mixed_spec(k):
        return pl.BlockSpec((own, count), lambda j, *_: (0, j ^ k))

    return kernel_call(
        feed_forward_kernel,
        (4,),
        [
            rows(width),
            rows(width),
            whole_spec(mods.shape),
            rows(1),
            *(mixed_spec(k) for k in range(4)),
            whole_spec(w_out.shape),
            whole_spec(w_up.shape),
        ],
        [
            rows(width),
            rows(columns),
            rows(columns // 2),
            rows(width),
            whole_spec((count, width)),
        ],
        [
            shaped((total, width), BF),
            shaped((total, columns), F32),
            shaped((total, columns // 2), BF),
            shaped((total, width), BF),
            shaped((count, width), F32),
        ],
        "feed_forward",
        [pltpu.VMEM((4 * own, count), BF)],
    )(me, tokens, upstream, mods, col, *mixed, w_out, w_up)


def feed_backward_kernel(
    me_ref, gate_up_ref, hidden_ref, fed_grad_ref, w_up_ref, w_down_ref, *rest
):
    grad_ref, m2_ref, fed_ref = rest[-3:]
    hidden_grad = dot(fed_grad_ref[...], w_down_ref[...], 1, 1)
    units = hidden_grad.shape[1]
    gate, up = gate_up_ref[:, :units], gate_up_ref[:, units:]
    sigma = jax.nn.sigmoid(gate)
    slope = sigma * (1.0 + gate * (1.0 - sigma))
    grad_ref[:, :units] = (hidden_grad * up * slope).astype(BF)
    grad_ref[:, units:] = (hidden_grad * (gate * sigma)).astype(BF)
    m2_ref[...] = dot(grad_ref[...], w_up_ref[...], 1, 1).astype(BF)
    fed_ref[...] = dot(hidden_ref[...], w_down_ref[...]).astype(BF)


def feed_backward(me, gate_up, hidden, fed_grad, w_up, w_down, at, held):
    total, columns = gate_up.shape
    width = fed_grad.shape[1]
    count = total // 4

    def rows(n):
        return pl.BlockSpec((count, n), lambda j, *_: (2 * j + at, 0))

    out = pl.BlockSpec((count, width), lambda j, *_: (j, 0))
    in_specs = [
        rows(columns),
        rows(columns // 2),
        rows(width),
        whole_spec(w_up.shape),
        whole_spec(w_down.shape),
    ]
    operands = [gate_up, hidden, fed_grad, w_up, w_down]
    alias = {}
    if held is not None:
        alias = {1 + len(operands): 0}
        operands.append(held)
        in_specs.append(pl.BlockSpec(memory_space=pl.ANY))
    return kernel_call(
        feed_backward_kernel,
        (2,),
        in_specs,
        [rows(columns), out, out],
        [
            shaped((total, columns), BF),
            shaped((2 * count, width), BF),
            shaped((2 * count, width), BF),
        ],
        "feed_backward",
        (),
        alias,
    )(me, *operands)


def own_sums(me_ref, column, items, *terms):
    lane = lax.broadcasted_iota(I32, (column.shape[0], items), 1)
    members = (column - me_ref[FIRST] == lane).astype(BF)
    return [dot(members, term.astype(BF), 0, 0).astype(BF) for term in terms]


def resid_kernel(
    me_ref, tokens_ref, upstream_ref, mods_ref, col_ref, attended_ref, near_ref, core_ref,
    side_ref, grad_ref, out_ref, sums_ref,
):
    width = tokens_ref.shape[1]
    members = members_of(col_ref[...], mods_ref.shape[0])
    token_mod = dot(members, mods_ref[:, 2 * width : 5 * width])
    gate, scale = token_mod[:, :width], token_mod[:, 2 * width :]
    attended = attended_ref[...]
    normed, inverse = layer_norm(tokens_ref[...].astype(F32) + gate * attended)
    m2 = near_ref[...].astype(F32) + core_ref[...].astype(F32) + side_ref[...].astype(F32)
    resid_grad = upstream_ref[...].astype(F32) + norm_back(m2 * (1.0 + scale), normed, inverse)
    grad_ref[...] = resid_grad
    out_ref[...] = (gate * resid_grad).astype(BF)
    sums = own_sums(
        me_ref, col_ref[...], sums_ref.shape[0], resid_grad * attended, m2, m2 * normed
    )
    for at, value in enumerate(sums):
        sums_ref[:, at * width : (at + 1) * width] = value


def resid_back(me, tokens, upstream, mods, col, attended, near, core, side, items):
    count, width = tokens.shape
    block = pl.BlockSpec((count, width), lambda i, *_: (0, 0))
    return kernel_call(
        resid_kernel,
        (1,),
        [
            block,
            block,
            whole_spec(mods.shape),
            pl.BlockSpec((count, 1), lambda i, *_: (0, 0)),
            block,
            block,
            block,
            block,
        ],
        [block, block, whole_spec((items, 3 * width))],
        [
            shaped((count, width), F32),
            shaped((count, width), BF),
            shaped((items, 3 * width), BF),
        ],
        "resid_back",
    )(me, tokens, upstream, mods, col, attended, near, core, side)


def output_kernel(
    me_ref, tokens_ref, upstream_ref, mods_ref, col_ref, attended_ref, near_ref, core_ref,
    side_ref, out_ref, sums_ref,
):
    width = tokens_ref.shape[1]
    members = members_of(col_ref[...], mods_ref.shape[0])
    attend_gate = dot(members, mods_ref[:, 2 * width : 3 * width])
    feed_gate = dot(members, mods_ref[:, 5 * width :])
    fed = near_ref[...].astype(F32) + core_ref[...].astype(F32) + side_ref[...].astype(F32)
    resid = tokens_ref[...].astype(F32) + attend_gate * attended_ref[...]
    out_ref[...] = (resid + feed_gate * fed).astype(BF)
    (sums_ref[...],) = own_sums(
        me_ref, col_ref[...], sums_ref.shape[0], upstream_ref[...].astype(F32) * fed
    )


def output(me, tokens, upstream, mods, col, attended, near, core, side, items):
    count, width = tokens.shape
    block = pl.BlockSpec((count, width), lambda i, *_: (0, 0))
    return kernel_call(
        output_kernel,
        (1,),
        [
            block,
            block,
            whole_spec(mods.shape),
            pl.BlockSpec((count, 1), lambda i, *_: (0, 0)),
            block,
            block,
            block,
            block,
        ],
        [block, whole_spec((items, width))],
        [shaped((count, width), BF), shaped((items, width), BF)],
        "output",
    )(me, tokens, upstream, mods, col, attended, near, core, side)


def tokens_kernel(
    me_ref, tokens_ref, mods_ref, col_ref, resid_ref, near_ref, core_ref, side_ref, out_ref
):
    width = tokens_ref.shape[1]
    members = members_of(col_ref[...], mods_ref.shape[0])
    scale = dot(members, mods_ref[:, width : 2 * width])
    normed, inverse = layer_norm(tokens_ref[...].astype(F32))
    m1 = near_ref[...].astype(F32) + core_ref[...].astype(F32) + side_ref[...].astype(F32)
    out_ref[...] = resid_ref[...] + norm_back(m1 * (1.0 + scale), normed, inverse)


def tokens_back(me, tokens, mods, col, resid_grad, near, core, side):
    count, width = tokens.shape
    block = pl.BlockSpec((count, width), lambda i, *_: (0, 0))
    return kernel_call(
        tokens_kernel,
        (1,),
        [
            block,
            whole_spec(mods.shape),
            pl.BlockSpec((count, 1), lambda i, *_: (0, 0)),
            block,
            block,
            block,
            block,
        ],
        block,
        shaped((count, width), F32),
        "tokens_back",
    )(me, tokens, mods, col, resid_grad, near, core, side)


def mod_back_kernel(planes, items, me_ref, rows_ref, weight_ref, *refs):
    count = len(gather_steps(planes)) + 1
    pieces = refs[: 2 * count]
    grad_ref, terms_ref, gains_ref, held_ref = refs[2 * count :]
    gains = jnp.zeros((1, held_ref.shape[1]), F32)
    for at, step in enumerate(gather_steps(planes)):
        plane = plane_of(me_ref[PLACE] + step, planes)
        for other in range(2):
            value = pieces[other * count + at][...].astype(F32)
            if at == count - 2:
                rest = pieces[other * count + at + 1][...].astype(F32)
                value = jnp.concatenate([value, rest], axis=0)
            row = (2 * plane + (me_ref[CORE] ^ other)) * items
            held_ref[pl.ds(pl.multiple_of(row, items), items), :] = value[:items].astype(BF)
            gains += value[items : items + 1]
    grad_ref[...] = dot(rows_ref[...], held_ref[...], 0, 0)
    terms_ref[...] = dot(held_ref[...], weight_ref[...], 1, 1).astype(BF)
    gains_ref[...] = gains


def mod_back(me, rows, weight, own, other, planes, items):
    pieces = list(own) + list(other)
    outs = [shaped(weight.shape, F32), shaped(rows.shape, BF), shaped((1, weight.shape[1]), F32)]
    return kernel_call(
        functools.partial(mod_back_kernel, planes, items),
        (1,),
        [whole_spec(v.shape) for v in (rows, weight, *pieces)],
        [whole_spec(v.shape) for v in outs],
        outs,
        "mod_back",
        [pltpu.VMEM((rows.shape[0], weight.shape[1]), BF)],
    )(me, rows, weight, *pieces)


def body(
    tokens,
    condition,
    lengths,
    positions,
    query_gain,
    key_gain,
    attend_in,
    attend_out,
    feed_in,
    feed_out,
    modulate_weight,
    cotangent,
):
    ndp, nmod = lax.axis_size("dp"), lax.axis_size("mod")
    planes = ndp // 2
    half = planes // 2
    dp, mod = lax.axis_index("dp"), lax.axis_index("mod")
    core, plane, side = dp % 2, dp // 2, mod % 2
    own_seqs, items_seq = lengths.shape
    own_count, width = tokens.shape
    count = own_count // own_seqs
    seqs = 4 * own_seqs
    head = query_gain.shape[0]
    heads = width // head // 4
    cls = 2 * side + core
    own_items = own_seqs * items_seq
    dp_items = condition.shape[0]
    ringed = nmod == 2 and attend_out.shape[0] == head
    hid = feed_out.shape[0] // 2
    place = jnp.where(plane % 2 == 0, plane // 2, planes - 1 - plane // 2)
    first_item = core * dp_items + mod * own_items
    me = jnp.stack([side, core, place, cls, first_item]).astype(I32)

    def relate(value, k):
        pairs = [
            (d * nmod + m, (d ^ (k >> 1)) * nmod + (m ^ (k & 1)))
            for d in range(ndp)
            for m in range(nmod)
        ]
        return lax.ppermute(value, ("dp", "mod"), pairs)

    def swap_core(value):
        return relate(value, 2)

    def swap_side(value):
        return relate(value, 1)

    def pick(which, pair0, pair1):
        return jnp.where(which == 0, pair0, pair1)

    def ordered(which, own, other):
        return pick(which, own, other), pick(which, other, own)

    def static_plane(ring):
        ring %= planes
        return 2 * ring if ring < half else 2 * (planes - 1 - ring) + 1

    def hop(value, step):
        pairs = [
            (2 * static_plane(r) + c, 2 * static_plane(r + step) + c)
            for r in range(planes)
            for c in range(2)
        ]
        return lax.ppermute(value, "dp", pairs)

    class Gather:
        def __init__(self, block, cut=None):
            self.pieces = [block]
            self.cut = block.shape[0] // 32 * 16 if cut is None else cut
            self.ahead = self.behind = block
            self.step = 0

        def go(self):
            self.step += 1
            if self.step == half:
                self.ahead, self.behind = self.ahead[: self.cut], self.behind[self.cut :]
            self.ahead, self.behind = hop(self.ahead, 1), hop(self.behind, -1)
            self.pieces += [self.ahead, self.behind]

    class Scatter:
        def __init__(self, blocks, name, slot=lambda index: index):
            self.blocks, self.slot, self.name = blocks, slot, name
            self.rows = blocks.shape[1]
            self.cut = self.rows // 32 * 16
            far = self.take(half)
            self.ahead, self.behind = far[: self.cut], far[self.cut :]
            self.step = half

        def take(self, step):
            start = (self.slot(plane_of(place + step, planes)), 0, 0)
            return lax.dynamic_slice(self.blocks, start, (1,) + self.blocks.shape[1:])[0]

        def go(self):
            self.ahead, self.behind = hop(self.ahead, 1), hop(self.behind, -1)
            self.step -= 1
            if self.step > 0:
                if not self.name:
                    mine = self.take(self.step).astype(F32), self.take(-self.step).astype(F32)
                    cut = self.cut if self.step == half - 1 else 0
                    if cut:
                        self.ahead = jnp.pad(self.ahead, ((0, self.rows - cut), (0, 0)))
                        self.behind = jnp.pad(self.behind, ((cut, 0), (0, 0)))
                    self.ahead = (mine[0] + self.ahead.astype(F32)).astype(BF)
                    self.behind = (mine[1] + self.behind.astype(F32)).astype(BF)
                    return
                self.ahead, self.behind = ring_add(
                    me,
                    self.blocks,
                    self.ahead,
                    self.behind,
                    self.step,
                    self.slot,
                    self.cut if self.step == half - 1 else 0,
                    self.name,
                )

        def last(self):
            return self.ahead, self.behind

        def result(self):
            return self.take(0).astype(F32) + self.ahead.astype(F32) + self.behind.astype(F32)

    def tie(rings, *values):
        state = [v for ring in rings for v in (ring.ahead, ring.behind)]
        out = list(lax.optimization_barrier(tuple(state) + values))
        for at, ring in enumerate(rings):
            ring.ahead, ring.behind = out[2 * at : 2 * at + 2]
        return out[2 * len(rings) :]

    def gather_whole(weight):
        return lax.all_gather(
            lax.all_gather(weight, "mod", axis=1, tiled=True), "dp", axis=0, tiled=True
        )

    def scatter_whole(padded):
        padded = lax.psum_scatter(padded.astype(BF), "mod", scatter_dimension=1, tiled=True)
        return lax.psum_scatter(padded, "dp", scatter_dimension=0, tiled=True).astype(F32)

    def stack_other_core(value):
        return jnp.stack(ordered(core, value, swap_core(value)))

    def group(value):
        first = jnp.stack([value, swap_side(value)])
        return jnp.concatenate([first, swap_core(first)])

    columns_in = attend_in.shape[1]
    rows = feed_in.shape[0]
    out_slot = lambda index: lax.rem(index, 2) * half + index // 2
    cond_float = condition.astype(F32)
    silu_cond = jax.nn.silu(cond_float).astype(BF)
    mod_cols = modulate_weight.shape[1]
    small = jnp.concatenate([lengths.reshape(-1), positions.reshape(-1)])
    if ringed:
        parts = sort_columns(me, attend_in, head, lambda s: (s // 2, s % 2), "sort_in")
        keep = pick(side, feed_out[:hid], feed_out[hid:])
        came = pick(side, feed_out[hid:], feed_out[:hid])
        silu_cond, keep, came, *parts = tie([], silu_cond, keep, came, *parts)
        silu_rows = lax.all_to_all(silu_cond, "dp", split_axis=1, concat_axis=0, tiled=True)
        parts = [parts[0]] + [relate(parts[k], k) for k in (1, 2, 3)]
        ring_a = Gather(make_unit(me, parts, [attend_out, keep, swap_side(came)], "unit_in"))
        silu_rows, small, tokens_ = tie([ring_a], silu_rows, small, tokens)
        ring_a.go()
        small_side = swap_side(small)
        tokens_side = swap_side(tokens_)
        kept, sent = mod_part(me, silu_rows, modulate_weight)
        kept, sent, small_side, feed_in_ = tie([ring_a], kept, sent, small_side, feed_in)
        ring_a.go()
        small = jnp.stack([small, small_side])
        small = jnp.concatenate([small, swap_core(small)])
        kept = (kept + swap_core(sent).astype(F32)).astype(BF)
        ring_m = Scatter(kept.reshape(planes, 2 * dp_items, mod_cols // 2), "")
        ring_m.go()
        parts = sort_columns(me, feed_in_, hid, lambda s: (s % 2, s // 2), "sort_up")
        tokens_side, small, *parts = tie([ring_a, ring_m], tokens_side, small, *parts)
        ring_a.go()
        ring_m.go()
        parts = [parts[0]] + [relate(parts[k], k) for k in (1, 2, 3)]
        tokens_g = jnp.stack([tokens, tokens_side])
        tokens_g = jnp.concatenate([tokens_g, swap_core(tokens_g)])
        tokens_g = tokens_g.reshape(4 * own_count, width)
        tie([ring_m])
        ring_m.go()
        *parts, tokens_g, cotangent_ = tie([ring_a, ring_m], *parts, tokens_g, cotangent)
        ring_a.go()
        ring_m.go()
        upstream_side = swap_side(cotangent_)
        unit_up = make_unit(me, parts, [], "unit_up")
        mods = ring_m.result().astype(BF)
        ring_b = Gather(unit_up)
        (mods,) = tie([ring_a, ring_b], mods)
        ring_b.go()
        ring_a.pieces[-2:] = [ring_a.ahead, ring_a.behind]
        w_in, w_out, w_down = assemble(
            me, ring_a.pieces, planes, 2 * rows, 3 * heads * head, "join_in"
        )
        mods = jnp.concatenate(ordered(core, mods, swap_core(mods)), axis=1)
        mods = jnp.concatenate(ordered(side, mods, swap_side(mods)), axis=1)
        w_out, mods, w_in, upstream_side = tie([ring_b], w_out, mods, w_in, upstream_side)
        ring_b.go()
        w_out = w_out.reshape(2, half * head, width // 2)
        w_out_side = swap_side(w_out)
    else:
        silu_rows = lax.all_to_all(silu_cond, "dp", split_axis=1, concat_axis=0, tiled=True)
        partial = dot(silu_rows, modulate_weight)
        small = group(small)
        tokens_g = group(tokens).reshape(4 * own_count, width)
        upstream_g = group(cotangent).reshape(4 * own_count, width)
        mods = lax.psum_scatter(partial, "dp", scatter_dimension=0, tiled=True).astype(BF)
        mods = lax.all_gather(mods, "mod", axis=1, tiled=True)
        mods = stack_other_core(mods).reshape(2 * dp_items, 6 * width)
        w_in = gather_whole(attend_in).reshape(width, 3 * heads, 4, head)
        w_in = lax.dynamic_index_in_dim(w_in, cls, 2, False).reshape(width, 3 * heads * head)
        w_out = gather_whole(attend_out).reshape(heads, 4, head, width)
        w_out = jnp.swapaxes(w_out, 0, 1).reshape(4, heads * head, width)
        share = 2 * core + side
        w_up = gather_whole(feed_in).reshape(width, 2 * planes, 4, hid)
        w_up = lax.dynamic_index_in_dim(w_up, share, 2, False).reshape(width, 2 * planes * hid)
        w_down = gather_whole(feed_out).reshape(planes, 4, hid, width)
        w_down = lax.dynamic_index_in_dim(w_down, share, 1, False).reshape(planes * hid, width)
    hidden_units = planes * hid

    lengths_g = small[:, : lengths.size].reshape(seqs, items_seq)
    places_g = small[:, lengths.size :].reshape(4, 2, own_seqs, count)
    places_g = jnp.swapaxes(places_g, 1, 2).reshape(seqs, 2, count)
    ends = jnp.cumsum(lengths_g, axis=1, dtype=I32)
    spots = jnp.arange(count, dtype=I32)
    items = jnp.sum((spots[None, :, None] >= ends[:, None, :]).astype(I32), axis=2, dtype=I32)
    rel = jnp.arange(4, dtype=I32)
    base = (core ^ (rel // 2)) * dp_items + (mod ^ (rel % 2)) * own_items
    base = base[:, None] + jnp.arange(own_seqs, dtype=I32)[None, :] * items_seq
    index = base.reshape(seqs, 1) + items

    quarter = head // 4
    entry = jnp.arange(head, dtype=I32)
    freq = jnp.power(10000.0, -(entry % quarter).astype(F32) / quarter)
    spot = jnp.where(
        (entry // (head // 2))[None, :, None] == 0, places_g[:, 0:1, :], places_g[:, 1:2, :]
    ).astype(F32)
    angle = spot * freq[None, :, None]
    cosine = jnp.cos(angle)
    sine = jnp.sin(angle)
    sine = jnp.where((entry % (head // 2) < quarter)[None, :, None], -sine, sine)
    qg = jnp.broadcast_to(query_gain[:, None], (head, count))
    kg = jnp.broadcast_to(key_gain[:, None], (head, count))
    item_row, item_col = index[:, None, :], index[:, :, None]
    col = index.reshape(-1, 1)

    modded_one, raw, low, mixed = attend_forward(
        me, tokens_g, mods, w_in, cosine, sine, qg, kg, item_row, item_col, heads
    )
    if ringed:
        mixed, w_out_side = tie([ring_b], mixed, w_out_side)
        ring_b.go()
        mixed_side = swap_side(mixed)
        mixed_core = swap_core(mixed)
        upstream_g = jnp.stack([cotangent, upstream_side])
        upstream_g = jnp.concatenate([upstream_g, swap_core(upstream_g)])
        upstream_g = upstream_g.reshape(4 * own_count, width)
        w_out = jnp.concatenate(ordered(side, w_out, w_out_side), axis=2)
        w_out = jnp.stack(ordered(core, w_out, swap_core(w_out)), axis=1)
        w_out = w_out.reshape(4, heads * head, width)
        mixed_core, mixed_side, w_out, upstream_g = tie(
            [ring_b], mixed_core, mixed_side, w_out, upstream_g
        )
        ring_b.go()
        (w_up,) = assemble(me, ring_b.pieces, planes, 2 * rows, unit_up.shape[1], "join_up")
    else:
        mixed_side = swap_side(mixed)
        mixed_core = swap_core(mixed)
    mixed_all = (mixed, mixed_side, mixed_core, swap_core(mixed_side))
    modded_two, gate_up, hidden, fed_grad, own_attended = feed_forward(
        me, tokens_g, upstream_g, mods, col, mixed_all, w_out.reshape(width, width), w_up
    )

    def two_cores(part):
        part = part.reshape(2, own_count, width)
        return (part[0].astype(F32) + swap_core(part[1]).astype(F32)).astype(BF)

    down_grad = weight_grad(me, hidden, fed_grad, hidden_units // 2, "down_grad")
    if ringed:
        ring_d = Scatter(down_grad.reshape(planes, hid, width), "down_add")
        (gate_up,) = tie([ring_d], gate_up)
        ring_d.go()
    gate_up_grad, m2_far, fed_far = feed_backward(
        me, gate_up, hidden, fed_grad, w_up, w_down, 1, None
    )
    if ringed:
        gate_up_grad, m2_far, fed_far = tie([ring_d], gate_up_grad, m2_far, fed_far)
    m2_far = two_cores(m2_far)
    if ringed:
        gate_up_grad, m2_far, fed_far = tie([ring_d], gate_up_grad, m2_far, fed_far)
        ring_d.go()
    m2_side = swap_side(m2_far)
    gate_up_grad, m2_near, fed_near = feed_backward(
        me, gate_up, hidden, fed_grad, w_up, w_down, 0, gate_up_grad
    )
    m2_core = swap_core(m2_near[own_count:])
    resid_grad, attended_grad, early_sums = resid_back(
        me, tokens, cotangent, mods, col, own_attended, m2_near, m2_core, m2_side, own_items
    )
    if ringed:
        attended_grad, gate_up_grad, fed_near, fed_far, early_sums = tie(
            [ring_d], attended_grad, gate_up_grad, fed_near, fed_far, early_sums
        )
        ring_d.go()
    side_grad = swap_side(attended_grad)
    core_grad = swap_core(attended_grad)
    up_grad = weight_grad(me, modded_two, gate_up_grad, width // 3, "up_grad")
    shared = (
        w_out, w_in, raw, low, cosine, sine, qg, kg, item_row, item_col, tokens_g,
        2 * dp_items, heads,
    )
    if ringed:
        ring_u = Scatter(up_grad.reshape(planes, 2 * rows, -1), "up_add")
        core_grad, fed_near, fed_far, early_sums = tie(
            [ring_d, ring_u], core_grad, fed_near, fed_far, early_sums
        )
        ring_d.go()
        ring_u.go()
    projected_grad, m1_near, qg_near, kg_near, sums_near = attend_backward(
        me, attended_grad, core_grad, *shared, 0, None
    )
    if ringed:
        projected_grad, side_grad, fed_far, m1_near, fed_near = tie(
            [ring_d, ring_u], projected_grad, side_grad, fed_far, m1_near, fed_near
        )
    both_grad = swap_core(side_grad)
    fed_far = two_cores(fed_far)
    fed_core = swap_core(fed_near[own_count:])
    if ringed:
        projected_grad, both_grad, fed_far, fed_core = tie(
            [ring_u], projected_grad, both_grad, fed_far, fed_core
        )
        ring_u.go()
    fed_side = swap_side(fed_far)
    projected_grad, m1_far, qg_far, kg_far, sums_far = attend_backward(
        me, side_grad, both_grad, *shared, 1, projected_grad
    )
    if ringed:
        projected_grad, m1_far, sums_far, fed_side, m1_near = tie(
            [ring_u], projected_grad, m1_far, sums_far, fed_side, m1_near
        )
        ring_u.go()
        grads = attend_grads(
            me,
            modded_one,
            projected_grad,
            mixed,
            mixed_side,
            (attended_grad, side_grad, core_grad, both_grad),
            planes,
        )
        ring_i = Scatter(grads, "in_add")
        m1_far, m1_near, fed_side, sums_far = tie(
            [ring_u, ring_i], m1_far, m1_near, fed_side, sums_far
        )
        ring_u.go()
        ring_i.go()
    block_out, late_sums = output(
        me, tokens, cotangent, mods, col, own_attended, fed_near, fed_core, fed_side, own_items
    )
    gains = jnp.stack([jnp.sum(qg_near + qg_far, axis=1), jnp.sum(kg_near + kg_far, axis=1)])
    early = jnp.concatenate([early_sums, late_sums], axis=1)
    sums = sums_near + sums_far
    keep, came = sums[:dp_items], sums[dp_items:]
    sums = pick(core, keep, came) + swap_core(pick(core, came, keep))

    if ringed:

        def as_row(values):
            top = lax.reduce_precision(values, 8, 7)
            row = jnp.concatenate([top.reshape(-1), (values - top).reshape(-1)]).astype(BF)
            return jnp.pad(row, (0, 2 * width - row.shape[0]))[None]

        def from_rows(row):
            return (row[: 2 * head] + row[2 * head : 4 * head]).reshape(2, head)

        gain_row = as_row(gains)
        found = swap_side(jnp.concatenate([sums.astype(BF), gain_row], axis=0))
        sums = (sums + found[:-1].astype(F32)).astype(BF)
        gains = from_rows(jnp.sum(gain_row.astype(F32) + found[-1:].astype(F32), axis=0))
        early = jnp.concatenate(ordered(side, early, swap_side(early)), axis=0)
        unit = pick(
            side, jnp.concatenate([sums, early[:, :width]], axis=1), early[:, width:]
        )
        gain_row = jnp.pad(as_row(gains), ((0, 0), (0, mod_cols - 2 * width)))
        ring_n = Gather(jnp.concatenate([unit, gain_row], axis=0), 8)
        m1_far, m1_near = tie([ring_u, ring_i, ring_n], m1_far, m1_near)
        ring_n.go()
        ring_i.go()
        up_parts = split_sum(me, ring_u.blocks, *ring_u.last(), planes * hid, "up_split")
        m1_far, m1_near, *up_parts = tie([ring_i, ring_n], m1_far, m1_near, *up_parts)
        ring_n.go()
        ring_i.go()
        up_parts = [up_parts[0]] + [relate(up_parts[k], k) for k in (1, 2, 3)]
        m1_far, m1_near, *up_parts = tie([ring_i, ring_n], m1_far, m1_near, *up_parts)
        ring_n.go()
        ring_i.go()
        m1_far = two_cores(m1_far)
        m1_core = swap_core(m1_near[own_count:])
        feed_in_grad = unsort_columns(
            me, up_parts, hid, lambda s: (s % 2, s // 2), "unsort_up"
        )
        m1_far, m1_core = tie([ring_i, ring_n], m1_far, m1_core)
        ring_n.go()
        m1_side = swap_side(m1_far)
        down_sum = ring_d.result().astype(BF)
        left, right = down_sum[:, : width // 2], down_sum[:, width // 2 :]
        came = swap_side(pick(side, right, left))
        feed_out_grad = jnp.concatenate(
            ordered(side, pick(side, left, right), came), axis=0
        ).astype(F32)
        *parts, attend_out_grad = split_sum(
            me, ring_i.blocks, *ring_i.last(), columns_in // 4, "in_split"
        )
        parts = [parts[0]] + [relate(parts[k], k) for k in (1, 2, 3)]
        attend_in_grad = unsort_columns(
            me, parts, head, lambda s: (s // 2, s % 2), "unsort_in"
        )
    else:
        m1_side = swap_side(two_cores(m1_far))
        m1_core = swap_core(m1_near[own_count:])

        def padded(shape, value, axis, which):
            zero = jnp.zeros(shape, value.dtype)
            return lax.dynamic_update_index_in_dim(zero, value, which, axis)

        grad = down_grad.reshape(planes, hid, width)
        grad = padded((planes, 4, hid, width), grad, 1, share)
        feed_out_grad = scatter_whole(grad.reshape(4 * hidden_units, width))
        grad = up_grad.reshape(width, 2 * planes, hid)
        grad = padded((width, 2 * planes, 4, hid), grad, 2, share)
        feed_in_grad = scatter_whole(grad.reshape(width, 8 * hidden_units))
        columns = [
            pick(side, value[:, : width // 2], value[:, width // 2 :])
            for value in (attended_grad, side_grad, core_grad, both_grad)
        ]
        near_rows = dot(mixed, jnp.concatenate(columns, axis=0))
        far_rows = dot(mixed_side, jnp.concatenate([columns[k] for k in (1, 0, 3, 2)], axis=0))
        out_grad = jnp.stack(ordered(side, near_rows, far_rows)).astype(BF)
        in_grad = weight_grad(me, modded_one, projected_grad, width // 3, "in_grad")
        grad = out_grad.reshape(2, heads, head, width // 2)
        grad = jnp.swapaxes(grad, 0, 1)
        grad = padded((heads, 2, head, 2, width // 2), grad, 3, side)
        grad = padded((heads, 2, 2, head, 2, width // 2), grad, 2, core)
        attend_out_grad = scatter_whole(grad.reshape(width, width))
        grad = in_grad.reshape(width, 3 * heads, head)
        grad = padded((width, 3 * heads, 4, head), grad, 2, cls)
        attend_in_grad = scatter_whole(grad.reshape(width, 3 * width))

    tokens_grad = tokens_back(
        me, tokens, mods, col, resid_grad, m1_near, m1_core, m1_side
    )

    if ringed:
        other = [swap_core(piece) for piece in ring_n.pieces]
        modulate_grad, cond_terms, gains = mod_back(
            me, silu_rows, modulate_weight, ring_n.pieces, other, planes, dp_items
        )
        gains = from_rows(gains[0])
    else:
        sums = sums + swap_side(sums)
        found = lax.dynamic_slice_in_dim(sums, mod * own_items, own_items, 0).astype(BF)
        mod_grad = jnp.concatenate([found, early], axis=1)
        mod_grad = lax.all_to_all(mod_grad, "mod", split_axis=1, concat_axis=0, tiled=True)
        mod_grad = lax.all_gather(mod_grad, "dp", axis=0, tiled=True)
        gains = lax.psum(gains, ("dp", "mod"))
        modulate_grad = dot(silu_rows, mod_grad, 0, 0)
        cond_terms = dot(mod_grad, modulate_weight, 1, 1).astype(BF)
    cond_terms = lax.all_to_all(cond_terms, "dp", split_axis=0, concat_axis=1, tiled=True)
    own_width = width // nmod
    if ringed:
        left, right = cond_terms[:, :own_width], cond_terms[:, own_width:]
        came = swap_side(pick(side, right, left))
        cond_share = pick(side, left, right).astype(F32) + came.astype(F32)
    else:
        cond_share = lax.psum_scatter(
            cond_terms, "mod", scatter_dimension=1, tiled=True
        ).astype(F32)
    cond_cols = lax.dynamic_slice_in_dim(cond_float, mod * own_width, own_width, 1)
    cond_sigma = jax.nn.sigmoid(cond_cols)
    condition_grad = cond_share * cond_sigma * (1.0 + cond_cols * (1.0 - cond_sigma))
    return (
        block_out,
        tokens_grad,
        condition_grad,
        gains[0],
        gains[1],
        attend_in_grad,
        attend_out_grad,
        feed_in_grad,
        feed_out_grad,
        modulate_grad,
    )


def solution(mesh):
    rows = P(("dp", "mod"), None)
    both = P("dp", "mod")
    return jax.shard_map(
        body,
        mesh=mesh,
        in_specs=(
            rows,
            P("dp", None),
            rows,
            P(None, ("dp", "mod")),
            P(),
            P(),
            both,
            both,
            both,
            both,
            both,
            rows,
        ),
        out_specs=(rows, rows, both, P(), P(), both, both, both, both, both),
        check_vma=False,
    )
```

```python
import functools

import jax
import jax.numpy as jnp
from jax import lax
from jax.experimental import pallas as pl
from jax.experimental.pallas import tpu as pltpu
from jax.sharding import PartitionSpec as P

HIGHEST = lax.Precision.HIGHEST
BF = jnp.bfloat16
F32 = jnp.float32
I32 = jnp.int32
MIB = 2**20
STEP_ROWS = 128
ROOM = {
    "attend_forward": 20,
    "attend_backward": 56,
    "feed_forward": 33,
    "feed_backward": 24,
    "feed_grads": 48,
    "attend_grads": 32,
    "mod_back": 56,
    "down_grad": 32,
    "up_grad": 32,
    "in_grad": 32,
    "join_in": 20,
    "join_up": 20,
}


def layer_norm(values):
    average = jnp.mean(values, axis=-1, keepdims=True)
    centred = values - average
    spread = jnp.mean(centred * centred, axis=-1, keepdims=True)
    inverse = lax.rsqrt(spread + 1e-06)
    return (centred * inverse, inverse)


def norm_back(upstream, normed, inverse):
    first = jnp.mean(upstream, axis=-1, keepdims=True)
    second = jnp.mean(upstream * normed, axis=-1, keepdims=True)
    return inverse * (upstream - first - normed * second)


def dot(left, right, left_dim=1, right_dim=0):
    return lax.dot_general(
        left, right, (((left_dim,), (right_dim,)), ((), ())), preferred_element_type=F32
    )


def fence(*values):
    return lax.optimization_barrier(values)


def kernel_call(kernel, grid, in_specs, out_specs, out_shape, name, scratch=(), alias=None):
    return pl.pallas_call(
        kernel,
        grid_spec=pltpu.PrefetchScalarGridSpec(
            num_scalar_prefetch=1,
            grid=grid,
            in_specs=in_specs,
            out_specs=out_specs,
            scratch_shapes=list(scratch),
        ),
        out_shape=out_shape,
        input_output_aliases=alias or {},
        compiler_params=pltpu.CompilerParams(vmem_limit_bytes=ROOM.get(name, 16) * MIB),
        cost_estimate=pl.CostEstimate(flops=1024, bytes_accessed=1024, transcendentals=0),
        name=name,
    )


def whole_spec(shape):
    return pl.BlockSpec(shape, lambda *_: (0,) * len(shape))


def fixed_spec(shape):
    return pl.BlockSpec(shape, lambda *_: (0,) * len(shape), pipeline_mode=pl.Buffered(1))


def lead_spec(shape):
    return pl.BlockSpec((1,) + shape[1:], lambda i, *_: (i,) + (0,) * (len(shape) - 1))


def shaped(shape, dtype):
    return jax.ShapeDtypeStruct(shape, dtype)


def plane_of(ring, planes):
    ring = lax.rem(ring + 2 * planes, planes)
    return jnp.where(ring < planes // 2, 2 * ring, 2 * (planes - 1 - ring) + 1)


SIDE, CORE, PLACE, CLS, FIRST = 0, 1, 2, 3, 4


def sort_kernel(width, share_of, me_ref, weight_ref, *outs):
    rows, columns = weight_ref.shape
    groups = columns // (4 * width)
    for share in range(4):
        side, core = share_of(share)
        pieces = [
            weight_ref[:, (4 * g + share) * width : (4 * g + share + 1) * width]
            for g in range(groups)
        ]
        value = jnp.concatenate(pieces, axis=1)
        relation = 2 * (me_ref[CORE] ^ core) + (me_ref[SIDE] ^ side)
        for k in range(4):

            @pl.when(relation == k)
            def _(k=k, value=value):
                outs[k][...] = value


def sort_columns(me, weight, width, share_of, name):
    rows, columns = weight.shape
    return kernel_call(
        functools.partial(sort_kernel, width, share_of),
        (1,),
        [whole_spec(weight.shape)],
        [whole_spec((rows, columns // 4))] * 4,
        [shaped((rows, columns // 4), weight.dtype)] * 4,
        name,
    )(me, weight)


def quad(me_ref, refs):
    own, side, core, both = (ref[...].astype(F32) for ref in refs)
    here = me_ref[SIDE] == 0
    near = jnp.concatenate([jnp.where(here, own, side), jnp.where(here, side, own)], axis=1)
    far = jnp.concatenate([jnp.where(here, core, both), jnp.where(here, both, core)], axis=1)
    here = me_ref[CORE] == 0
    return jnp.concatenate([jnp.where(here, near, far), jnp.where(here, far, near)], axis=0)


def unit_kernel(me_ref, a_ref, b_ref, c_ref, d_ref, *rest):
    out_ref = rest[-1]
    value = quad(me_ref, (a_ref, b_ref, c_ref, d_ref)).astype(BF)
    rows, columns = value.shape
    out_ref[:rows, :columns] = value
    if len(rest) == 1:
        return
    extra = rest[0][...].astype(F32)
    half = extra.shape[1] // 2
    extra = jnp.concatenate([extra[:, :half], extra[:, half:]], axis=0).astype(BF)
    out_ref[:rows, columns:] = extra
    keep, came = rest[1][...].astype(F32), rest[2][...].astype(F32)
    here = me_ref[SIDE] == 0
    value = jnp.concatenate([jnp.where(here, keep, came), jnp.where(here, came, keep)], axis=1)
    out_ref[rows:, :] = value.astype(BF)


def make_unit(me, parts, extras, name):
    rows, columns = parts[0].shape
    high, wide = 2 * rows, 2 * columns
    if extras:
        high, wide = high + extras[1].shape[0], wide + extras[0].shape[1] // 2
    operands = list(parts) + list(extras)
    return kernel_call(
        unit_kernel,
        (1,),
        [whole_spec(v.shape) for v in operands],
        whole_spec((high, wide)),
        shaped((high, wide), BF),
        name,
    )(me, *operands)


def gather_steps(planes):
    return [0] + [s * d for d in range(1, planes // 2) for s in (-1, 1)] + [planes // 2]


def assemble_kernel(planes, rows, split, me_ref, *refs):
    pieces = len(gather_steps(planes)) + 1
    outs = refs[pieces:]
    high = refs[0].shape[0]
    for at, step in enumerate(gather_steps(planes)):
        plane = plane_of(me_ref[PLACE] + step, planes)
        if at == pieces - 2:
            value = jnp.concatenate(
                [refs[at][...].astype(F32), refs[at + 1][...].astype(F32)], axis=0
            ).astype(BF)
        else:
            value = refs[at][...]
        outs[0][pl.ds(pl.multiple_of(plane * rows, 16), rows), :] = value[:rows, :split]
        if len(outs) > 1:
            slot = lax.rem(plane, 2) * (planes // 2) + plane // 2
            extra = value[:rows, split:].astype(F32)
            extra = jnp.concatenate([extra[: rows // 2], extra[rows // 2 :]], axis=1)
            outs[1][slot] = extra.astype(BF)
            rest = high - rows
            outs[2][pl.ds(pl.multiple_of(plane * rest, 16), rest), :] = value[rows:]


def assemble(me, pieces, planes, rows, split, name):
    high, columns = pieces[0].shape
    outs = [shaped((planes * rows, split), BF)]
    if split < columns:
        outs.append(shaped((planes, rows // 2, 2 * (columns - split)), BF))
        outs.append(shaped((planes * (high - rows), columns), BF))
    return kernel_call(
        functools.partial(assemble_kernel, planes, rows, split),
        (1,),
        [whole_spec(v.shape) for v in pieces],
        [whole_spec(v.shape) for v in outs],
        outs,
        name,
    )(me, *pieces)


def mod_part_kernel(me_ref, rows_ref, weight_ref, keep_ref, send_ref):
    columns = keep_ref.shape[2]
    product = dot(rows_ref[...], weight_ref[...]).reshape(keep_ref.shape[:2] + (2 * columns,))
    here = me_ref[CORE] == 0
    left, right = product[:, :, :columns], product[:, :, columns:]
    keep_ref[...] = jnp.where(here, left, right)
    send_ref[...] = jnp.where(here, right, left).astype(BF)


def mod_part(me, rows, weight, planes):
    shape = (planes, rows.shape[0] // planes, weight.shape[1] // 2)
    return kernel_call(
        mod_part_kernel,
        (1,),
        [whole_spec(rows.shape), whole_spec(weight.shape)],
        [whole_spec(shape)] * 2,
        [shaped(shape, F32), shaped(shape, BF)],
        "mod_part",
    )(me, rows, weight)


def split_kernel(rows, columns, me_ref, own_ref, ahead_ref, behind_ref, *outs):
    height = own_ref.shape[1]
    total = own_ref[0].astype(F32) + ahead_ref[:height].astype(F32)
    total = total + behind_ref[:height].astype(F32)
    for side in range(2):
        for core in range(2):
            value = total[core * rows : (core + 1) * rows, side * columns : (side + 1) * columns]
            relation = 2 * (me_ref[CORE] ^ core) + (me_ref[SIDE] ^ side)
            for k in range(4):

                @pl.when(relation == k)
                def _(k=k, value=value):
                    outs[k][...] = value.astype(BF)

    if len(outs) == 5:
        extra = total[: 2 * rows, 2 * columns :]
        outs[4][...] = jnp.concatenate([extra[:rows], extra[rows:]], axis=1)
    if len(outs) == 6:
        low, width = outs[4].shape
        width *= 2
        value = total[2 * rows :]
        high = value.shape[0]
        tail = value[:, width:]
        step = low - high
        tail = [tail[at : at + step] for at in range(0, high, step)]
        value = jnp.concatenate([value[:, :width], jnp.concatenate(tail, axis=1)], axis=0)
        here = me_ref[SIDE] == 0
        left, right = value[:, : width // 2], value[:, width // 2 :]
        outs[4][...] = jnp.where(here, left, right).astype(BF)
        outs[5][...] = jnp.where(here, right, left).astype(BF)


def split_sum(me, blocks, ahead, behind, rows, columns, low, name):
    planes, height, wide = blocks.shape
    outs = [shaped((rows, columns), BF)] * 4
    if low:
        outs += [shaped((low, (height - 2 * rows) * wide // low // 2), BF)] * 2
    else:
        outs.append(shaped((rows, 2 * (wide - 2 * columns)), F32))
    return kernel_call(
        functools.partial(split_kernel, rows, columns),
        (1,),
        [
            pl.BlockSpec((1, height, wide), lambda i, me: (plane_of(me[PLACE], planes), 0, 0)),
            whole_spec(ahead.shape),
            whole_spec(behind.shape),
        ],
        [whole_spec(v.shape) for v in outs],
        outs,
        name,
    )(me, blocks, ahead, behind)


def unsort_kernel(width, share_of, me_ref, *refs):
    out_ref = refs[-1]
    groups = refs[0].shape[1] // width
    found = [ref[...].astype(F32) for ref in refs[:4]]
    shares = []
    for share in range(4):
        side, core = share_of(share)
        near, far = me_ref[SIDE] == side, me_ref[CORE] == core
        shares.append(
            jnp.where(
                far,
                jnp.where(near, found[0], found[1]),
                jnp.where(near, found[2], found[3]),
            )
        )
    out_ref[...] = jnp.concatenate(
        [shares[s][:, g * width : (g + 1) * width] for g in range(groups) for s in range(4)],
        axis=1,
    )


def unsort_columns(me, parts, width, share_of, name):
    rows, columns = parts[0].shape
    return kernel_call(
        functools.partial(unsort_kernel, width, share_of),
        (1,),
        [whole_spec(v.shape) for v in parts],
        whole_spec((rows, 4 * columns)),
        shaped((rows, 4 * columns), F32),
        name,
    )(me, *parts)


def attend_grads_kernel(
    planes, me_ref, modded_ref, grad_ref, mixed_ref, mixed_side_ref, a_ref, b_ref, c_ref, d_ref,
    out_ref,
):
    rows = out_ref.shape[1]
    columns = grad_ref.shape[1]
    count, width = a_ref.shape
    whole = dot(modded_ref[...], grad_ref[...], 0, 0).astype(BF)
    for plane in range(planes):
        out_ref[plane, :, :columns] = whole[plane * rows : (plane + 1) * rows]
    here = me_ref[SIDE] == 0
    blocks = [
        jnp.where(here, ref[:, : width // 2].astype(F32), ref[:, width // 2 :].astype(F32))
        for ref in (a_ref, b_ref, c_ref, d_ref)
    ]
    head = rows // 2
    half = width // 4
    for flip, ref in enumerate((mixed_ref, mixed_side_ref)):
        order = jnp.concatenate([blocks[k ^ flip] for k in range(4)], axis=0).astype(BF)
        found = dot(ref[...], order)
        for j in range(found.shape[0] // head):
            value = found[j * head : (j + 1) * head]
            value = jnp.concatenate([value[:, :half], value[:, half:]], axis=0).astype(BF)
            out_ref[2 * j + (me_ref[SIDE] ^ flip), :, columns:] = value


def attend_grads(me, modded, grad, mixed, mixed_side, attended_grads, planes):
    width = modded.shape[1]
    rows = width // planes
    out = shaped((planes, rows, grad.shape[1] + width // 4), BF)
    operands = [modded, grad, mixed, mixed_side, *attended_grads]
    return kernel_call(
        functools.partial(attend_grads_kernel, planes),
        (1,),
        [whole_spec(v.shape) for v in operands],
        whole_spec(out.shape),
        out,
        "attend_grads",
    )(me, *operands)


def ring_first_kernel(cut, me_ref, mine_ref, *refs):
    ahead_out, behind_out = refs[-2:]
    rows = mine_ref.shape[1]
    ahead_out[:cut] = mine_ref[0, :cut]
    behind_out[: rows - cut] = mine_ref[0, cut:]
    if len(refs) > 2:
        ahead_out[cut:] = refs[0][...]
        behind_out[rows - cut :] = refs[0][...]


def ring_first(me, blocks, along, cut, name):
    planes, rows, columns = blocks.shape
    more = 0 if along is None else along.shape[0]
    operands = [blocks] if along is None else [blocks, along]
    outs = [shaped((cut + more, columns), BF), shaped((rows - cut + more, columns), BF)]
    return kernel_call(
        functools.partial(ring_first_kernel, cut),
        (1,),
        [
            pl.BlockSpec(
                (1, rows, columns),
                lambda i, me: (plane_of(me[PLACE] + planes // 2, planes), 0, 0),
            ),
            *[whole_spec(v.shape) for v in operands[1:]],
        ],
        [whole_spec(v.shape) for v in outs],
        outs,
        name,
    )(me, *operands)


def ring_add_kernel(cut, me_ref, ahead_mine, behind_mine, ahead, behind, ahead_out, behind_out):
    rows = ahead_mine.shape[1]
    came = cut or rows
    ahead_out[:came] = (ahead_mine[0, :came].astype(F32) + ahead[:came].astype(F32)).astype(BF)
    if cut:
        ahead_out[cut:rows] = ahead_mine[0, cut:]
    kept = ahead_out.shape[0] - rows
    if kept:
        ahead_out[rows:] = ahead[came : came + kept]
    start = cut
    came = rows - cut
    behind_out[start:rows] = (
        behind_mine[0, start:].astype(F32) + behind[:came].astype(F32)
    ).astype(BF)
    if cut:
        behind_out[:cut] = behind_mine[0, :cut]
    if kept:
        behind_out[rows:] = behind[behind.shape[0] - kept :]


def ring_add(me, blocks, ahead, behind, step, cut, kept, name):
    planes, rows, columns = blocks.shape

    def at(sign):
        return lambda i, me: (plane_of(me[PLACE] + sign * step, planes), 0, 0)

    block = (1, rows, columns)
    out = shaped((rows + kept, columns), BF)
    return kernel_call(
        functools.partial(ring_add_kernel, cut),
        (1,),
        [
            pl.BlockSpec(block, at(1)),
            pl.BlockSpec(block, at(-1)),
            whole_spec(ahead.shape),
            whole_spec(behind.shape),
        ],
        [whole_spec(out.shape)] * 2,
        [out] * 2,
        name,
    )(me, blocks, blocks, ahead, behind)


def weight_grad_kernel(me_ref, left_ref, right_ref, out_ref):
    out_ref[...] = dot(left_ref[...], right_ref[...], 0, 0).astype(BF)


def weight_grad(me, left, right, tile, name):
    count, rows = left.shape
    columns = right.shape[1]
    return kernel_call(
        weight_grad_kernel,
        (rows // tile,),
        [pl.BlockSpec((count, tile), lambda i, *_: (0, i)), whole_spec(right.shape)],
        pl.BlockSpec((tile, columns), lambda i, *_: (i, 0)),
        shaped((rows, columns), BF),
        name,
    )(me, left, right)


def feed_grads_kernel(planes, me_ref, modded_ref, grad_ref, hidden_ref, fed_grad_ref, out_ref):
    wide = out_ref.shape[2]
    width = modded_ref.shape[1]
    rows, low = width // planes, hidden_ref.shape[1] // planes
    high = low * width // wide
    rest = wide - width
    down = dot(hidden_ref[...], fed_grad_ref[...], 0, 0)
    for plane in range(planes):
        value = down[plane * low : (plane + 1) * low]
        tail = [value[high:, at : at + rest] for at in range(0, width, rest)]
        value = jnp.concatenate([value[:high], jnp.concatenate(tail, axis=0)], axis=1)
        out_ref[plane, rows:, :] = value.astype(BF)
    up = dot(modded_ref[...], grad_ref[...], 0, 0)
    for plane in range(planes):
        out_ref[plane, :rows, :] = up[plane * rows : (plane + 1) * rows].astype(BF)


def feed_grads(me, modded, grad, hidden, fed_grad, planes):
    width, wide = modded.shape[1], grad.shape[1]
    rows = width // planes + hidden.shape[1] // planes * width // wide
    out = shaped((planes, rows, wide), BF)
    operands = [modded, grad, hidden, fed_grad]
    return kernel_call(
        functools.partial(feed_grads_kernel, planes),
        (1,),
        [whole_spec(v.shape) for v in operands],
        whole_spec(out.shape),
        out,
        "feed_grads",
    )(me, *operands)


def turned(values, first):
    quarter = values.shape[0] // 4
    ahead = pltpu.roll(values, values.shape[0] - quarter, 0)
    behind = pltpu.roll(values, quarter, 0)
    return jnp.where(first, ahead, behind)


def rms(values):
    return lax.rsqrt(jnp.mean(values * values, axis=0, keepdims=True) + 1e-06)


def scores_t(key_rot, query_rot, same, scale):
    raw = dot(key_rot, query_rot, 0, 0) * scale
    return jnp.where(same, raw, -1e30)


def softmax_t(scores):
    peak = jnp.max(scores, axis=0, keepdims=True)
    exponent = jnp.exp(scores - peak)
    return exponent / jnp.sum(exponent, axis=0, keepdims=True)


def first_mask(head, count):
    row = lax.broadcasted_iota(I32, (head, count), 0)
    return lax.rem(row, head // 2) < head // 4


def by_rows(count, work, step=STEP_ROWS):
    step = min(step, count)
    for at in range(0, count, step):
        work(slice(at, at + step))


def put_chosen(out_ref, refs, at, per):
    for k, ref in enumerate(refs):

        @pl.when(at // per == k)
        def _(ref=ref):
            out_ref[...] = ref[...]


def chosen(refs, at, per):
    value = refs[0][...]
    for k, ref in enumerate(refs[1:], 1):
        value = jnp.where(at >= k * per, ref[...], value)
    return value


def quarter_specs(shape, per, parts):
    return [
        pl.BlockSpec(shape, lambda i, *_, k=k: (jnp.clip(i - k * per, 0, per - 1), 0))
        for k in range(parts)
    ]


def join_mods_kernel(me_ref, a_ref, b_ref, c_ref, d_ref, out_ref):
    own, side, core, both = (ref[...].astype(F32) for ref in (a_ref, b_ref, c_ref, d_ref))
    here = me_ref[CORE] == 0
    near = [jnp.where(here, own, core), jnp.where(here, core, own)]
    far = [jnp.where(here, side, both), jnp.where(here, both, side)]
    here = me_ref[SIDE] == 0
    parts = [jnp.where(here, n, f) for n, f in zip(near, far)]
    parts += [jnp.where(here, f, n) for n, f in zip(near, far)]
    out_ref[...] = jnp.concatenate(parts, axis=1).astype(BF)


def join_mods(me, parts):
    items, columns = parts[0].shape
    return kernel_call(
        join_mods_kernel,
        (1,),
        [whole_spec(v.shape) for v in parts],
        whole_spec((items, 4 * columns)),
        shaped((items, 4 * columns), BF),
        "join_mods",
    )(me, *parts)


def join_out_kernel(me_ref, a_ref, b_ref, c_ref, d_ref, out_ref):
    here = me_ref[SIDE] == 0
    for other, (near, far) in enumerate(((a_ref, b_ref), (c_ref, d_ref))):
        for side in range(2):
            own, off = near[side].astype(F32), far[side].astype(F32)
            value = jnp.concatenate([jnp.where(here, own, off), jnp.where(here, off, own)], axis=1)
            out_ref[2 * side + (me_ref[CORE] ^ other)] = value.astype(BF)


def join_out(me, parts):
    _, rows, columns = parts[0].shape
    return kernel_call(
        join_out_kernel,
        (1,),
        [whole_spec(v.shape) for v in parts],
        whole_spec((4, rows, 2 * columns)),
        shaped((4, rows, 2 * columns), BF),
        "join_out",
    )(me, *parts)


def tables_kernel(dp_items, own_items, me_ref, freq_ref, *refs):
    cos_ref, sin_ref, row_ref, col_ref = refs[4:]
    head, count = freq_ref.shape
    seqs = cos_ref.shape[0] // 4
    items = own_items // seqs
    entry = lax.broadcasted_iota(I32, (head, count), 0)
    low = lax.rem(entry, head // 2) < head // 4
    for k in range(4):
        base = (me_ref[CORE] ^ (k >> 1)) * dp_items
        base += me_ref[FIRST] - me_ref[CORE] * dp_items
        base += jnp.where(me_ref[SIDE] == 0, k & 1, -(k & 1)) * own_items
        for q in range(seqs):
            at = k * seqs + q
            spots = refs[k][:2, q * count : (q + 1) * count]
            spot = jnp.where(entry < head // 2, spots[0:1], spots[1:2]).astype(F32)
            angle = spot * freq_ref[...]
            sine = jnp.sin(angle)
            cos_ref[at] = jnp.cos(angle)
            sin_ref[at] = jnp.where(low, -sine, sine)
            for ref, shape, axis in ((row_ref, (1, count), 1), (col_ref, (count, 1), 0)):
                token = lax.broadcasted_iota(I32, shape, axis)
                end = jnp.zeros((1, 1), I32)
                item = jnp.zeros(shape, I32) + (base + q * items)
                for j in range(items):
                    end = end + refs[k][2 + q : 3 + q, j : j + 1]
                    item = item + (token >= end).astype(I32)
                ref[at] = item


def make_tables(me, freq, small, seqs, dp_items, own_items):
    head, count = freq.shape
    outs = [
        shaped((seqs, head, count), F32),
        shaped((seqs, head, count), F32),
        shaped((seqs, 1, count), I32),
        shaped((seqs, count, 1), I32),
    ]
    return kernel_call(
        functools.partial(tables_kernel, dp_items, own_items),
        (1,),
        [whole_spec(v.shape) for v in (freq, *small)],
        [whole_spec(v.shape) for v in outs],
        outs,
        "tables",
    )(me, freq, *small)


def members_of(column, items):
    lane = lax.broadcasted_iota(I32, (column.shape[0], items), 1)
    return (column == lane).astype(BF)


def attend_forward_kernel(
    heads, head, me_ref, t0_ref, t1_ref, t2_ref, t3_ref, mods_ref, weight_ref, cos_ref, sin_ref,
    qg_ref, kg_ref, row_ref, col_ref, modded_ref, raw_ref, low_ref, mixed_ref, held_ref,
    tokens_ref, token_mod_ref,
):
    count, width = t0_ref.shape
    per = pl.num_programs(0) // 4
    put_chosen(tokens_ref, (t0_ref, t1_ref, t2_ref, t3_ref), pl.program_id(0), per)
    own = heads * head
    members = members_of(col_ref[0], mods_ref.shape[0])
    token_mod_ref[...] = dot(members, mods_ref[:, : 2 * width])

    def modulated(at):
        normed, _ = layer_norm(tokens_ref[at, :].astype(F32))
        modded = normed * (1.0 + token_mod_ref[at, width:]) + token_mod_ref[at, :width]
        modded_ref[at, :] = modded.astype(BF)

    by_rows(count, modulated)
    projected = dot(modded_ref[...], weight_ref[...]).T
    raw_ref[0] = projected[: 2 * own]
    values = projected[2 * own :]
    low_ref[0] = values.astype(BF)
    same = col_ref[0] == row_ref[0]
    first = first_mask(head, count)
    cosine, sine = cos_ref[0], sin_ref[0]
    scale = head ** (-0.5)

    def rotated(raw, gain):
        normed = raw * rms(raw) * gain
        return (normed * cosine + turned(normed, first) * sine).astype(BF)

    for h in range(heads):
        query_rot = rotated(projected[h * head : (h + 1) * head], qg_ref[...])
        key_rot = rotated(projected[own + h * head : own + (h + 1) * head], kg_ref[...])
        prob = softmax_t(scores_t(key_rot, query_rot, same, scale)).astype(BF)
        mixed = dot(values[h * head : (h + 1) * head].astype(BF), prob)
        held_ref[h * head : (h + 1) * head, :] = mixed
    mixed_ref[...] = held_ref[...].astype(BF)


def attend_forward(me, tokens, mods, weight, cosine, sine, qg, kg, row, col, heads):
    seqs, head, count = cosine.shape
    width = tokens[0].shape[1]
    own = heads * head
    return kernel_call(
        functools.partial(attend_forward_kernel, heads, head),
        (seqs,),
        [
            *quarter_specs((count, width), seqs // 4, 4),
            whole_spec(mods.shape),
            whole_spec(weight.shape),
            lead_spec(cosine.shape),
            lead_spec(sine.shape),
            whole_spec(qg.shape),
            whole_spec(kg.shape),
            lead_spec(row.shape),
            lead_spec(col.shape),
        ],
        [
            pl.BlockSpec((count, width), lambda i, *_: (i, 0)),
            lead_spec((seqs, 2 * own, count)),
            lead_spec((seqs, own, count)),
            pl.BlockSpec((own, count), lambda i, *_: (0, i)),
        ],
        [
            shaped((seqs * count, width), BF),
            shaped((seqs, 2 * own, count), F32),
            shaped((seqs, own, count), BF),
            shaped((own, seqs * count), BF),
        ],
        "attend_forward",
        [
            pltpu.VMEM((own, count), F32),
            pltpu.VMEM((count, width), BF),
            pltpu.VMEM((count, 2 * width), F32),
        ],
    )(me, *tokens, mods, weight, cosine, sine, qg, kg, row, col)


def attend_backward_kernel(
    heads, head, me_ref, near_ref, far_ref, out_w_ref, in_w_ref, raw_ref, low_ref, cos_ref,
    sin_ref, qg_ref, kg_ref, row_ref, col_ref, near_tokens_ref, far_tokens_ref, *rest,
):
    out_ref, m1_ref, qgg_ref, kgg_ref, sums_ref, held_ref, tokens_ref, m1_held, scaled_ref = rest[
        -9:
    ]
    own = heads * head
    half = pl.num_programs(0) // 2
    grad = chosen((near_ref, far_ref), pl.program_id(0), half)
    put_chosen(tokens_ref, (near_tokens_ref, far_tokens_ref), pl.program_id(0), half)
    count = grad.shape[0]
    mixed_grad = dot(out_w_ref[0], grad, 1, 1)
    same = col_ref[0] == row_ref[0]
    first = first_mask(head, count)
    cosine, sine = cos_ref[0], sin_ref[0]
    scale = head ** (-0.5)

    @pl.when(pl.program_id(0) == 0)
    def _():
        qgg_ref[...] = jnp.zeros_like(qgg_ref)
        kgg_ref[...] = jnp.zeros_like(kgg_ref)
        sums_ref[...] = jnp.zeros_like(sums_ref)

    def rotated(raw, gain):
        inverse = rms(raw)
        normed = raw * inverse * gain
        return inverse, (normed * cosine + turned(normed, first) * sine).astype(BF)

    def back(rot_grad, raw, inverse, gain):
        norm_grad = rot_grad * cosine + turned(rot_grad * sine, first)
        gain_grad = norm_grad * raw * inverse
        scaled = norm_grad * gain
        inner = jnp.mean(scaled * raw, axis=0, keepdims=True)
        return inverse * scaled - raw * (inverse * inverse * inverse * inner), gain_grad

    query_total = jnp.zeros((head, count), F32)
    key_total = jnp.zeros((head, count), F32)
    low = low_ref[0].astype(F32)
    for h in range(heads):
        rows = slice(h * head, (h + 1) * head)
        query_raw = raw_ref[0, h * head : (h + 1) * head]
        key_raw = raw_ref[0, own + h * head : own + (h + 1) * head]
        values = low[rows].astype(BF)
        upstream = mixed_grad[rows].astype(BF)
        query_inverse, query_rot = rotated(query_raw, qg_ref[...])
        key_inverse, key_rot = rotated(key_raw, kg_ref[...])
        prob = softmax_t(scores_t(key_rot, query_rot, same, scale))
        prob_grad = dot(values, upstream, 0, 0)
        inner = jnp.sum(prob * prob_grad, axis=0, keepdims=True)
        score_grad = (prob * (prob_grad - inner)).astype(BF)
        query_rot_grad = dot(key_rot, score_grad) * scale
        key_rot_grad = dot(query_rot, score_grad, 1, 1) * scale
        values_grad = dot(upstream, prob.astype(BF), 1, 1)
        query_grad, query_part = back(query_rot_grad, query_raw, query_inverse, qg_ref[...])
        key_grad, key_part = back(key_rot_grad, key_raw, key_inverse, kg_ref[...])
        query_total += query_part
        key_total += key_part
        held_ref[h * head : (h + 1) * head, :] = query_grad
        held_ref[own + h * head : own + (h + 1) * head, :] = key_grad
        held_ref[2 * own + h * head : 2 * own + (h + 1) * head, :] = values_grad
    qgg_ref[...] += query_total
    kgg_ref[...] += key_total
    projected_grad = held_ref[...].T.astype(BF)
    out_ref[...] = projected_grad
    m1_held[...] = dot(projected_grad, in_w_ref[...], 1, 1)

    def scaled(at):
        m1 = m1_held[at, :]
        normed, _ = layer_norm(tokens_ref[at, :].astype(F32))
        m1_ref[at, :] = m1.astype(BF)
        scaled_ref[at, :] = (m1 * normed).astype(BF)

    by_rows(count, scaled)
    members = members_of(col_ref[0], sums_ref.shape[0])
    width = m1_ref.shape[1]
    sums_ref[:, :width] += dot(members, m1_ref[...], 0, 0)
    sums_ref[:, width:] += dot(members, scaled_ref[...], 0, 0)


def attend_backward(
    me, near, far, w_out, w_in, raw, low, cosine, sine, qg, kg, row, col, tokens, items, heads,
    at, held,
):
    seqs, head, count = cosine.shape
    width = near.shape[1]
    own = heads * head
    per = seqs // 4

    def seq(i):
        return at * per + i + jnp.where(i < per, 0, per)

    def block(shape):
        return pl.BlockSpec((1,) + shape[1:], lambda i, *_: (seq(i), 0, 0))

    in_specs = [
        *quarter_specs((count, width), per, 2),
        pl.BlockSpec((1,) + w_out.shape[1:], lambda i, me: (me[CLS], 0, 0)),
        whole_spec(w_in.shape),
        block(raw.shape),
        block(low.shape),
        block(cosine.shape),
        block(sine.shape),
        whole_spec(qg.shape),
        whole_spec(kg.shape),
        block(row.shape),
        block(col.shape),
        *quarter_specs((count, width), per, 2),
    ]
    operands = [near, far, w_out, w_in, raw, low, cosine, sine, qg, kg, row, col]
    operands += [tokens[at], tokens[at + 2]]
    alias = {}
    if held is not None:
        alias = {1 + len(operands): 0}
        operands.append(held)
        in_specs.append(pl.BlockSpec(memory_space=pl.ANY))
    return kernel_call(
        functools.partial(attend_backward_kernel, heads, head),
        (2 * per,),
        in_specs,
        [
            pl.BlockSpec((count, 3 * own), lambda i, *_: (seq(i), 0)),
            pl.BlockSpec((count, width), lambda i, *_: (i, 0)),
            whole_spec((head, count)),
            whole_spec((head, count)),
            whole_spec((items, 2 * width)),
        ],
        [
            shaped((seqs * count, 3 * own), BF),
            shaped((2 * per * count, width), BF),
            shaped((head, count), F32),
            shaped((head, count), F32),
            shaped((items, 2 * width), F32),
        ],
        "attend_backward",
        [
            pltpu.VMEM((3 * own, count), F32),
            pltpu.VMEM((count, width), BF),
            pltpu.VMEM((count, width), F32),
            pltpu.VMEM((count, width), BF),
        ],
        alias,
    )(me, *operands)


def feed_forward_kernel(me_ref, *refs):
    mods_ref, col_ref, m0_ref, m1_ref, m2_ref, m3_ref, w_out_ref, w_up_ref = refs[8:16]
    modded_ref, gate_up_ref, hidden_ref, fed_grad_ref, attended_ref = refs[16:21]
    mixed_ref, tokens_ref, upstream_ref, held_ref, token_mod_ref = refs[21:]
    put_chosen(tokens_ref, refs[:4], pl.program_id(0), 1)
    put_chosen(upstream_ref, refs[4:8], pl.program_id(0), 1)
    count, width = tokens_ref.shape
    own = m0_ref.shape[0]
    for k, ref in enumerate((m0_ref, m1_ref, m2_ref, m3_ref)):
        cls = 2 * (me_ref[SIDE] ^ (k & 1)) + (me_ref[CORE] ^ (k >> 1))
        mixed_ref[pl.ds(pl.multiple_of(cls * own, 16), own), :] = ref[...]
    held_ref[...] = dot(mixed_ref[...], w_out_ref[...], 0, 0)

    @pl.when(pl.program_id(0) == 0)
    def _():
        attended_ref[...] = held_ref[...]

    members = members_of(col_ref[...].reshape(-1, 1), mods_ref.shape[0])
    token_mod_ref[...] = dot(members, mods_ref[:, 2 * width :])

    def modulated(at):
        resid = tokens_ref[at, :].astype(F32) + token_mod_ref[at, :width] * held_ref[at, :]
        normed, _ = layer_norm(resid)
        scale = token_mod_ref[at, 2 * width : 3 * width]
        modded = normed * (1.0 + scale) + token_mod_ref[at, width : 2 * width]
        modded_ref[at, :] = modded.astype(BF)
        grad = token_mod_ref[at, 3 * width :] * upstream_ref[at, :].astype(F32)
        fed_grad_ref[at, :] = grad.astype(BF)

    by_rows(count, modulated)
    gate_up_ref[...] = dot(modded_ref[...], w_up_ref[...])
    units = hidden_ref.shape[1]

    def activated(at):
        gate, up = gate_up_ref[at, :units], gate_up_ref[at, units:]
        hidden_ref[at, :] = (gate * jax.nn.sigmoid(gate) * up).astype(BF)

    by_rows(count, activated)


def feed_forward(me, tokens, upstream, mods, col, mixed, w_out, w_up):
    count, width = tokens[0].shape
    total = 4 * count
    own = mixed[0].shape[0]
    per = col.shape[0] // 4
    columns = w_up.shape[1]

    def rows(n):
        return pl.BlockSpec((count, n), lambda j, *_: (j, 0))

    def mixed_spec(k):
        return pl.BlockSpec((own, count), lambda j, *_: (0, j ^ k))

    return kernel_call(
        feed_forward_kernel,
        (4,),
        [
            *[fixed_spec((count, width))] * 8,
            fixed_spec(mods.shape),
            pl.BlockSpec((per,) + col.shape[1:], lambda j, *_: (j, 0, 0)),
            *(mixed_spec(k) for k in range(4)),
            fixed_spec(w_out.shape),
            fixed_spec(w_up.shape),
        ],
        [
            rows(width),
            rows(columns),
            rows(columns // 2),
            rows(width),
            whole_spec((count, width)),
        ],
        [
            shaped((total, width), BF),
            shaped((total, columns), F32),
            shaped((total, columns // 2), BF),
            shaped((total, width), BF),
            shaped((count, width), F32),
        ],
        "feed_forward",
        [
            pltpu.VMEM((4 * own, count), BF),
            pltpu.VMEM((count, width), BF),
            pltpu.VMEM((count, width), BF),
            pltpu.VMEM((count, width), F32),
            pltpu.VMEM((count, 4 * width), F32),
        ],
    )(me, *tokens, *upstream, mods, col, *mixed, w_out, w_up)


def feed_backward_kernel(
    me_ref, gate_up_ref, hidden_ref, fed_grad_ref, w_up_ref, w_down_ref, *rest
):
    grad_ref, m2_ref, fed_ref, held_ref = rest[-4:]
    held_ref[...] = dot(fed_grad_ref[...], w_down_ref[...], 1, 1)
    count, units = held_ref.shape

    def back(at):
        hidden_grad = held_ref[at, :]
        gate, up = gate_up_ref[at, :units], gate_up_ref[at, units:]
        sigma = jax.nn.sigmoid(gate)
        slope = sigma * (1.0 + gate * (1.0 - sigma))
        grad_ref[at, :units] = (hidden_grad * up * slope).astype(BF)
        grad_ref[at, units:] = (hidden_grad * (gate * sigma)).astype(BF)

    by_rows(count, back)
    m2_ref[...] = dot(grad_ref[...], w_up_ref[...], 1, 1).astype(BF)
    fed_ref[...] = dot(hidden_ref[...], w_down_ref[...]).astype(BF)


def feed_backward(me, gate_up, hidden, fed_grad, w_up, w_down, at, held):
    total, columns = gate_up.shape
    width = fed_grad.shape[1]
    count = total // 4

    def rows(n):
        return pl.BlockSpec((count, n), lambda j, *_: (2 * j + at, 0))

    out = pl.BlockSpec((count, width), lambda j, *_: (j, 0))
    in_specs = [
        rows(columns),
        rows(columns // 2),
        rows(width),
        fixed_spec(w_up.shape),
        fixed_spec(w_down.shape),
    ]
    operands = [gate_up, hidden, fed_grad, w_up, w_down]
    alias = {}
    if held is not None:
        alias = {1 + len(operands): 0}
        operands.append(held)
        in_specs.append(pl.BlockSpec(memory_space=pl.ANY))
    return kernel_call(
        feed_backward_kernel,
        (2,),
        in_specs,
        [rows(columns), out, out],
        [
            shaped((total, columns), BF),
            shaped((2 * count, width), BF),
            shaped((2 * count, width), BF),
        ],
        "feed_backward",
        [pltpu.VMEM((count, columns // 2), F32)],
        alias,
    )(me, *operands)


def own_sums(me_ref, column, sums_ref, *terms):
    lane = lax.broadcasted_iota(I32, (column.shape[0], sums_ref.shape[0]), 1)
    members = (column - me_ref[FIRST] == lane).astype(BF)
    width = terms[0].shape[1]
    for at, term in enumerate(terms):
        sums_ref[:, at * width : (at + 1) * width] = dot(members, term[...], 0, 0).astype(BF)


def resid_kernel(
    me_ref, tokens_ref, upstream_ref, mods_ref, col_ref, attended_ref, near_ref, core_ref,
    side_ref, grad_ref, out_ref, sums_ref, token_mod_ref, gate_sum_ref, shift_sum_ref,
    scale_sum_ref,
):
    count, width = tokens_ref.shape
    column = col_ref[...].reshape(-1, 1)
    members = members_of(column, mods_ref.shape[0])
    token_mod_ref[:, :width] = dot(members, mods_ref[:, 2 * width : 3 * width])
    token_mod_ref[:, width:] = dot(members, mods_ref[:, 4 * width : 5 * width])

    def back(at):
        attended = attended_ref[at, :]
        resid = tokens_ref[at, :].astype(F32) + token_mod_ref[at, :width] * attended
        normed, inverse = layer_norm(resid)
        m2 = near_ref[at, :].astype(F32) + core_ref[at, :].astype(F32)
        m2 = m2 + side_ref[at, :].astype(F32)
        shift_sum_ref[at, :] = m2.astype(BF)
        scale_sum_ref[at, :] = (m2 * normed).astype(BF)
        grad = norm_back(m2 * (1.0 + token_mod_ref[at, width:]), normed, inverse)
        grad = grad + upstream_ref[at, :].astype(F32)
        grad_ref[at, :] = grad
        out_ref[at, :] = (token_mod_ref[at, :width] * grad).astype(BF)
        gate_sum_ref[at, :] = (grad * attended).astype(BF)

    by_rows(count, back)
    own_sums(me_ref, column, sums_ref, gate_sum_ref, shift_sum_ref, scale_sum_ref)


def resid_back(me, tokens, upstream, mods, col, attended, near, core, side, items):
    count, width = tokens.shape
    block = pl.BlockSpec((count, width), lambda i, *_: (0, 0))
    return kernel_call(
        resid_kernel,
        (1,),
        [
            block,
            block,
            whole_spec(mods.shape),
            pl.BlockSpec((col.shape[0] // 4,) + col.shape[1:], lambda i, *_: (0, 0, 0)),
            block,
            block,
            block,
            block,
        ],
        [block, block, whole_spec((items, 3 * width))],
        [
            shaped((count, width), F32),
            shaped((count, width), BF),
            shaped((items, 3 * width), BF),
        ],
        "resid_back",
        [pltpu.VMEM((count, 2 * width), F32)] + [pltpu.VMEM((count, width), BF)] * 3,
    )(me, tokens, upstream, mods, col, attended, near, core, side)


def output_kernel(
    me_ref, tokens_ref, upstream_ref, mods_ref, col_ref, attended_ref, near_ref, core_ref,
    side_ref, out_ref, sums_ref, token_mod_ref, gate_sum_ref,
):
    count, width = tokens_ref.shape
    column = col_ref[...].reshape(-1, 1)
    members = members_of(column, mods_ref.shape[0])
    token_mod_ref[:, :width] = dot(members, mods_ref[:, 2 * width : 3 * width])
    token_mod_ref[:, width:] = dot(members, mods_ref[:, 5 * width :])

    def add(at):
        fed = near_ref[at, :].astype(F32) + core_ref[at, :].astype(F32)
        fed = fed + side_ref[at, :].astype(F32)
        resid = tokens_ref[at, :].astype(F32) + token_mod_ref[at, :width] * attended_ref[at, :]
        out_ref[at, :] = (resid + token_mod_ref[at, width:] * fed).astype(BF)
        gate_sum_ref[at, :] = (upstream_ref[at, :].astype(F32) * fed).astype(BF)

    by_rows(count, add)
    own_sums(me_ref, column, sums_ref, gate_sum_ref)


def output(me, tokens, upstream, mods, col, attended, near, core, side, items):
    count, width = tokens.shape
    block = pl.BlockSpec((count, width), lambda i, *_: (0, 0))
    return kernel_call(
        output_kernel,
        (1,),
        [
            block,
            block,
            whole_spec(mods.shape),
            pl.BlockSpec((col.shape[0] // 4,) + col.shape[1:], lambda i, *_: (0, 0, 0)),
            block,
            block,
            block,
            block,
        ],
        [block, whole_spec((items, width))],
        [shaped((count, width), BF), shaped((items, width), BF)],
        "output",
        [pltpu.VMEM((count, 2 * width), F32), pltpu.VMEM((count, width), BF)],
    )(me, tokens, upstream, mods, col, attended, near, core, side)


def tokens_kernel(
    me_ref, tokens_ref, mods_ref, col_ref, resid_ref, near_ref, core_ref, side_ref, out_ref,
    scale_ref,
):
    count, width = tokens_ref.shape
    members = members_of(col_ref[...].reshape(-1, 1), mods_ref.shape[0])
    scale_ref[...] = dot(members, mods_ref[:, width : 2 * width])

    def back(at):
        normed, inverse = layer_norm(tokens_ref[at, :].astype(F32))
        m1 = near_ref[at, :].astype(F32) + core_ref[at, :].astype(F32)
        m1 = (m1 + side_ref[at, :].astype(F32)) * (1.0 + scale_ref[at, :])
        out_ref[at, :] = resid_ref[at, :] + norm_back(m1, normed, inverse)

    by_rows(count, back)


def tokens_back(me, tokens, mods, col, resid_grad, near, core, side):
    count, width = tokens.shape
    block = pl.BlockSpec((count, width), lambda i, *_: (0, 0))
    return kernel_call(
        tokens_kernel,
        (1,),
        [
            block,
            whole_spec(mods.shape),
            pl.BlockSpec((col.shape[0] // 4,) + col.shape[1:], lambda i, *_: (0, 0, 0)),
            block,
            block,
            block,
            block,
        ],
        block,
        shaped((count, width), F32),
        "tokens_back",
        [pltpu.VMEM((count, width), F32)],
    )(me, tokens, mods, col, resid_grad, near, core, side)


def mod_back_kernel(planes, items, me_ref, rows_ref, weight_ref, *refs):
    count = len(gather_steps(planes)) + 1
    pieces = refs[: 2 * count]
    grad_ref, terms_ref, gains_ref, held_ref = refs[2 * count :]
    more, width = refs[0].shape
    gains = jnp.zeros((1, width), F32)
    for at, step in enumerate(gather_steps(planes)):
        plane = plane_of(me_ref[PLACE] + step, planes)
        for other in range(2):
            refs = pieces[other * count + at : other * count + at + 2]
            if at == count - 2:
                value = jnp.concatenate(
                    [ref[ref.shape[0] - more // 2 :].astype(F32) for ref in refs], axis=0
                )
            else:
                value = refs[0][refs[0].shape[0] - more :].astype(F32)
            row = (2 * plane + (me_ref[CORE] ^ other)) * items
            row = pl.ds(pl.multiple_of(row, items), items)
            for part in range(weight_ref.shape[1] // width):
                held_ref[row, part * width : (part + 1) * width] = value[
                    part * items : (part + 1) * items
                ].astype(BF)
            at_gain = held_ref.shape[1] // width * items
            gains += value[at_gain : at_gain + 1]
    grad_ref[...] = dot(rows_ref[...], held_ref[...], 0, 0)
    terms_ref[...] = dot(held_ref[...], weight_ref[...], 1, 1).astype(BF)
    gains_ref[...] = gains


def mod_back(me, rows, weight, own, other, planes, items):
    pieces = list(own) + list(other)
    outs = [shaped(weight.shape, F32), shaped(rows.shape, BF), shaped((1, own[0].shape[1]), F32)]
    return kernel_call(
        functools.partial(mod_back_kernel, planes, items),
        (1,),
        [whole_spec(v.shape) for v in (rows, weight, *pieces)],
        [whole_spec(v.shape) for v in outs],
        outs,
        "mod_back",
        [pltpu.VMEM((rows.shape[0], weight.shape[1]), BF)],
    )(me, rows, weight, *pieces)


def body(
    tokens,
    condition,
    lengths,
    positions,
    query_gain,
    key_gain,
    attend_in,
    attend_out,
    feed_in,
    feed_out,
    modulate_weight,
    cotangent,
):
    ndp, nmod = lax.axis_size("dp"), lax.axis_size("mod")
    planes = ndp // 2
    half = planes // 2
    dp, mod = lax.axis_index("dp"), lax.axis_index("mod")
    core, plane, side = dp % 2, dp // 2, mod % 2
    own_seqs, items_seq = lengths.shape
    own_count, width = tokens.shape
    count = own_count // own_seqs
    seqs = 4 * own_seqs
    head = query_gain.shape[0]
    heads = width // head // 4
    cls = 2 * side + core
    own_items = own_seqs * items_seq
    dp_items = condition.shape[0]
    ringed = nmod == 2 and attend_out.shape[0] == head
    hid = feed_out.shape[0] // 2
    place = jnp.where(plane % 2 == 0, plane // 2, planes - 1 - plane // 2)
    first_item = core * dp_items + mod * own_items
    me = jnp.stack([side, core, place, cls, first_item]).astype(I32)

    def relate(value, k):
        pairs = [
            (d * nmod + m, (d ^ (k >> 1)) * nmod + (m ^ (k & 1)))
            for d in range(ndp)
            for m in range(nmod)
        ]
        return lax.ppermute(value, ("dp", "mod"), pairs)

    def swap_core(value):
        return relate(value, 2)

    def swap_side(value):
        return relate(value, 1)

    def pick(which, pair0, pair1):
        return jnp.where(which == 0, pair0, pair1)

    def ordered(which, own, other):
        return pick(which, own, other), pick(which, other, own)

    def static_plane(ring):
        ring %= planes
        return 2 * ring if ring < half else 2 * (planes - 1 - ring) + 1

    def hop(value, step):
        pairs = [
            (2 * static_plane(r) + c, 2 * static_plane(r + step) + c)
            for r in range(planes)
            for c in range(2)
        ]
        return lax.ppermute(value, "dp", pairs)

    class Gather:
        def __init__(self, block, cut=None):
            self.pieces = [block]
            self.cut = block.shape[0] // 32 * 16 if cut is None else cut
            self.ahead = self.behind = block
            self.step = 0

        def go(self):
            self.step += 1
            if self.step == half:
                self.ahead, self.behind = self.ahead[: self.cut], self.behind[self.cut :]
            self.ahead, self.behind = hop(self.ahead, 1), hop(self.behind, -1)
            self.pieces += [self.ahead, self.behind]

    class Scatter:
        def __init__(self, blocks, name, along=None):
            self.blocks, self.name = blocks, name
            self.rows = blocks.shape[1]
            self.cut = self.rows // 32 * 16
            self.more = 0 if along is None else along.shape[0]
            self.pieces = [along]
            self.step = half
            if name:
                self.ahead, self.behind = ring_first(
                    me, blocks, along, self.cut, name + "_first"
                )
            else:
                far = self.take(half)
                self.ahead, self.behind = far[: self.cut], far[self.cut :]

        def take(self, step):
            start = (plane_of(place + step, planes), 0, 0)
            return lax.dynamic_slice(self.blocks, start, (1,) + self.blocks.shape[1:])[0]

        def go(self):
            self.hop()
            self.add()

        def hop(self):
            self.ahead, self.behind = hop(self.ahead, 1), hop(self.behind, -1)
            self.pieces += [self.ahead, self.behind]
            self.step -= 1

        def add(self):
            if self.step == 0:
                return
            cut = self.cut if self.step == half - 1 else 0
            if self.name:
                self.ahead, self.behind = ring_add(
                    me,
                    self.blocks,
                    self.ahead,
                    self.behind,
                    self.step,
                    cut,
                    self.more // 2 if self.step == 1 else self.more,
                    self.name,
                )
                return
            mine = self.take(self.step).astype(F32), self.take(-self.step).astype(F32)
            if cut:
                self.ahead = jnp.pad(self.ahead, ((0, self.rows - cut), (0, 0)))
                self.behind = jnp.pad(self.behind, ((cut, 0), (0, 0)))
            self.ahead = (mine[0] + self.ahead.astype(F32)).astype(BF)
            self.behind = (mine[1] + self.behind.astype(F32)).astype(BF)

        def last(self):
            return self.ahead, self.behind

        def result(self):
            return self.take(0).astype(F32) + self.ahead.astype(F32) + self.behind.astype(F32)

    def tie(rings, *values):
        state = [v for ring in rings for v in (ring.ahead, ring.behind)]
        out = list(lax.optimization_barrier(tuple(state) + values))
        for at, ring in enumerate(rings):
            ring.ahead, ring.behind = out[2 * at : 2 * at + 2]
        return out[2 * len(rings) :]

    def gather_whole(weight):
        return lax.all_gather(
            lax.all_gather(weight, "mod", axis=1, tiled=True), "dp", axis=0, tiled=True
        )

    def scatter_whole(padded):
        padded = lax.psum_scatter(padded.astype(BF), "mod", scatter_dimension=1, tiled=True)
        return lax.psum_scatter(padded, "dp", scatter_dimension=0, tiled=True).astype(F32)

    def stack_other_core(value):
        return jnp.stack(ordered(core, value, swap_core(value)))

    def group(value):
        other = swap_side(value)
        return [value, other, swap_core(value), swap_core(other)]

    columns_in = attend_in.shape[1]
    rows = feed_in.shape[0]
    out_slot = lambda index: lax.rem(index, 2) * half + index // 2
    cond_float = condition.astype(F32)
    silu_cond = jax.nn.silu(cond_float).astype(BF)
    mod_cols = modulate_weight.shape[1]
    small = jnp.pad(lengths, ((0, 0), (0, own_count - items_seq)))
    small = jnp.concatenate([positions, small], axis=0)
    quarter = head // 4
    entry = jnp.arange(head, dtype=I32)
    freq = jnp.power(10000.0, -(entry % quarter).astype(F32) / quarter)
    freq = jnp.broadcast_to(freq[:, None], (head, count))

    if ringed:
        silu_rows = lax.all_to_all(silu_cond, "dp", split_axis=1, concat_axis=0, tiled=True)
        silu_rows, attend_in_, feed_out_ = tie([], silu_rows, attend_in, feed_out)
        parts = sort_columns(me, attend_in_, head, lambda s: (s // 2, s % 2), "sort_in")
        keep = pick(side, feed_out_[:hid], feed_out_[hid:])
        came = swap_side(pick(side, feed_out_[hid:], feed_out_[:hid]))
        parts = [parts[0]] + [relate(parts[k], k) for k in (1, 2, 3)]
        kept, sent = mod_part(me, silu_rows, modulate_weight, planes)
        ring_a = Gather(make_unit(me, parts, [attend_out, keep, came], "unit_in"))
        kept, sent, small, tokens_ = tie([ring_a], kept, sent, small, tokens)
        ring_a.go()
        small_side = swap_side(small)
        tokens_side = swap_side(tokens_)
        ring_m = Scatter((kept + swap_core(sent).astype(F32)).astype(BF), "")
        small_side, feed_in_ = tie([ring_a, ring_m], small_side, feed_in)
        ring_a.go()
        ring_m.hop()
        small = [small, small_side, swap_core(small), swap_core(small_side)]
        parts = sort_columns(me, feed_in_, hid, lambda s: (s % 2, s // 2), "sort_up")
        tokens_side, cotangent_, *parts = tie([ring_a, ring_m], tokens_side, cotangent, *parts)
        ring_m.add()
        ring_a.go()
        ring_m.hop()
        parts = [parts[0]] + [relate(parts[k], k) for k in (1, 2, 3)]
        tokens_g = [tokens, tokens_side, swap_core(tokens), swap_core(tokens_side)]
        upstream_side = swap_side(cotangent_)
        small = tie([ring_a, ring_m], *small)
        ring_m.add()
        ring_a.go()
        ring_m.hop()
        ring_b = Gather(make_unit(me, parts, [], "unit_up"))
        tabled = make_tables(me, freq, small, seqs, dp_items, own_items)
        tabled = tie([ring_a, ring_b, ring_m], *tabled)
        ring_m.add()
        ring_b.go()
        ring_m.hop()
        ring_a.pieces[-2:] = [ring_a.ahead, ring_a.behind]
        w_in, w_out, w_down = assemble(
            me, ring_a.pieces, planes, 2 * rows, 3 * heads * head, "join_in"
        )
        w_out, w_in, upstream_side = tie([ring_b, ring_m], w_out, w_in, upstream_side)
        mods = group(ring_m.result().astype(BF))
        ring_b.go()
        w_out, *mods = tie([ring_b], w_out, *mods)
        mods = join_mods(me, mods)
        ring_b.go()
        w_out = w_out.reshape(2, half * head, width // 2)
        w_out_side = swap_side(w_out)
    else:
        silu_rows = lax.all_to_all(silu_cond, "dp", split_axis=1, concat_axis=0, tiled=True)
        partial = dot(silu_rows, modulate_weight)
        tabled = make_tables(me, freq, group(small), seqs, dp_items, own_items)
        tokens_g = group(tokens)
        upstream_g = group(cotangent)
        mods = lax.psum_scatter(partial, "dp", scatter_dimension=0, tiled=True).astype(BF)
        mods = lax.all_gather(mods, "mod", axis=1, tiled=True)
        mods = stack_other_core(mods).reshape(2 * dp_items, 6 * width)
        w_in = gather_whole(attend_in).reshape(width, 3 * heads, 4, head)
        w_in = lax.dynamic_index_in_dim(w_in, cls, 2, False).reshape(width, 3 * heads * head)
        w_out = gather_whole(attend_out).reshape(heads, 4, head, width)
        w_out = jnp.swapaxes(w_out, 0, 1).reshape(4, heads * head, width)
        share = 2 * core + side
        w_up = gather_whole(feed_in).reshape(width, 2 * planes, 4, hid)
        w_up = lax.dynamic_index_in_dim(w_up, share, 2, False).reshape(width, 2 * planes * hid)
        w_down = gather_whole(feed_out).reshape(planes, 4, hid, width)
        w_down = lax.dynamic_index_in_dim(w_down, share, 1, False).reshape(planes * hid, width)
    hidden_units = planes * hid

    cosine, sine, item_row, col = tabled
    item_col = col
    qg = jnp.broadcast_to(query_gain[:, None], (head, count))
    kg = jnp.broadcast_to(key_gain[:, None], (head, count))
    modded_one, raw, low, mixed = attend_forward(
        me, tokens_g, mods, w_in, cosine, sine, qg, kg, item_row, item_col, heads
    )
    if ringed:
        mixed, w_out_side = tie([ring_b], mixed, w_out_side)
        ring_b.go()
        mixed_side = swap_side(mixed)
        mixed_core = swap_core(mixed)
        upstream_g = [
            cotangent, upstream_side, swap_core(cotangent), swap_core(upstream_side)
        ]
        w_out = join_out(me, [w_out, w_out_side, swap_core(w_out), swap_core(w_out_side)])
        mixed_side, w_out, mixed_core, *upstream_g = tie(
            [ring_b], mixed_side, w_out, mixed_core, *upstream_g
        )
        ring_b.pieces[-2:] = [ring_b.ahead, ring_b.behind]
        (w_up,) = assemble(me, ring_b.pieces, planes, 2 * rows, ring_b.pieces[0].shape[1], "join_up")
    else:
        mixed_side = swap_side(mixed)
        mixed_core = swap_core(mixed)
    mixed_all = (mixed, mixed_side, mixed_core, swap_core(mixed_side))
    modded_two, gate_up, hidden, fed_grad, own_attended = feed_forward(
        me, tokens_g, upstream_g, mods, col, mixed_all, w_out.reshape(width, width), w_up
    )

    def two_cores(part):
        part = part.reshape(2, own_count, width)
        return (part[0].astype(F32) + swap_core(part[1]).astype(F32)).astype(BF)

    gate_up_grad, m2_far, fed_far = feed_backward(
        me, gate_up, hidden, fed_grad, w_up, w_down, 1, None
    )
    m2_far = two_cores(m2_far)
    if ringed:
        gate_up_grad, m2_far, fed_far = tie([], gate_up_grad, m2_far, fed_far)
    m2_side = swap_side(m2_far)
    gate_up_grad, m2_near, fed_near = feed_backward(
        me, gate_up, hidden, fed_grad, w_up, w_down, 0, gate_up_grad
    )
    if ringed:
        gate_up_grad, m2_near, fed_near = tie([], gate_up_grad, m2_near, fed_near)
        m2_core = swap_core(m2_near[own_count:])
        grads = feed_grads(me, modded_two, gate_up_grad, hidden, fed_grad, planes)
        ring_u = Scatter(grads, "up_add")
        fed_far = two_cores(fed_far)
        m2_side, m2_core, fed_near, fed_far = tie([ring_u], m2_side, m2_core, fed_near, fed_far)
        ring_u.hop()
    else:
        m2_core = swap_core(m2_near[own_count:])
        fed_far = two_cores(fed_far)
    resid_grad, attended_grad, early_sums = resid_back(
        me, tokens, cotangent, mods, col, own_attended, m2_near, m2_core, m2_side, own_items
    )
    side_grad = swap_side(attended_grad)
    core_grad = swap_core(attended_grad)
    shared = (
        w_out, w_in, raw, low, cosine, sine, qg, kg, item_row, item_col, tokens_g,
        2 * dp_items, heads,
    )
    projected_grad, m1_near, qg_near, kg_near, sums_near = attend_backward(
        me, attended_grad, core_grad, *shared, 0, None
    )
    if ringed:
        projected_grad, side_grad, fed_far, m1_near, fed_near = tie(
            [ring_u], projected_grad, side_grad, fed_far, m1_near, fed_near
        )
        ring_u.add()
    both_grad = swap_core(side_grad)
    fed_core = swap_core(fed_near[own_count:])
    if ringed:
        projected_grad, both_grad, fed_far = tie([ring_u], projected_grad, both_grad, fed_far)
        ring_u.hop()
    fed_side = swap_side(fed_far)
    projected_grad, m1_far, qg_far, kg_far, sums_far = attend_backward(
        me, side_grad, both_grad, *shared, 1, projected_grad
    )
    if ringed:
        projected_grad, m1_far, sums_far, fed_side, m1_near = tie(
            [ring_u], projected_grad, m1_far, sums_far, fed_side, m1_near
        )
        ring_u.add()
    gains = jnp.stack([jnp.sum(qg_near + qg_far, axis=1), jnp.sum(kg_near + kg_far, axis=1)])
    sums = sums_near + sums_far
    keep, came = sums[:dp_items], sums[dp_items:]
    sums = pick(core, keep, came) + swap_core(pick(core, came, keep))

    def as_row(values):
        top = lax.reduce_precision(values, 8, 7)
        row = jnp.concatenate([top.reshape(-1), (values - top).reshape(-1)]).astype(BF)
        return jnp.pad(row, (0, 2 * width - row.shape[0]))[None]

    def from_rows(row):
        return (row[: 2 * head] + row[2 * head : 4 * head]).reshape(2, head)

    if not ringed:
        block_out, late_sums = output(
            me, tokens, cotangent, mods, col, own_attended, fed_near, fed_core, fed_side, own_items
        )
        early = jnp.concatenate([early_sums, late_sums], axis=1)

    if ringed:
        gain_row = as_row(gains)
        found = swap_side(jnp.concatenate([sums.astype(BF), gain_row], axis=0))
        projected_grad, m1_far, m1_near = tie([ring_u], projected_grad, m1_far, m1_near)
        ring_u.hop()
        grads = attend_grads(
            me,
            modded_one,
            projected_grad,
            mixed,
            mixed_side,
            (attended_grad, side_grad, core_grad, both_grad),
            planes,
        )
        block_out, late_sums = output(
            me, tokens, cotangent, mods, col, own_attended, fed_near, fed_core, fed_side,
            own_items,
        )
        early = jnp.concatenate([early_sums, late_sums], axis=1)
        grads, m1_far, m1_near, found, early = tie(
            [ring_u], grads, m1_far, m1_near, found, early
        )
        ring_u.add()
        early_side = swap_side(early)
        sums = (sums + found[:-1].astype(F32)).astype(BF)
        gains = from_rows(jnp.sum(gain_row.astype(F32) + found[-1:].astype(F32), axis=0))
        early = jnp.concatenate(ordered(side, early, early_side), axis=0)
        parts = [
            pick(side, sums[:, :width], early[:, width : 2 * width]),
            pick(side, sums[:, width:], early[:, 2 * width : 3 * width]),
            pick(side, early[:, :width], early[:, 3 * width :]),
            as_row(gains)[:, :width],
        ]
        along = jnp.concatenate(parts, axis=0)
        along = jnp.pad(along, ((0, 64 - along.shape[0]), (0, 0)))
        ring_i = Scatter(grads, "in_add", along)
        m1_far, m1_near = tie([ring_u, ring_i], m1_far, m1_near)
        ring_u.hop()
        ring_i.hop()
        m1_far = two_cores(m1_far)
        m1_core = swap_core(m1_near[own_count:])
        m1_far, m1_core = tie([ring_u, ring_i], m1_far, m1_core)
        ring_i.add()
        ring_i.hop()
        m1_side = swap_side(m1_far)
        *up_parts, keep, came = split_sum(
            me, ring_u.blocks, *ring_u.last(), rows, planes * hid, hid, "up_split"
        )
        m1_side, came, *up_parts = tie([ring_i], m1_side, came, *up_parts)
        ring_i.add()
        ring_i.hop()
        up_parts = [up_parts[0]] + [relate(up_parts[k], k) for k in (1, 2, 3)]
        came = swap_side(came)
        tokens_grad = tokens_back(
            me, tokens, mods, col, resid_grad, m1_near, m1_core, m1_side
        )
        tokens_grad, came, *up_parts = tie([ring_i], tokens_grad, came, *up_parts)
        ring_i.add()
        ring_i.hop()
        feed_in_grad = unsort_columns(
            me, up_parts, hid, lambda s: (s % 2, s // 2), "unsort_up"
        )
        feed_out_grad = jnp.concatenate(ordered(side, keep, came), axis=0).astype(F32)
        feed_in_grad, feed_out_grad = tie([ring_i], feed_in_grad, feed_out_grad)
        ring_i.pieces[-2:] = [ring_i.ahead, ring_i.behind]
        other = [swap_core(piece) for piece in ring_i.pieces]
        modulate_grad, cond_terms, gains = mod_back(
            me, silu_rows, modulate_weight, ring_i.pieces, other, planes, dp_items
        )
        gains = from_rows(gains[0])
        ring_i.ahead, ring_i.behind, cond_terms = tie(
            [], ring_i.ahead, ring_i.behind, cond_terms
        )
        *parts, attend_out_grad = split_sum(
            me, ring_i.blocks, *ring_i.last(), head, columns_in // 4, 0, "in_split"
        )
        parts = [parts[0]] + [relate(parts[k], k) for k in (1, 2, 3)]
        attend_in_grad = unsort_columns(
            me, parts, head, lambda s: (s // 2, s % 2), "unsort_in"
        )
    else:
        m1_side = swap_side(two_cores(m1_far))
        m1_core = swap_core(m1_near[own_count:])

        def padded(shape, value, axis, which):
            zero = jnp.zeros(shape, value.dtype)
            return lax.dynamic_update_index_in_dim(zero, value, which, axis)

        down_grad = weight_grad(me, hidden, fed_grad, hidden_units // 2, "down_grad")
        up_grad = weight_grad(me, modded_two, gate_up_grad, width // 3, "up_grad")
        grad = down_grad.reshape(planes, hid, width)
        grad = padded((planes, 4, hid, width), grad, 1, share)
        feed_out_grad = scatter_whole(grad.reshape(4 * hidden_units, width))
        grad = up_grad.reshape(width, 2 * planes, hid)
        grad = padded((width, 2 * planes, 4, hid), grad, 2, share)
        feed_in_grad = scatter_whole(grad.reshape(width, 8 * hidden_units))
        columns = [
            pick(side, value[:, : width // 2], value[:, width // 2 :])
            for value in (attended_grad, side_grad, core_grad, both_grad)
        ]
        near_rows = dot(mixed, jnp.concatenate(columns, axis=0))
        far_rows = dot(mixed_side, jnp.concatenate([columns[k] for k in (1, 0, 3, 2)], axis=0))
        out_grad = jnp.stack(ordered(side, near_rows, far_rows)).astype(BF)
        in_grad = weight_grad(me, modded_one, projected_grad, width // 3, "in_grad")
        grad = out_grad.reshape(2, heads, head, width // 2)
        grad = jnp.swapaxes(grad, 0, 1)
        grad = padded((heads, 2, head, 2, width // 2), grad, 3, side)
        grad = padded((heads, 2, 2, head, 2, width // 2), grad, 2, core)
        attend_out_grad = scatter_whole(grad.reshape(width, width))
        grad = in_grad.reshape(width, 3 * heads, head)
        grad = padded((width, 3 * heads, 4, head), grad, 2, cls)
        attend_in_grad = scatter_whole(grad.reshape(width, 3 * width))

    if not ringed:
        tokens_grad = tokens_back(
            me, tokens, mods, col, resid_grad, m1_near, m1_core, m1_side
        )

    if not ringed:
        sums = sums + swap_side(sums)
        found = lax.dynamic_slice_in_dim(sums, mod * own_items, own_items, 0).astype(BF)
        mod_grad = jnp.concatenate([found, early], axis=1)
        mod_grad = lax.all_to_all(mod_grad, "mod", split_axis=1, concat_axis=0, tiled=True)
        mod_grad = lax.all_gather(mod_grad, "dp", axis=0, tiled=True)
        gains = lax.psum(gains, ("dp", "mod"))
        modulate_grad = dot(silu_rows, mod_grad, 0, 0)
        cond_terms = dot(mod_grad, modulate_weight, 1, 1).astype(BF)
    cond_terms = lax.all_to_all(cond_terms, "dp", split_axis=0, concat_axis=1, tiled=True)
    own_width = width // nmod
    if ringed:
        left, right = cond_terms[:, :own_width], cond_terms[:, own_width:]
        came = swap_side(pick(side, right, left))
        cond_share = pick(side, left, right).astype(F32) + came.astype(F32)
    else:
        cond_share = lax.psum_scatter(
            cond_terms, "mod", scatter_dimension=1, tiled=True
        ).astype(F32)
    cond_cols = lax.dynamic_slice_in_dim(cond_float, mod * own_width, own_width, 1)
    cond_sigma = jax.nn.sigmoid(cond_cols)
    condition_grad = cond_share * cond_sigma * (1.0 + cond_cols * (1.0 - cond_sigma))
    return (
        block_out,
        tokens_grad,
        condition_grad,
        gains[0],
        gains[1],
        attend_in_grad,
        attend_out_grad,
        feed_in_grad,
        feed_out_grad,
        modulate_grad,
    )


def solution(mesh):
    rows = P(("dp", "mod"), None)
    both = P("dp", "mod")
    return jax.shard_map(
        body,
        mesh=mesh,
        in_specs=(
            rows,
            P("dp", None),
            rows,
            P(None, ("dp", "mod")),
            P(),
            P(),
            both,
            both,
            both,
            both,
            both,
            rows,
        ),
        out_specs=(rows, rows, both, P(), P(), both, both, both, both, both),
        check_vma=False,
    )
```

```python
import functools

import jax
import jax.numpy as jnp
from jax import lax
from jax.experimental import pallas as pl
from jax.experimental.pallas import tpu as pltpu
from jax.sharding import PartitionSpec as P

HIGHEST = lax.Precision.HIGHEST
BF = jnp.bfloat16
F32 = jnp.float32
I32 = jnp.int32
MIB = 2**20
STEP_ROWS = 128
ROOM = {
    "attend_forward": 24,
    "attend_backward": 56,
    "feed_forward": 33,
    "feed_backward": 18,
    "feed_grads": 40,
    "attend_grads": 32,
    "mod_back": 56,
    "down_grad": 32,
    "up_grad": 32,
    "in_grad": 32,
    "join_in": 20,
    "join_up": 20,
}


def layer_norm(values):
    average = jnp.mean(values, axis=-1, keepdims=True)
    centred = values - average
    spread = jnp.mean(centred * centred, axis=-1, keepdims=True)
    inverse = lax.rsqrt(spread + 1e-06)
    return (centred * inverse, inverse)


def norm_back(upstream, normed, inverse):
    first = jnp.mean(upstream, axis=-1, keepdims=True)
    second = jnp.mean(upstream * normed, axis=-1, keepdims=True)
    return inverse * (upstream - first - normed * second)


def dot(left, right, left_dim=1, right_dim=0):
    return lax.dot_general(
        left, right, (((left_dim,), (right_dim,)), ((), ())), preferred_element_type=F32
    )


def fence(*values):
    return lax.optimization_barrier(values)


def kernel_call(kernel, grid, in_specs, out_specs, out_shape, name, scratch=(), alias=None):
    return pl.pallas_call(
        kernel,
        grid_spec=pltpu.PrefetchScalarGridSpec(
            num_scalar_prefetch=1,
            grid=grid,
            in_specs=in_specs,
            out_specs=out_specs,
            scratch_shapes=list(scratch),
        ),
        out_shape=out_shape,
        input_output_aliases=alias or {},
        compiler_params=pltpu.CompilerParams(vmem_limit_bytes=ROOM.get(name, 16) * MIB),
        cost_estimate=pl.CostEstimate(flops=1024, bytes_accessed=1024, transcendentals=0),
        name=name,
    )


def whole_spec(shape):
    return pl.BlockSpec(shape, lambda *_: (0,) * len(shape))


def fixed_spec(shape):
    return pl.BlockSpec(shape, lambda *_: (0,) * len(shape), pipeline_mode=pl.Buffered(1))


def lead_spec(shape):
    return pl.BlockSpec((1,) + shape[1:], lambda i, *_: (i,) + (0,) * (len(shape) - 1))


def shaped(shape, dtype):
    return jax.ShapeDtypeStruct(shape, dtype)


def plane_of(ring, planes):
    ring = lax.rem(ring + 2 * planes, planes)
    return jnp.where(ring < planes // 2, 2 * ring, 2 * (planes - 1 - ring) + 1)


SIDE, CORE, PLACE, CLS, FIRST = 0, 1, 2, 3, 4


def sort_kernel(width, share_of, me_ref, weight_ref, *outs):
    rows, columns = weight_ref.shape
    groups = columns // (4 * width)
    for share in range(4):
        side, core = share_of(share)
        pieces = [
            weight_ref[:, (4 * g + share) * width : (4 * g + share + 1) * width]
            for g in range(groups)
        ]
        value = jnp.concatenate(pieces, axis=1)
        relation = 2 * (me_ref[CORE] ^ core) + (me_ref[SIDE] ^ side)
        for k in range(4):

            @pl.when(relation == k)
            def _(k=k, value=value):
                outs[k][...] = value


def sort_columns(me, weight, width, share_of, name):
    rows, columns = weight.shape
    return kernel_call(
        functools.partial(sort_kernel, width, share_of),
        (1,),
        [whole_spec(weight.shape)],
        [whole_spec((rows, columns // 4))] * 4,
        [shaped((rows, columns // 4), weight.dtype)] * 4,
        name,
    )(me, weight)


def quad(me_ref, refs):
    own, side, core, both = (ref[...].astype(F32) for ref in refs)
    here = me_ref[SIDE] == 0
    near = jnp.concatenate([jnp.where(here, own, side), jnp.where(here, side, own)], axis=1)
    far = jnp.concatenate([jnp.where(here, core, both), jnp.where(here, both, core)], axis=1)
    here = me_ref[CORE] == 0
    return jnp.concatenate([jnp.where(here, near, far), jnp.where(here, far, near)], axis=0)


def unit_kernel(me_ref, a_ref, b_ref, c_ref, d_ref, *rest):
    out_ref = rest[-1]
    value = quad(me_ref, (a_ref, b_ref, c_ref, d_ref)).astype(BF)
    rows, columns = value.shape
    out_ref[:rows, :columns] = value
    if len(rest) == 1:
        return
    extra = rest[0][...].astype(F32)
    half = extra.shape[1] // 2
    extra = jnp.concatenate([extra[:, :half], extra[:, half:]], axis=0).astype(BF)
    out_ref[:rows, columns:] = extra
    keep, came = rest[1][...].astype(F32), rest[2][...].astype(F32)
    here = me_ref[SIDE] == 0
    value = jnp.concatenate([jnp.where(here, keep, came), jnp.where(here, came, keep)], axis=1)
    out_ref[rows:, :] = value.astype(BF)


def make_unit(me, parts, extras, name):
    rows, columns = parts[0].shape
    high, wide = 2 * rows, 2 * columns
    if extras:
        high, wide = high + extras[1].shape[0], wide + extras[0].shape[1] // 2
    operands = list(parts) + list(extras)
    return kernel_call(
        unit_kernel,
        (1,),
        [whole_spec(v.shape) for v in operands],
        whole_spec((high, wide)),
        shaped((high, wide), BF),
        name,
    )(me, *operands)


def gather_steps(planes):
    return [0] + [s * d for d in range(1, planes // 2) for s in (-1, 1)] + [planes // 2]


def assemble_kernel(planes, rows, split, me_ref, *refs):
    pieces = len(gather_steps(planes)) + 1
    outs = refs[pieces:]
    high = refs[0].shape[0]
    for at, step in enumerate(gather_steps(planes)):
        plane = plane_of(me_ref[PLACE] + step, planes)
        if at == pieces - 2:
            value = jnp.concatenate(
                [refs[at][...].astype(F32), refs[at + 1][...].astype(F32)], axis=0
            ).astype(BF)
        else:
            value = refs[at][...]
        outs[0][pl.ds(pl.multiple_of(plane * rows, 16), rows), :] = value[:rows, :split]
        if len(outs) > 1:
            slot = lax.rem(plane, 2) * (planes // 2) + plane // 2
            extra = value[:rows, split:].astype(F32)
            extra = jnp.concatenate([extra[: rows // 2], extra[rows // 2 :]], axis=1)
            outs[1][slot] = extra.astype(BF)
            rest = high - rows
            outs[2][pl.ds(pl.multiple_of(plane * rest, 16), rest), :] = value[rows:]


def assemble(me, pieces, planes, rows, split, name):
    high, columns = pieces[0].shape
    outs = [shaped((planes * rows, split), BF)]
    if split < columns:
        outs.append(shaped((planes, rows // 2, 2 * (columns - split)), BF))
        outs.append(shaped((planes * (high - rows), columns), BF))
    return kernel_call(
        functools.partial(assemble_kernel, planes, rows, split),
        (1,),
        [whole_spec(v.shape) for v in pieces],
        [whole_spec(v.shape) for v in outs],
        outs,
        name,
    )(me, *pieces)


def mod_part_kernel(me_ref, rows_ref, weight_ref, keep_ref, send_ref):
    columns = keep_ref.shape[2]
    product = dot(rows_ref[...], weight_ref[...]).reshape(keep_ref.shape[:2] + (2 * columns,))
    here = me_ref[CORE] == 0
    left, right = product[:, :, :columns], product[:, :, columns:]
    keep_ref[...] = jnp.where(here, left, right)
    send_ref[...] = jnp.where(here, right, left).astype(BF)


def mod_part(me, rows, weight, planes):
    shape = (planes, rows.shape[0] // planes, weight.shape[1] // 2)
    return kernel_call(
        mod_part_kernel,
        (1,),
        [whole_spec(rows.shape), whole_spec(weight.shape)],
        [whole_spec(shape)] * 2,
        [shaped(shape, F32), shaped(shape, BF)],
        "mod_part",
    )(me, rows, weight)


def split_kernel(rows, columns, me_ref, own_ref, ahead_ref, behind_ref, *outs):
    height = own_ref.shape[1]
    total = own_ref[0].astype(F32) + ahead_ref[:height].astype(F32)
    total = total + behind_ref[:height].astype(F32)
    for side in range(2):
        for core in range(2):
            value = total[core * rows : (core + 1) * rows, side * columns : (side + 1) * columns]
            relation = 2 * (me_ref[CORE] ^ core) + (me_ref[SIDE] ^ side)
            for k in range(4):

                @pl.when(relation == k)
                def _(k=k, value=value):
                    outs[k][...] = value.astype(BF)

    if len(outs) == 5:
        extra = total[: 2 * rows, 2 * columns :]
        outs[4][...] = jnp.concatenate([extra[:rows], extra[rows:]], axis=1)
    if len(outs) == 6:
        low, width = outs[4].shape
        width *= 2
        value = total[2 * rows :]
        high = value.shape[0]
        tail = value[:, width:]
        step = low - high
        tail = [tail[at : at + step] for at in range(0, high, step)]
        value = jnp.concatenate([value[:, :width], jnp.concatenate(tail, axis=1)], axis=0)
        here = me_ref[SIDE] == 0
        left, right = value[:, : width // 2], value[:, width // 2 :]
        outs[4][...] = jnp.where(here, left, right).astype(BF)
        outs[5][...] = jnp.where(here, right, left).astype(BF)


def split_sum(me, blocks, ahead, behind, rows, columns, low, name):
    planes, height, wide = blocks.shape
    outs = [shaped((rows, columns), BF)] * 4
    if low:
        outs += [shaped((low, (height - 2 * rows) * wide // low // 2), BF)] * 2
    else:
        outs.append(shaped((rows, 2 * (wide - 2 * columns)), F32))
    return kernel_call(
        functools.partial(split_kernel, rows, columns),
        (1,),
        [
            pl.BlockSpec((1, height, wide), lambda i, me: (plane_of(me[PLACE], planes), 0, 0)),
            whole_spec(ahead.shape),
            whole_spec(behind.shape),
        ],
        [whole_spec(v.shape) for v in outs],
        outs,
        name,
    )(me, blocks, ahead, behind)


def unsort_kernel(width, share_of, me_ref, *refs):
    out_ref = refs[-1]
    groups = refs[0].shape[1] // width
    found = [ref[...].astype(F32) for ref in refs[:4]]
    shares = []
    for share in range(4):
        side, core = share_of(share)
        near, far = me_ref[SIDE] == side, me_ref[CORE] == core
        shares.append(
            jnp.where(
                far,
                jnp.where(near, found[0], found[1]),
                jnp.where(near, found[2], found[3]),
            )
        )
    out_ref[...] = jnp.concatenate(
        [shares[s][:, g * width : (g + 1) * width] for g in range(groups) for s in range(4)],
        axis=1,
    )


def unsort_columns(me, parts, width, share_of, name):
    rows, columns = parts[0].shape
    return kernel_call(
        functools.partial(unsort_kernel, width, share_of),
        (1,),
        [whole_spec(v.shape) for v in parts],
        whole_spec((rows, 4 * columns)),
        shaped((rows, 4 * columns), F32),
        name,
    )(me, *parts)


def attend_grads_kernel(
    planes, me_ref, modded_ref, grad_ref, mixed_ref, mixed_side_ref, a_ref, b_ref, c_ref, d_ref,
    out_ref,
):
    rows = out_ref.shape[1]
    columns = grad_ref.shape[1]
    count, width = a_ref.shape
    whole = dot(modded_ref[...], grad_ref[...], 0, 0).astype(BF)
    for plane in range(planes):
        out_ref[plane, :, :columns] = whole[plane * rows : (plane + 1) * rows]
    here = me_ref[SIDE] == 0
    blocks = [
        jnp.where(here, ref[:, : width // 2].astype(F32), ref[:, width // 2 :].astype(F32))
        for ref in (a_ref, b_ref, c_ref, d_ref)
    ]
    head = rows // 2
    half = width // 4
    for flip, ref in enumerate((mixed_ref, mixed_side_ref)):
        order = jnp.concatenate([blocks[k ^ flip] for k in range(4)], axis=0).astype(BF)
        found = dot(ref[...], order)
        for j in range(found.shape[0] // head):
            value = found[j * head : (j + 1) * head]
            value = jnp.concatenate([value[:, :half], value[:, half:]], axis=0).astype(BF)
            out_ref[2 * j + (me_ref[SIDE] ^ flip), :, columns:] = value


def attend_grads(me, modded, grad, mixed, mixed_side, attended_grads, planes):
    width = modded.shape[1]
    rows = width // planes
    out = shaped((planes, rows, grad.shape[1] + width // 4), BF)
    operands = [modded, grad, mixed, mixed_side, *attended_grads]
    return kernel_call(
        functools.partial(attend_grads_kernel, planes),
        (1,),
        [whole_spec(v.shape) for v in operands],
        whole_spec(out.shape),
        out,
        "attend_grads",
    )(me, *operands)


def ring_first_kernel(cut, me_ref, mine_ref, *refs):
    ahead_out, behind_out = refs[-2:]
    rows = mine_ref.shape[1]
    ahead_out[:cut] = mine_ref[0, :cut]
    behind_out[: rows - cut] = mine_ref[0, cut:]
    if len(refs) > 2:
        ahead_out[cut:] = refs[0][...]
        behind_out[rows - cut :] = refs[0][...]


def ring_first(me, blocks, along, cut, name):
    planes, rows, columns = blocks.shape
    more = 0 if along is None else along.shape[0]
    operands = [blocks] if along is None else [blocks, along]
    outs = [shaped((cut + more, columns), BF), shaped((rows - cut + more, columns), BF)]
    return kernel_call(
        functools.partial(ring_first_kernel, cut),
        (1,),
        [
            pl.BlockSpec(
                (1, rows, columns),
                lambda i, me: (plane_of(me[PLACE] + planes // 2, planes), 0, 0),
            ),
            *[whole_spec(v.shape) for v in operands[1:]],
        ],
        [whole_spec(v.shape) for v in outs],
        outs,
        name,
    )(me, *operands)


def ring_add_kernel(cut, me_ref, ahead_mine, behind_mine, ahead, behind, ahead_out, behind_out):
    rows = ahead_mine.shape[1]
    came = cut or rows
    ahead_out[:came] = (ahead_mine[0, :came].astype(F32) + ahead[:came].astype(F32)).astype(BF)
    if cut:
        ahead_out[cut:rows] = ahead_mine[0, cut:]
    kept = ahead_out.shape[0] - rows
    if kept:
        ahead_out[rows:] = ahead[came : came + kept]
    start = cut
    came = rows - cut
    behind_out[start:rows] = (
        behind_mine[0, start:].astype(F32) + behind[:came].astype(F32)
    ).astype(BF)
    if cut:
        behind_out[:cut] = behind_mine[0, :cut]
    if kept:
        behind_out[rows:] = behind[behind.shape[0] - kept :]


def ring_add(me, blocks, ahead, behind, step, cut, kept, name):
    planes, rows, columns = blocks.shape

    def at(sign):
        return lambda i, me: (plane_of(me[PLACE] + sign * step, planes), 0, 0)

    block = (1, rows, columns)
    out = shaped((rows + kept, columns), BF)
    return kernel_call(
        functools.partial(ring_add_kernel, cut),
        (1,),
        [
            pl.BlockSpec(block, at(1)),
            pl.BlockSpec(block, at(-1)),
            whole_spec(ahead.shape),
            whole_spec(behind.shape),
        ],
        [whole_spec(out.shape)] * 2,
        [out] * 2,
        name,
    )(me, blocks, blocks, ahead, behind)


def weight_grad_kernel(me_ref, left_ref, right_ref, out_ref):
    out_ref[...] = dot(left_ref[...], right_ref[...], 0, 0).astype(BF)


def weight_grad(me, left, right, tile, name):
    count, rows = left.shape
    columns = right.shape[1]
    return kernel_call(
        weight_grad_kernel,
        (rows // tile,),
        [pl.BlockSpec((count, tile), lambda i, *_: (0, i)), whole_spec(right.shape)],
        pl.BlockSpec((tile, columns), lambda i, *_: (i, 0)),
        shaped((rows, columns), BF),
        name,
    )(me, left, right)


def feed_grads_kernel(planes, me_ref, modded_ref, grad_ref, hidden_ref, fed_grad_ref, out_ref):
    wide = out_ref.shape[2]
    width = modded_ref.shape[1]
    rows, low = width // planes, hidden_ref.shape[1] // planes
    high = low * width // wide
    rest = wide - width
    down = dot(hidden_ref[...], fed_grad_ref[...], 0, 0)
    for plane in range(planes):
        value = down[plane * low : (plane + 1) * low]
        tail = [value[high:, at : at + rest] for at in range(0, width, rest)]
        value = jnp.concatenate([value[:high], jnp.concatenate(tail, axis=0)], axis=1)
        out_ref[plane, rows:, :] = value.astype(BF)
    up = dot(modded_ref[...], grad_ref[...], 0, 0)
    for plane in range(planes):
        out_ref[plane, :rows, :] = up[plane * rows : (plane + 1) * rows].astype(BF)


def feed_grads(me, modded, grad, hidden, fed_grad, planes):
    width, wide = modded.shape[1], grad.shape[1]
    rows = width // planes + hidden.shape[1] // planes * width // wide
    out = shaped((planes, rows, wide), BF)
    operands = [modded, grad, hidden, fed_grad]
    return kernel_call(
        functools.partial(feed_grads_kernel, planes),
        (1,),
        [whole_spec(v.shape) for v in operands],
        whole_spec(out.shape),
        out,
        "feed_grads",
    )(me, *operands)


def turned(values, first):
    quarter = values.shape[0] // 4
    ahead = pltpu.roll(values, values.shape[0] - quarter, 0)
    behind = pltpu.roll(values, quarter, 0)
    return jnp.where(first, ahead, behind)


def rms(values):
    return lax.rsqrt(jnp.mean(values * values, axis=0, keepdims=True) + 1e-06)


def scores_t(key_rot, query_rot, same, scale):
    raw = dot(key_rot, query_rot, 0, 0) * scale
    return jnp.where(same, raw, -1e30)


def softmax_t(scores):
    peak = jnp.max(scores, axis=0, keepdims=True)
    exponent = jnp.exp(scores - peak)
    return exponent / jnp.sum(exponent, axis=0, keepdims=True)


def first_mask(head, count):
    row = lax.broadcasted_iota(I32, (head, count), 0)
    return lax.rem(row, head // 2) < head // 4


def by_rows(count, work, step=STEP_ROWS):
    step = min(step, count)
    for at in range(0, count, step):
        work(slice(at, at + step))


def put_chosen(out_ref, refs, at, per):
    for k, ref in enumerate(refs):

        @pl.when(at // per == k)
        def _(ref=ref):
            out_ref[...] = ref[...]


def chosen(refs, at, per):
    value = refs[0][...]
    for k, ref in enumerate(refs[1:], 1):
        value = jnp.where(at >= k * per, ref[...], value)
    return value


def quarter_specs(shape, per, parts):
    return [
        pl.BlockSpec(shape, lambda i, *_, k=k: (jnp.clip(i - k * per, 0, per - 1), 0))
        for k in range(parts)
    ]


def join_mods_kernel(me_ref, a_ref, b_ref, c_ref, d_ref, out_ref):
    own, side, core, both = (ref[...].astype(F32) for ref in (a_ref, b_ref, c_ref, d_ref))
    here = me_ref[CORE] == 0
    near = [jnp.where(here, own, core), jnp.where(here, core, own)]
    far = [jnp.where(here, side, both), jnp.where(here, both, side)]
    here = me_ref[SIDE] == 0
    parts = [jnp.where(here, n, f) for n, f in zip(near, far)]
    parts += [jnp.where(here, f, n) for n, f in zip(near, far)]
    out_ref[...] = jnp.concatenate(parts, axis=1).astype(BF)


def join_mods(me, parts):
    items, columns = parts[0].shape
    return kernel_call(
        join_mods_kernel,
        (1,),
        [whole_spec(v.shape) for v in parts],
        whole_spec((items, 4 * columns)),
        shaped((items, 4 * columns), BF),
        "join_mods",
    )(me, *parts)


def join_out_kernel(me_ref, a_ref, b_ref, c_ref, d_ref, out_ref):
    here = me_ref[SIDE] == 0
    for other, (near, far) in enumerate(((a_ref, b_ref), (c_ref, d_ref))):
        for side in range(2):
            own, off = near[side].astype(F32), far[side].astype(F32)
            value = jnp.concatenate([jnp.where(here, own, off), jnp.where(here, off, own)], axis=1)
            out_ref[2 * side + (me_ref[CORE] ^ other)] = value.astype(BF)


def join_out(me, parts):
    _, rows, columns = parts[0].shape
    return kernel_call(
        join_out_kernel,
        (1,),
        [whole_spec(v.shape) for v in parts],
        whole_spec((4, rows, 2 * columns)),
        shaped((4, rows, 2 * columns), BF),
        "join_out",
    )(me, *parts)


def tables_kernel(dp_items, own_items, me_ref, freq_ref, *refs):
    cos_ref, sin_ref, row_ref, col_ref = refs[4:]
    head, count = freq_ref.shape
    seqs = cos_ref.shape[0] // 4
    items = own_items // seqs
    entry = lax.broadcasted_iota(I32, (head, count), 0)
    low = lax.rem(entry, head // 2) < head // 4
    for k in range(4):
        base = (me_ref[CORE] ^ (k >> 1)) * dp_items
        base += me_ref[FIRST] - me_ref[CORE] * dp_items
        base += jnp.where(me_ref[SIDE] == 0, k & 1, -(k & 1)) * own_items
        for q in range(seqs):
            at = k * seqs + q
            spots = refs[k][:2, q * count : (q + 1) * count]
            spot = jnp.where(entry < head // 2, spots[0:1], spots[1:2]).astype(F32)
            angle = spot * freq_ref[...]
            sine = jnp.sin(angle)
            cos_ref[at] = jnp.cos(angle)
            sin_ref[at] = jnp.where(low, -sine, sine)
            for ref, shape, axis in ((row_ref, (1, count), 1), (col_ref, (count, 1), 0)):
                token = lax.broadcasted_iota(I32, shape, axis)
                end = jnp.zeros((1, 1), I32)
                item = jnp.zeros(shape, I32) + (base + q * items)
                for j in range(items):
                    end = end + refs[k][2 + q : 3 + q, j : j + 1]
                    item = item + (token >= end).astype(I32)
                ref[at] = item


def make_tables(me, freq, small, seqs, dp_items, own_items):
    head, count = freq.shape
    outs = [
        shaped((seqs, head, count), F32),
        shaped((seqs, head, count), F32),
        shaped((seqs, 1, count), I32),
        shaped((seqs, count, 1), I32),
    ]
    return kernel_call(
        functools.partial(tables_kernel, dp_items, own_items),
        (1,),
        [whole_spec(v.shape) for v in (freq, *small)],
        [whole_spec(v.shape) for v in outs],
        outs,
        "tables",
    )(me, freq, *small)


def members_of(column, items):
    lane = lax.broadcasted_iota(I32, (column.shape[0], items), 1)
    return (column == lane).astype(BF)


def attend_forward_kernel(
    heads, head, me_ref, t0_ref, t1_ref, t2_ref, t3_ref, mods_ref, weight_ref, cos_ref, sin_ref,
    qg_ref, kg_ref, row_ref, col_ref, modded_ref, raw_ref, low_ref, mixed_ref, held_ref,
    tokens_ref, token_mod_ref,
):
    count, width = t0_ref.shape
    per = pl.num_programs(0) // 4
    put_chosen(tokens_ref, (t0_ref, t1_ref, t2_ref, t3_ref), pl.program_id(0), per)
    own = heads * head
    members = members_of(col_ref[0], mods_ref.shape[0])
    token_mod_ref[...] = dot(members, mods_ref[:, : 2 * width])

    def modulated(at):
        normed, _ = layer_norm(tokens_ref[at, :].astype(F32))
        modded = normed * (1.0 + token_mod_ref[at, width:]) + token_mod_ref[at, :width]
        modded_ref[at, :] = modded.astype(BF)

    by_rows(count, modulated)
    projected = dot(modded_ref[...], weight_ref[...]).T
    raw_ref[0] = projected[: 2 * own]
    values = projected[2 * own :]
    low_ref[0] = values.astype(BF)
    same = col_ref[0] == row_ref[0]
    first = first_mask(head, count)
    cosine, sine = cos_ref[0], sin_ref[0]
    scale = head ** (-0.5)

    def rotated(raw, gain):
        normed = raw * rms(raw) * gain
        return (normed * cosine + turned(normed, first) * sine).astype(BF)

    for h in range(heads):
        query_rot = rotated(projected[h * head : (h + 1) * head], qg_ref[...])
        key_rot = rotated(projected[own + h * head : own + (h + 1) * head], kg_ref[...])
        prob = softmax_t(scores_t(key_rot, query_rot, same, scale)).astype(BF)
        mixed = dot(values[h * head : (h + 1) * head].astype(BF), prob)
        held_ref[h * head : (h + 1) * head, :] = mixed
    mixed_ref[...] = held_ref[...].astype(BF)


def attend_forward(me, tokens, mods, weight, cosine, sine, qg, kg, row, col, heads):
    seqs, head, count = cosine.shape
    width = tokens[0].shape[1]
    own = heads * head
    return kernel_call(
        functools.partial(attend_forward_kernel, heads, head),
        (seqs,),
        [
            *quarter_specs((count, width), seqs // 4, 4),
            whole_spec(mods.shape),
            whole_spec(weight.shape),
            lead_spec(cosine.shape),
            lead_spec(sine.shape),
            whole_spec(qg.shape),
            whole_spec(kg.shape),
            lead_spec(row.shape),
            lead_spec(col.shape),
        ],
        [
            pl.BlockSpec((count, width), lambda i, *_: (i, 0)),
            lead_spec((seqs, 2 * own, count)),
            lead_spec((seqs, own, count)),
            pl.BlockSpec((own, count), lambda i, *_: (0, i)),
        ],
        [
            shaped((seqs * count, width), BF),
            shaped((seqs, 2 * own, count), F32),
            shaped((seqs, own, count), BF),
            shaped((own, seqs * count), BF),
        ],
        "attend_forward",
        [
            pltpu.VMEM((own, count), F32),
            pltpu.VMEM((count, width), BF),
            pltpu.VMEM((count, 2 * width), F32),
        ],
    )(me, *tokens, mods, weight, cosine, sine, qg, kg, row, col)


def attend_backward_kernel(
    heads, head, me_ref, near_ref, far_ref, out_w_ref, in_w_ref, raw_ref, low_ref, cos_ref,
    sin_ref, qg_ref, kg_ref, row_ref, col_ref, near_tokens_ref, far_tokens_ref, *rest,
):
    out_ref, m1_ref, qgg_ref, kgg_ref, sums_ref, held_ref, tokens_ref, m1_held, scaled_ref = rest[
        -9:
    ]
    own = heads * head
    half = pl.num_programs(0) // 2
    grad = chosen((near_ref, far_ref), pl.program_id(0), half)
    put_chosen(tokens_ref, (near_tokens_ref, far_tokens_ref), pl.program_id(0), half)
    count = grad.shape[0]
    mixed_grad = dot(out_w_ref[0], grad, 1, 1)
    same = col_ref[0] == row_ref[0]
    first = first_mask(head, count)
    cosine, sine = cos_ref[0], sin_ref[0]
    scale = head ** (-0.5)

    @pl.when(pl.program_id(0) == 0)
    def _():
        qgg_ref[...] = jnp.zeros_like(qgg_ref)
        kgg_ref[...] = jnp.zeros_like(kgg_ref)
        sums_ref[...] = jnp.zeros_like(sums_ref)

    def rotated(raw, gain):
        inverse = rms(raw)
        normed = raw * inverse * gain
        return inverse, (normed * cosine + turned(normed, first) * sine).astype(BF)

    def back(rot_grad, raw, inverse, gain):
        norm_grad = rot_grad * cosine + turned(rot_grad * sine, first)
        gain_grad = norm_grad * raw * inverse
        scaled = norm_grad * gain
        inner = jnp.mean(scaled * raw, axis=0, keepdims=True)
        return inverse * scaled - raw * (inverse * inverse * inverse * inner), gain_grad

    query_total = jnp.zeros((head, count), F32)
    key_total = jnp.zeros((head, count), F32)
    low = low_ref[0].astype(F32)
    for h in range(heads):
        rows = slice(h * head, (h + 1) * head)
        query_raw = raw_ref[0, h * head : (h + 1) * head]
        key_raw = raw_ref[0, own + h * head : own + (h + 1) * head]
        values = low[rows].astype(BF)
        upstream = mixed_grad[rows].astype(BF)
        query_inverse, query_rot = rotated(query_raw, qg_ref[...])
        key_inverse, key_rot = rotated(key_raw, kg_ref[...])
        prob = softmax_t(scores_t(key_rot, query_rot, same, scale))
        prob_grad = dot(values, upstream, 0, 0)
        inner = jnp.sum(prob * prob_grad, axis=0, keepdims=True)
        score_grad = (prob * (prob_grad - inner)).astype(BF)
        query_rot_grad = dot(key_rot, score_grad) * scale
        key_rot_grad = dot(query_rot, score_grad, 1, 1) * scale
        values_grad = dot(upstream, prob.astype(BF), 1, 1)
        query_grad, query_part = back(query_rot_grad, query_raw, query_inverse, qg_ref[...])
        key_grad, key_part = back(key_rot_grad, key_raw, key_inverse, kg_ref[...])
        query_total += query_part
        key_total += key_part
        held_ref[h * head : (h + 1) * head, :] = query_grad
        held_ref[own + h * head : own + (h + 1) * head, :] = key_grad
        held_ref[2 * own + h * head : 2 * own + (h + 1) * head, :] = values_grad
    qgg_ref[...] += query_total
    kgg_ref[...] += key_total
    projected_grad = held_ref[...].T.astype(BF)
    out_ref[...] = projected_grad
    m1_held[...] = dot(projected_grad, in_w_ref[...], 1, 1)

    def scaled(at):
        m1 = m1_held[at, :]
        normed, _ = layer_norm(tokens_ref[at, :].astype(F32))
        m1_ref[at, :] = m1.astype(BF)
        scaled_ref[at, :] = (m1 * normed).astype(BF)

    by_rows(count, scaled)
    members = members_of(col_ref[0], sums_ref.shape[0])
    width = m1_ref.shape[1]
    sums_ref[:, :width] += dot(members, m1_ref[...], 0, 0)
    sums_ref[:, width:] += dot(members, scaled_ref[...], 0, 0)


def attend_backward(
    me, near, far, w_out, w_in, raw, low, cosine, sine, qg, kg, row, col, tokens, items, heads,
    at, held,
):
    seqs, head, count = cosine.shape
    width = near.shape[1]
    own = heads * head
    per = seqs // 4

    def seq(i):
        return at * per + i + jnp.where(i < per, 0, per)

    def block(shape):
        return pl.BlockSpec((1,) + shape[1:], lambda i, *_: (seq(i), 0, 0))

    in_specs = [
        *quarter_specs((count, width), per, 2),
        pl.BlockSpec((1,) + w_out.shape[1:], lambda i, me: (me[CLS], 0, 0)),
        whole_spec(w_in.shape),
        block(raw.shape),
        block(low.shape),
        block(cosine.shape),
        block(sine.shape),
        whole_spec(qg.shape),
        whole_spec(kg.shape),
        block(row.shape),
        block(col.shape),
        *quarter_specs((count, width), per, 2),
    ]
    operands = [near, far, w_out, w_in, raw, low, cosine, sine, qg, kg, row, col]
    operands += [tokens[at], tokens[at + 2]]
    alias = {}
    if held is not None:
        alias = {1 + len(operands): 0}
        operands.append(held)
        in_specs.append(pl.BlockSpec(memory_space=pl.ANY))
    return kernel_call(
        functools.partial(attend_backward_kernel, heads, head),
        (2 * per,),
        in_specs,
        [
            pl.BlockSpec((count, 3 * own), lambda i, *_: (seq(i), 0)),
            pl.BlockSpec((count, width), lambda i, *_: (i, 0)),
            whole_spec((head, count)),
            whole_spec((head, count)),
            whole_spec((items, 2 * width)),
        ],
        [
            shaped((seqs * count, 3 * own), BF),
            shaped((2 * per * count, width), BF),
            shaped((head, count), F32),
            shaped((head, count), F32),
            shaped((items, 2 * width), F32),
        ],
        "attend_backward",
        [
            pltpu.VMEM((3 * own, count), F32),
            pltpu.VMEM((count, width), BF),
            pltpu.VMEM((count, width), F32),
            pltpu.VMEM((count, width), BF),
        ],
        alias,
    )(me, *operands)


def feed_forward_kernel(me_ref, *refs):
    mods_ref, col_ref, m0_ref, m1_ref, m2_ref, m3_ref, w_out_ref, w_up_ref = refs[8:16]
    modded_ref, gate_up_ref, hidden_ref, fed_grad_ref, attended_ref = refs[16:21]
    mixed_ref, tokens_ref, upstream_ref, held_ref, token_mod_ref, gate_up_held = refs[21:]
    put_chosen(tokens_ref, refs[:4], pl.program_id(0), 1)
    put_chosen(upstream_ref, refs[4:8], pl.program_id(0), 1)
    count, width = tokens_ref.shape
    own = m0_ref.shape[0]
    for k, ref in enumerate((m0_ref, m1_ref, m2_ref, m3_ref)):
        cls = 2 * (me_ref[SIDE] ^ (k & 1)) + (me_ref[CORE] ^ (k >> 1))
        mixed_ref[pl.ds(pl.multiple_of(cls * own, 16), own), :] = ref[...]
    held_ref[...] = dot(mixed_ref[...], w_out_ref[...], 0, 0)

    @pl.when(pl.program_id(0) == 0)
    def _():
        attended_ref[...] = held_ref[...]

    members = members_of(col_ref[...].reshape(-1, 1), mods_ref.shape[0])
    token_mod_ref[...] = dot(members, mods_ref[:, 2 * width :])

    def modulated(at):
        resid = tokens_ref[at, :].astype(F32) + token_mod_ref[at, :width] * held_ref[at, :]
        normed, _ = layer_norm(resid)
        scale = token_mod_ref[at, 2 * width : 3 * width]
        modded = normed * (1.0 + scale) + token_mod_ref[at, width : 2 * width]
        modded_ref[at, :] = modded.astype(BF)
        grad = token_mod_ref[at, 3 * width :] * upstream_ref[at, :].astype(F32)
        fed_grad_ref[at, :] = grad.astype(BF)

    by_rows(count, modulated)
    gate_up_held[...] = dot(modded_ref[...], w_up_ref[...])
    units = hidden_ref.shape[1]

    def activated(at):
        gate, up = gate_up_held[at, :units], gate_up_held[at, units:]
        sigma = jax.nn.sigmoid(gate)
        silu = gate * sigma
        hidden_ref[at, :] = (silu * up).astype(BF)
        gate_up_ref[at, :units] = (up * (sigma * (1.0 + gate * (1.0 - sigma)))).astype(BF)
        gate_up_ref[at, units:] = silu.astype(BF)

    by_rows(count, activated)


def feed_forward(me, tokens, upstream, mods, col, mixed, w_out, w_up):
    count, width = tokens[0].shape
    total = 4 * count
    own = mixed[0].shape[0]
    per = col.shape[0] // 4
    columns = w_up.shape[1]

    def rows(n):
        return pl.BlockSpec((count, n), lambda j, *_: (j, 0))

    def mixed_spec(k):
        return pl.BlockSpec((own, count), lambda j, *_: (0, j ^ k))

    return kernel_call(
        feed_forward_kernel,
        (4,),
        [
            *[fixed_spec((count, width))] * 8,
            fixed_spec(mods.shape),
            pl.BlockSpec((per,) + col.shape[1:], lambda j, *_: (j, 0, 0)),
            *(mixed_spec(k) for k in range(4)),
            fixed_spec(w_out.shape),
            fixed_spec(w_up.shape),
        ],
        [
            rows(width),
            rows(columns),
            rows(columns // 2),
            rows(width),
            whole_spec((count, width)),
        ],
        [
            shaped((total, width), BF),
            shaped((total, columns), BF),
            shaped((total, columns // 2), BF),
            shaped((total, width), BF),
            shaped((count, width), F32),
        ],
        "feed_forward",
        [
            pltpu.VMEM((4 * own, count), BF),
            pltpu.VMEM((count, width), BF),
            pltpu.VMEM((count, width), BF),
            pltpu.VMEM((count, width), F32),
            pltpu.VMEM((count, 4 * width), F32),
            pltpu.VMEM((count, columns), F32),
        ],
    )(me, *tokens, *upstream, mods, col, *mixed, w_out, w_up)


def feed_backward_kernel(
    me_ref, gate_up_ref, hidden_ref, fed_grad_ref, w_up_ref, w_down_ref, *rest
):
    grad_ref, m2_ref, fed_ref, held_ref = rest[-4:]
    held_ref[...] = dot(fed_grad_ref[...], w_down_ref[...], 1, 1)
    count, units = held_ref.shape

    def back(at):
        hidden_grad = held_ref[at, :]
        slope, silu = gate_up_ref[at, :units], gate_up_ref[at, units:]
        grad_ref[at, :units] = (hidden_grad * slope.astype(F32)).astype(BF)
        grad_ref[at, units:] = (hidden_grad * silu.astype(F32)).astype(BF)

    by_rows(count, back)
    m2_ref[...] = dot(grad_ref[...], w_up_ref[...], 1, 1).astype(BF)
    fed_ref[...] = dot(hidden_ref[...], w_down_ref[...]).astype(BF)


def feed_backward(me, gate_up, hidden, fed_grad, w_up, w_down, at, held):
    total, columns = gate_up.shape
    width = fed_grad.shape[1]
    count = total // 4

    def rows(n):
        return pl.BlockSpec((count, n), lambda j, *_: (2 * j + at, 0))

    out = pl.BlockSpec((count, width), lambda j, *_: (j, 0))
    in_specs = [
        rows(columns),
        rows(columns // 2),
        rows(width),
        fixed_spec(w_up.shape),
        fixed_spec(w_down.shape),
    ]
    operands = [gate_up, hidden, fed_grad, w_up, w_down]
    alias = {}
    if held is not None:
        alias = {1 + len(operands): 0}
        operands.append(held)
        in_specs.append(pl.BlockSpec(memory_space=pl.ANY))
    return kernel_call(
        feed_backward_kernel,
        (2,),
        in_specs,
        [rows(columns), out, out],
        [
            shaped((total, columns), BF),
            shaped((2 * count, width), BF),
            shaped((2 * count, width), BF),
        ],
        "feed_backward",
        [pltpu.VMEM((count, columns // 2), F32)],
        alias,
    )(me, *operands)


def own_sums(me_ref, column, sums_ref, *terms):
    lane = lax.broadcasted_iota(I32, (column.shape[0], sums_ref.shape[0]), 1)
    members = (column - me_ref[FIRST] == lane).astype(BF)
    width = terms[0].shape[1]
    for at, term in enumerate(terms):
        sums_ref[:, at * width : (at + 1) * width] = dot(members, term[...], 0, 0).astype(BF)


def resid_kernel(
    me_ref, tokens_ref, upstream_ref, mods_ref, col_ref, attended_ref, near_ref, core_ref,
    side_ref, grad_ref, out_ref, sums_ref, token_mod_ref, gate_sum_ref, shift_sum_ref,
    scale_sum_ref,
):
    count, width = tokens_ref.shape
    column = col_ref[...].reshape(-1, 1)
    members = members_of(column, mods_ref.shape[0])
    token_mod_ref[:, :width] = dot(members, mods_ref[:, 2 * width : 3 * width])
    token_mod_ref[:, width:] = dot(members, mods_ref[:, 4 * width : 5 * width])

    def back(at):
        attended = attended_ref[at, :]
        resid = tokens_ref[at, :].astype(F32) + token_mod_ref[at, :width] * attended
        normed, inverse = layer_norm(resid)
        m2 = near_ref[at, :].astype(F32) + core_ref[at, :].astype(F32)
        m2 = m2 + side_ref[at, :].astype(F32)
        shift_sum_ref[at, :] = m2.astype(BF)
        scale_sum_ref[at, :] = (m2 * normed).astype(BF)
        grad = norm_back(m2 * (1.0 + token_mod_ref[at, width:]), normed, inverse)
        grad = grad + upstream_ref[at, :].astype(F32)
        grad_ref[at, :] = grad
        out_ref[at, :] = (token_mod_ref[at, :width] * grad).astype(BF)
        gate_sum_ref[at, :] = (grad * attended).astype(BF)

    by_rows(count, back)
    own_sums(me_ref, column, sums_ref, gate_sum_ref, shift_sum_ref, scale_sum_ref)


def resid_back(me, tokens, upstream, mods, col, attended, near, core, side, items):
    count, width = tokens.shape
    block = pl.BlockSpec((count, width), lambda i, *_: (0, 0))
    return kernel_call(
        resid_kernel,
        (1,),
        [
            block,
            block,
            whole_spec(mods.shape),
            pl.BlockSpec((col.shape[0] // 4,) + col.shape[1:], lambda i, *_: (0, 0, 0)),
            block,
            block,
            block,
            block,
        ],
        [block, block, whole_spec((items, 3 * width))],
        [
            shaped((count, width), F32),
            shaped((count, width), BF),
            shaped((items, 3 * width), BF),
        ],
        "resid_back",
        [pltpu.VMEM((count, 2 * width), F32)] + [pltpu.VMEM((count, width), BF)] * 3,
    )(me, tokens, upstream, mods, col, attended, near, core, side)


def output_kernel(
    me_ref, tokens_ref, upstream_ref, mods_ref, col_ref, attended_ref, near_ref, core_ref,
    side_ref, out_ref, sums_ref, token_mod_ref, gate_sum_ref,
):
    count, width = tokens_ref.shape
    column = col_ref[...].reshape(-1, 1)
    members = members_of(column, mods_ref.shape[0])
    token_mod_ref[:, :width] = dot(members, mods_ref[:, 2 * width : 3 * width])
    token_mod_ref[:, width:] = dot(members, mods_ref[:, 5 * width :])

    def add(at):
        fed = near_ref[at, :].astype(F32) + core_ref[at, :].astype(F32)
        fed = fed + side_ref[at, :].astype(F32)
        resid = tokens_ref[at, :].astype(F32) + token_mod_ref[at, :width] * attended_ref[at, :]
        out_ref[at, :] = (resid + token_mod_ref[at, width:] * fed).astype(BF)
        gate_sum_ref[at, :] = (upstream_ref[at, :].astype(F32) * fed).astype(BF)

    by_rows(count, add)
    own_sums(me_ref, column, sums_ref, gate_sum_ref)


def output(me, tokens, upstream, mods, col, attended, near, core, side, items):
    count, width = tokens.shape
    block = pl.BlockSpec((count, width), lambda i, *_: (0, 0))
    return kernel_call(
        output_kernel,
        (1,),
        [
            block,
            block,
            whole_spec(mods.shape),
            pl.BlockSpec((col.shape[0] // 4,) + col.shape[1:], lambda i, *_: (0, 0, 0)),
            block,
            block,
            block,
            block,
        ],
        [block, whole_spec((items, width))],
        [shaped((count, width), BF), shaped((items, width), BF)],
        "output",
        [pltpu.VMEM((count, 2 * width), F32), pltpu.VMEM((count, width), BF)],
    )(me, tokens, upstream, mods, col, attended, near, core, side)


def tokens_kernel(
    me_ref, tokens_ref, mods_ref, col_ref, resid_ref, near_ref, core_ref, side_ref, out_ref,
    scale_ref,
):
    count, width = tokens_ref.shape
    members = members_of(col_ref[...].reshape(-1, 1), mods_ref.shape[0])
    scale_ref[...] = dot(members, mods_ref[:, width : 2 * width])

    def back(at):
        normed, inverse = layer_norm(tokens_ref[at, :].astype(F32))
        m1 = near_ref[at, :].astype(F32) + core_ref[at, :].astype(F32)
        m1 = (m1 + side_ref[at, :].astype(F32)) * (1.0 + scale_ref[at, :])
        out_ref[at, :] = resid_ref[at, :] + norm_back(m1, normed, inverse)

    by_rows(count, back)


def tokens_back(me, tokens, mods, col, resid_grad, near, core, side):
    count, width = tokens.shape
    block = pl.BlockSpec((count, width), lambda i, *_: (0, 0))
    return kernel_call(
        tokens_kernel,
        (1,),
        [
            block,
            whole_spec(mods.shape),
            pl.BlockSpec((col.shape[0] // 4,) + col.shape[1:], lambda i, *_: (0, 0, 0)),
            block,
            block,
            block,
            block,
        ],
        block,
        shaped((count, width), F32),
        "tokens_back",
        [pltpu.VMEM((count, width), F32)],
    )(me, tokens, mods, col, resid_grad, near, core, side)


def mod_back_kernel(planes, items, me_ref, rows_ref, weight_ref, *refs):
    count = len(gather_steps(planes)) + 1
    pieces = refs[: 2 * count]
    grad_ref, terms_ref, gains_ref, held_ref = refs[2 * count :]
    more, width = refs[0].shape
    gains = jnp.zeros((1, width), F32)
    for at, step in enumerate(gather_steps(planes)):
        plane = plane_of(me_ref[PLACE] + step, planes)
        for other in range(2):
            refs = pieces[other * count + at : other * count + at + 2]
            if at == count - 2:
                value = jnp.concatenate(
                    [ref[ref.shape[0] - more // 2 :].astype(F32) for ref in refs], axis=0
                )
            else:
                value = refs[0][refs[0].shape[0] - more :].astype(F32)
            row = (2 * plane + (me_ref[CORE] ^ other)) * items
            row = pl.ds(pl.multiple_of(row, items), items)
            for part in range(weight_ref.shape[1] // width):
                held_ref[row, part * width : (part + 1) * width] = value[
                    part * items : (part + 1) * items
                ].astype(BF)
            at_gain = held_ref.shape[1] // width * items
            gains += value[at_gain : at_gain + 1]
    grad_ref[...] = dot(rows_ref[...], held_ref[...], 0, 0)
    terms_ref[...] = dot(held_ref[...], weight_ref[...], 1, 1).astype(BF)
    gains_ref[...] = gains


def mod_back(me, rows, weight, own, other, planes, items):
    pieces = list(own) + list(other)
    outs = [shaped(weight.shape, F32), shaped(rows.shape, BF), shaped((1, own[0].shape[1]), F32)]
    return kernel_call(
        functools.partial(mod_back_kernel, planes, items),
        (1,),
        [whole_spec(v.shape) for v in (rows, weight, *pieces)],
        [whole_spec(v.shape) for v in outs],
        outs,
        "mod_back",
        [pltpu.VMEM((rows.shape[0], weight.shape[1]), BF)],
    )(me, rows, weight, *pieces)


def body(
    tokens,
    condition,
    lengths,
    positions,
    query_gain,
    key_gain,
    attend_in,
    attend_out,
    feed_in,
    feed_out,
    modulate_weight,
    cotangent,
):
    ndp, nmod = lax.axis_size("dp"), lax.axis_size("mod")
    planes = ndp // 2
    half = planes // 2
    dp, mod = lax.axis_index("dp"), lax.axis_index("mod")
    core, plane, side = dp % 2, dp // 2, mod % 2
    own_seqs, items_seq = lengths.shape
    own_count, width = tokens.shape
    count = own_count // own_seqs
    seqs = 4 * own_seqs
    head = query_gain.shape[0]
    heads = width // head // 4
    cls = 2 * side + core
    own_items = own_seqs * items_seq
    dp_items = condition.shape[0]
    ringed = nmod == 2 and attend_out.shape[0] == head
    hid = feed_out.shape[0] // 2
    place = jnp.where(plane % 2 == 0, plane // 2, planes - 1 - plane // 2)
    first_item = core * dp_items + mod * own_items
    me = jnp.stack([side, core, place, cls, first_item]).astype(I32)

    def relate(value, k):
        pairs = [
            (d * nmod + m, (d ^ (k >> 1)) * nmod + (m ^ (k & 1)))
            for d in range(ndp)
            for m in range(nmod)
        ]
        return lax.ppermute(value, ("dp", "mod"), pairs)

    def swap_core(value):
        return relate(value, 2)

    def swap_side(value):
        return relate(value, 1)

    def pick(which, pair0, pair1):
        return jnp.where(which == 0, pair0, pair1)

    def ordered(which, own, other):
        return pick(which, own, other), pick(which, other, own)

    def static_plane(ring):
        ring %= planes
        return 2 * ring if ring < half else 2 * (planes - 1 - ring) + 1

    def hop(value, step):
        pairs = [
            (2 * static_plane(r) + c, 2 * static_plane(r + step) + c)
            for r in range(planes)
            for c in range(2)
        ]
        return lax.ppermute(value, "dp", pairs)

    class Gather:
        def __init__(self, block, cut=None):
            self.pieces = [block]
            self.cut = block.shape[0] // 32 * 16 if cut is None else cut
            self.ahead = self.behind = block
            self.step = 0

        def go(self):
            self.step += 1
            if self.step == half:
                self.ahead, self.behind = self.ahead[: self.cut], self.behind[self.cut :]
            self.ahead, self.behind = hop(self.ahead, 1), hop(self.behind, -1)
            self.pieces += [self.ahead, self.behind]

    class Scatter:
        def __init__(self, blocks, name, along=None):
            self.blocks, self.name = blocks, name
            self.rows = blocks.shape[1]
            self.cut = self.rows // 32 * 16
            self.more = 0 if along is None else along.shape[0]
            self.pieces = [along]
            self.step = half
            if name:
                self.ahead, self.behind = ring_first(
                    me, blocks, along, self.cut, name + "_first"
                )
            else:
                far = self.take(half)
                self.ahead, self.behind = far[: self.cut], far[self.cut :]

        def take(self, step):
            start = (plane_of(place + step, planes), 0, 0)
            return lax.dynamic_slice(self.blocks, start, (1,) + self.blocks.shape[1:])[0]

        def go(self):
            self.hop()
            self.add()

        def hop(self):
            self.ahead, self.behind = hop(self.ahead, 1), hop(self.behind, -1)
            self.pieces += [self.ahead, self.behind]
            self.step -= 1

        def add(self):
            if self.step == 0:
                return
            cut = self.cut if self.step == half - 1 else 0
            if self.name:
                self.ahead, self.behind = ring_add(
                    me,
                    self.blocks,
                    self.ahead,
                    self.behind,
                    self.step,
                    cut,
                    self.more // 2 if self.step == 1 else self.more,
                    self.name,
                )
                return
            mine = self.take(self.step).astype(F32), self.take(-self.step).astype(F32)
            if cut:
                self.ahead = jnp.pad(self.ahead, ((0, self.rows - cut), (0, 0)))
                self.behind = jnp.pad(self.behind, ((cut, 0), (0, 0)))
            self.ahead = (mine[0] + self.ahead.astype(F32)).astype(BF)
            self.behind = (mine[1] + self.behind.astype(F32)).astype(BF)

        def last(self):
            return self.ahead, self.behind

        def result(self):
            return self.take(0).astype(F32) + self.ahead.astype(F32) + self.behind.astype(F32)

    def tie(rings, *values):
        state = [v for ring in rings for v in (ring.ahead, ring.behind)]
        out = list(lax.optimization_barrier(tuple(state) + values))
        for at, ring in enumerate(rings):
            ring.ahead, ring.behind = out[2 * at : 2 * at + 2]
        return out[2 * len(rings) :]

    def gather_whole(weight):
        return lax.all_gather(
            lax.all_gather(weight, "mod", axis=1, tiled=True), "dp", axis=0, tiled=True
        )

    def scatter_whole(padded):
        padded = lax.psum_scatter(padded.astype(BF), "mod", scatter_dimension=1, tiled=True)
        return lax.psum_scatter(padded, "dp", scatter_dimension=0, tiled=True).astype(F32)

    def stack_other_core(value):
        return jnp.stack(ordered(core, value, swap_core(value)))

    def group(value):
        other = swap_side(value)
        return [value, other, swap_core(value), swap_core(other)]

    columns_in = attend_in.shape[1]
    rows = feed_in.shape[0]
    out_slot = lambda index: lax.rem(index, 2) * half + index // 2
    cond_float = condition.astype(F32)
    silu_cond = jax.nn.silu(cond_float).astype(BF)
    mod_cols = modulate_weight.shape[1]
    small = jnp.pad(lengths, ((0, 0), (0, own_count - items_seq)))
    small = jnp.concatenate([positions, small], axis=0)
    quarter = head // 4
    entry = jnp.arange(head, dtype=I32)
    freq = jnp.power(10000.0, -(entry % quarter).astype(F32) / quarter)
    freq = jnp.broadcast_to(freq[:, None], (head, count))

    if ringed:
        silu_rows = lax.all_to_all(silu_cond, "dp", split_axis=1, concat_axis=0, tiled=True)
        silu_rows, attend_in_, feed_out_ = tie([], silu_rows, attend_in, feed_out)
        parts = sort_columns(me, attend_in_, head, lambda s: (s // 2, s % 2), "sort_in")
        keep = pick(side, feed_out_[:hid], feed_out_[hid:])
        came = swap_side(pick(side, feed_out_[hid:], feed_out_[:hid]))
        parts = [parts[0]] + [relate(parts[k], k) for k in (1, 2, 3)]
        kept, sent = mod_part(me, silu_rows, modulate_weight, planes)
        ring_a = Gather(make_unit(me, parts, [attend_out, keep, came], "unit_in"))
        kept, sent, small, tokens_ = tie([ring_a], kept, sent, small, tokens)
        ring_a.go()
        small_side = swap_side(small)
        tokens_side = swap_side(tokens_)
        ring_m = Scatter((kept + swap_core(sent).astype(F32)).astype(BF), "")
        small_side, feed_in_ = tie([ring_a, ring_m], small_side, feed_in)
        ring_a.go()
        ring_m.hop()
        small = [small, small_side, swap_core(small), swap_core(small_side)]
        parts = sort_columns(me, feed_in_, hid, lambda s: (s % 2, s // 2), "sort_up")
        tokens_side, cotangent_, *parts = tie([ring_a, ring_m], tokens_side, cotangent, *parts)
        ring_m.add()
        ring_a.go()
        ring_m.hop()
        parts = [parts[0]] + [relate(parts[k], k) for k in (1, 2, 3)]
        tokens_g = [tokens, tokens_side, swap_core(tokens), swap_core(tokens_side)]
        upstream_side = swap_side(cotangent_)
        small = tie([ring_a, ring_m], *small)
        ring_m.add()
        ring_a.go()
        ring_m.hop()
        ring_b = Gather(make_unit(me, parts, [], "unit_up"))
        tabled = make_tables(me, freq, small, seqs, dp_items, own_items)
        tabled = tie([ring_a, ring_b, ring_m], *tabled)
        ring_m.add()
        ring_b.go()
        ring_m.hop()
        ring_a.pieces[-2:] = [ring_a.ahead, ring_a.behind]
        w_in, w_out, w_down = assemble(
            me, ring_a.pieces, planes, 2 * rows, 3 * heads * head, "join_in"
        )
        w_out, w_in, upstream_side = tie([ring_b, ring_m], w_out, w_in, upstream_side)
        mods = group(ring_m.result().astype(BF))
        ring_b.go()
        w_out, *mods = tie([ring_b], w_out, *mods)
        mods = join_mods(me, mods)
        ring_b.go()
        w_out = w_out.reshape(2, half * head, width // 2)
        w_out_side = swap_side(w_out)
    else:
        silu_rows = lax.all_to_all(silu_cond, "dp", split_axis=1, concat_axis=0, tiled=True)
        partial = dot(silu_rows, modulate_weight)
        tabled = make_tables(me, freq, group(small), seqs, dp_items, own_items)
        tokens_g = group(tokens)
        upstream_g = group(cotangent)
        mods = lax.psum_scatter(partial, "dp", scatter_dimension=0, tiled=True).astype(BF)
        mods = lax.all_gather(mods, "mod", axis=1, tiled=True)
        mods = stack_other_core(mods).reshape(2 * dp_items, 6 * width)
        w_in = gather_whole(attend_in).reshape(width, 3 * heads, 4, head)
        w_in = lax.dynamic_index_in_dim(w_in, cls, 2, False).reshape(width, 3 * heads * head)
        w_out = gather_whole(attend_out).reshape(heads, 4, head, width)
        w_out = jnp.swapaxes(w_out, 0, 1).reshape(4, heads * head, width)
        share = 2 * core + side
        w_up = gather_whole(feed_in).reshape(width, 2 * planes, 4, hid)
        w_up = lax.dynamic_index_in_dim(w_up, share, 2, False).reshape(width, 2 * planes * hid)
        w_down = gather_whole(feed_out).reshape(planes, 4, hid, width)
        w_down = lax.dynamic_index_in_dim(w_down, share, 1, False).reshape(planes * hid, width)
    hidden_units = planes * hid

    cosine, sine, item_row, col = tabled
    item_col = col
    qg = jnp.broadcast_to(query_gain[:, None], (head, count))
    kg = jnp.broadcast_to(key_gain[:, None], (head, count))
    modded_one, raw, low, mixed = attend_forward(
        me, tokens_g, mods, w_in, cosine, sine, qg, kg, item_row, item_col, heads
    )
    if ringed:
        mixed, w_out_side = tie([ring_b], mixed, w_out_side)
        ring_b.go()
        mixed_side = swap_side(mixed)
        mixed_core = swap_core(mixed)
        upstream_g = [
            cotangent, upstream_side, swap_core(cotangent), swap_core(upstream_side)
        ]
        w_out = join_out(me, [w_out, w_out_side, swap_core(w_out), swap_core(w_out_side)])
        mixed_side, w_out, mixed_core, *upstream_g = tie(
            [ring_b], mixed_side, w_out, mixed_core, *upstream_g
        )
        ring_b.pieces[-2:] = [ring_b.ahead, ring_b.behind]
        (w_up,) = assemble(me, ring_b.pieces, planes, 2 * rows, ring_b.pieces[0].shape[1], "join_up")
    else:
        mixed_side = swap_side(mixed)
        mixed_core = swap_core(mixed)
    mixed_all = (mixed, mixed_side, mixed_core, swap_core(mixed_side))
    modded_two, gate_up, hidden, fed_grad, own_attended = feed_forward(
        me, tokens_g, upstream_g, mods, col, mixed_all, w_out.reshape(width, width), w_up
    )

    def two_cores(part):
        part = part.reshape(2, own_count, width)
        return (part[0].astype(F32) + swap_core(part[1]).astype(F32)).astype(BF)

    gate_up_grad, m2_far, fed_far = feed_backward(
        me, gate_up, hidden, fed_grad, w_up, w_down, 1, None
    )
    m2_far = two_cores(m2_far)
    if ringed:
        gate_up_grad, m2_far, fed_far = tie([], gate_up_grad, m2_far, fed_far)
    m2_side = swap_side(m2_far)
    gate_up_grad, m2_near, fed_near = feed_backward(
        me, gate_up, hidden, fed_grad, w_up, w_down, 0, gate_up_grad
    )
    if ringed:
        gate_up_grad, m2_near, fed_near = tie([], gate_up_grad, m2_near, fed_near)
        m2_core = swap_core(m2_near[own_count:])
        grads = feed_grads(me, modded_two, gate_up_grad, hidden, fed_grad, planes)
        ring_u = Scatter(grads, "up_add")
        fed_far = two_cores(fed_far)
        m2_side, m2_core, fed_near, fed_far = tie([ring_u], m2_side, m2_core, fed_near, fed_far)
        ring_u.hop()
    else:
        m2_core = swap_core(m2_near[own_count:])
        fed_far = two_cores(fed_far)
    resid_grad, attended_grad, early_sums = resid_back(
        me, tokens, cotangent, mods, col, own_attended, m2_near, m2_core, m2_side, own_items
    )
    side_grad = swap_side(attended_grad)
    core_grad = swap_core(attended_grad)
    shared = (
        w_out, w_in, raw, low, cosine, sine, qg, kg, item_row, item_col, tokens_g,
        2 * dp_items, heads,
    )
    projected_grad, m1_near, qg_near, kg_near, sums_near = attend_backward(
        me, attended_grad, core_grad, *shared, 0, None
    )
    if ringed:
        projected_grad, side_grad, fed_far, m1_near, fed_near = tie(
            [ring_u], projected_grad, side_grad, fed_far, m1_near, fed_near
        )
        ring_u.add()
    both_grad = swap_core(side_grad)
    fed_core = swap_core(fed_near[own_count:])
    if ringed:
        projected_grad, both_grad, fed_far = tie([ring_u], projected_grad, both_grad, fed_far)
        ring_u.hop()
    fed_side = swap_side(fed_far)
    projected_grad, m1_far, qg_far, kg_far, sums_far = attend_backward(
        me, side_grad, both_grad, *shared, 1, projected_grad
    )
    if ringed:
        projected_grad, m1_far, sums_far, fed_side, m1_near = tie(
            [ring_u], projected_grad, m1_far, sums_far, fed_side, m1_near
        )
        ring_u.add()
    gains = jnp.stack([jnp.sum(qg_near + qg_far, axis=1), jnp.sum(kg_near + kg_far, axis=1)])
    sums = sums_near + sums_far
    keep, came = sums[:dp_items], sums[dp_items:]
    sums = pick(core, keep, came) + swap_core(pick(core, came, keep))

    def as_row(values):
        top = lax.reduce_precision(values, 8, 7)
        row = jnp.concatenate([top.reshape(-1), (values - top).reshape(-1)]).astype(BF)
        return jnp.pad(row, (0, 2 * width - row.shape[0]))[None]

    def from_rows(row):
        return (row[: 2 * head] + row[2 * head : 4 * head]).reshape(2, head)

    if not ringed:
        block_out, late_sums = output(
            me, tokens, cotangent, mods, col, own_attended, fed_near, fed_core, fed_side, own_items
        )
        early = jnp.concatenate([early_sums, late_sums], axis=1)

    if ringed:
        gain_row = as_row(gains)
        found = swap_side(jnp.concatenate([sums.astype(BF), gain_row], axis=0))
        projected_grad, m1_far, m1_near = tie([ring_u], projected_grad, m1_far, m1_near)
        ring_u.hop()
        grads = attend_grads(
            me,
            modded_one,
            projected_grad,
            mixed,
            mixed_side,
            (attended_grad, side_grad, core_grad, both_grad),
            planes,
        )
        block_out, late_sums = output(
            me, tokens, cotangent, mods, col, own_attended, fed_near, fed_core, fed_side,
            own_items,
        )
        early = jnp.concatenate([early_sums, late_sums], axis=1)
        early_side = swap_side(early)
        grads, m1_far, m1_near, found, early, early_side = tie(
            [ring_u], grads, m1_far, m1_near, found, early, early_side
        )
        ring_u.add()
        sums = (sums + found[:-1].astype(F32)).astype(BF)
        gains = from_rows(jnp.sum(gain_row.astype(F32) + found[-1:].astype(F32), axis=0))
        early = jnp.concatenate(ordered(side, early, early_side), axis=0)
        parts = [
            pick(side, sums[:, :width], early[:, width : 2 * width]),
            pick(side, sums[:, width:], early[:, 2 * width : 3 * width]),
            pick(side, early[:, :width], early[:, 3 * width :]),
            as_row(gains)[:, :width],
        ]
        along = jnp.concatenate(parts, axis=0)
        along = jnp.pad(along, ((0, 64 - along.shape[0]), (0, 0)))
        ring_i = Scatter(grads, "in_add", along)
        m1_far, m1_near = tie([ring_u, ring_i], m1_far, m1_near)
        ring_u.hop()
        ring_i.hop()
        m1_far = two_cores(m1_far)
        m1_core = swap_core(m1_near[own_count:])
        m1_far, m1_core = tie([ring_u, ring_i], m1_far, m1_core)
        ring_i.add()
        ring_i.hop()
        m1_side = swap_side(m1_far)
        *up_parts, keep, came = split_sum(
            me, ring_u.blocks, *ring_u.last(), rows, planes * hid, hid, "up_split"
        )
        m1_side, came, *up_parts = tie([ring_i], m1_side, came, *up_parts)
        ring_i.add()
        ring_i.hop()
        up_parts = [up_parts[0]] + [relate(up_parts[k], k) for k in (1, 2, 3)]
        came = swap_side(came)
        tokens_grad = tokens_back(
            me, tokens, mods, col, resid_grad, m1_near, m1_core, m1_side
        )
        tokens_grad, came, *up_parts = tie([ring_i], tokens_grad, came, *up_parts)
        ring_i.add()
        ring_i.hop()
        feed_in_grad = unsort_columns(
            me, up_parts, hid, lambda s: (s % 2, s // 2), "unsort_up"
        )
        feed_out_grad = jnp.concatenate(ordered(side, keep, came), axis=0).astype(F32)
        other = [swap_core(piece) for piece in ring_i.pieces[:-2]]
        feed_in_grad, feed_out_grad, *other = tie([ring_i], feed_in_grad, feed_out_grad, *other)
        ring_i.pieces[-2:] = [ring_i.ahead, ring_i.behind]
        other += [swap_core(ring_i.ahead), swap_core(ring_i.behind)]
        *parts, attend_out_grad = split_sum(
            me, ring_i.blocks, *ring_i.last(), head, columns_in // 4, 0, "in_split"
        )
        other[-2], other[-1], *parts = tie([], other[-2], other[-1], *parts)
        modulate_grad, cond_terms, gains = mod_back(
            me, silu_rows, modulate_weight, ring_i.pieces, other, planes, dp_items
        )
        gains = from_rows(gains[0])
        cond_terms, *parts = tie([], cond_terms, *parts)
        parts = [parts[0]] + [relate(parts[k], k) for k in (1, 2, 3)]
        attend_in_grad = unsort_columns(
            me, parts, head, lambda s: (s // 2, s % 2), "unsort_in"
        )
    else:
        m1_side = swap_side(two_cores(m1_far))
        m1_core = swap_core(m1_near[own_count:])

        def padded(shape, value, axis, which):
            zero = jnp.zeros(shape, value.dtype)
            return lax.dynamic_update_index_in_dim(zero, value, which, axis)

        down_grad = weight_grad(me, hidden, fed_grad, hidden_units // 2, "down_grad")
        up_grad = weight_grad(me, modded_two, gate_up_grad, width // 3, "up_grad")
        grad = down_grad.reshape(planes, hid, width)
        grad = padded((planes, 4, hid, width), grad, 1, share)
        feed_out_grad = scatter_whole(grad.reshape(4 * hidden_units, width))
        grad = up_grad.reshape(width, 2 * planes, hid)
        grad = padded((width, 2 * planes, 4, hid), grad, 2, share)
        feed_in_grad = scatter_whole(grad.reshape(width, 8 * hidden_units))
        columns = [
            pick(side, value[:, : width // 2], value[:, width // 2 :])
            for value in (attended_grad, side_grad, core_grad, both_grad)
        ]
        near_rows = dot(mixed, jnp.concatenate(columns, axis=0))
        far_rows = dot(mixed_side, jnp.concatenate([columns[k] for k in (1, 0, 3, 2)], axis=0))
        out_grad = jnp.stack(ordered(side, near_rows, far_rows)).astype(BF)
        in_grad = weight_grad(me, modded_one, projected_grad, width // 3, "in_grad")
        grad = out_grad.reshape(2, heads, head, width // 2)
        grad = jnp.swapaxes(grad, 0, 1)
        grad = padded((heads, 2, head, 2, width // 2), grad, 3, side)
        grad = padded((heads, 2, 2, head, 2, width // 2), grad, 2, core)
        attend_out_grad = scatter_whole(grad.reshape(width, width))
        grad = in_grad.reshape(width, 3 * heads, head)
        grad = padded((width, 3 * heads, 4, head), grad, 2, cls)
        attend_in_grad = scatter_whole(grad.reshape(width, 3 * width))

    if not ringed:
        tokens_grad = tokens_back(
            me, tokens, mods, col, resid_grad, m1_near, m1_core, m1_side
        )

    if not ringed:
        sums = sums + swap_side(sums)
        found = lax.dynamic_slice_in_dim(sums, mod * own_items, own_items, 0).astype(BF)
        mod_grad = jnp.concatenate([found, early], axis=1)
        mod_grad = lax.all_to_all(mod_grad, "mod", split_axis=1, concat_axis=0, tiled=True)
        mod_grad = lax.all_gather(mod_grad, "dp", axis=0, tiled=True)
        gains = lax.psum(gains, ("dp", "mod"))
        modulate_grad = dot(silu_rows, mod_grad, 0, 0)
        cond_terms = dot(mod_grad, modulate_weight, 1, 1).astype(BF)
    cond_terms = lax.all_to_all(cond_terms, "dp", split_axis=0, concat_axis=1, tiled=True)
    own_width = width // nmod
    if ringed:
        left, right = cond_terms[:, :own_width], cond_terms[:, own_width:]
        came = swap_side(pick(side, right, left))
        cond_share = pick(side, left, right).astype(F32) + came.astype(F32)
    else:
        cond_share = lax.psum_scatter(
            cond_terms, "mod", scatter_dimension=1, tiled=True
        ).astype(F32)
    cond_cols = lax.dynamic_slice_in_dim(cond_float, mod * own_width, own_width, 1)
    cond_sigma = jax.nn.sigmoid(cond_cols)
    condition_grad = cond_share * cond_sigma * (1.0 + cond_cols * (1.0 - cond_sigma))
    return (
        block_out,
        tokens_grad,
        condition_grad,
        gains[0],
        gains[1],
        attend_in_grad,
        attend_out_grad,
        feed_in_grad,
        feed_out_grad,
        modulate_grad,
    )


def solution(mesh):
    rows = P(("dp", "mod"), None)
    both = P("dp", "mod")
    return jax.shard_map(
        body,
        mesh=mesh,
        in_specs=(
            rows,
            P("dp", None),
            rows,
            P(None, ("dp", "mod")),
            P(),
            P(),
            both,
            both,
            both,
            both,
            both,
            rows,
        ),
        out_specs=(rows, rows, both, P(), P(), both, both, both, both, both),
        check_vma=False,
    )
```

```python
import functools

import jax
import jax.numpy as jnp
from jax import lax
from jax.experimental import pallas as pl
from jax.experimental.pallas import tpu as pltpu
from jax.sharding import PartitionSpec as P

HIGHEST = lax.Precision.HIGHEST
BF = jnp.bfloat16
F32 = jnp.float32
I32 = jnp.int32
MIB = 2**20
STEP_ROWS = 128
ROOM = {
    "attend_forward": 24,
    "attend_backward": 56,
    "feed_forward": 33,
    "feed_backward": 18,
    "feed_grads": 40,
    "attend_grads": 32,
    "mod_back": 56,
    "down_grad": 32,
    "up_grad": 32,
    "in_grad": 32,
    "join_in": 20,
    "join_up": 20,
}


def layer_norm(values):
    average = jnp.mean(values, axis=-1, keepdims=True)
    centred = values - average
    spread = jnp.mean(centred * centred, axis=-1, keepdims=True)
    inverse = lax.rsqrt(spread + 1e-06)
    return (centred * inverse, inverse)


def norm_back(upstream, normed, inverse):
    first = jnp.mean(upstream, axis=-1, keepdims=True)
    second = jnp.mean(upstream * normed, axis=-1, keepdims=True)
    return inverse * (upstream - first - normed * second)


def dot(left, right, left_dim=1, right_dim=0):
    return lax.dot_general(
        left, right, (((left_dim,), (right_dim,)), ((), ())), preferred_element_type=F32
    )


def fence(*values):
    return lax.optimization_barrier(values)


def kernel_call(kernel, grid, in_specs, out_specs, out_shape, name, scratch=(), alias=None):
    return pl.pallas_call(
        kernel,
        grid_spec=pltpu.PrefetchScalarGridSpec(
            num_scalar_prefetch=1,
            grid=grid,
            in_specs=in_specs,
            out_specs=out_specs,
            scratch_shapes=list(scratch),
        ),
        out_shape=out_shape,
        input_output_aliases=alias or {},
        compiler_params=pltpu.CompilerParams(vmem_limit_bytes=ROOM.get(name, 16) * MIB),
        cost_estimate=pl.CostEstimate(flops=1024, bytes_accessed=1024, transcendentals=0),
        name=name,
    )


def whole_spec(shape):
    return pl.BlockSpec(shape, lambda *_: (0,) * len(shape))


def fixed_spec(shape):
    return pl.BlockSpec(shape, lambda *_: (0,) * len(shape), pipeline_mode=pl.Buffered(1))


def lead_spec(shape):
    return pl.BlockSpec((1,) + shape[1:], lambda i, *_: (i,) + (0,) * (len(shape) - 1))


def shaped(shape, dtype):
    return jax.ShapeDtypeStruct(shape, dtype)


def plane_of(ring, planes):
    ring = lax.rem(ring + 2 * planes, planes)
    return jnp.where(ring < planes // 2, 2 * ring, 2 * (planes - 1 - ring) + 1)


SIDE, CORE, PLACE, CLS, FIRST = 0, 1, 2, 3, 4


def sort_kernel(width, share_of, me_ref, weight_ref, *outs):
    rows, columns = weight_ref.shape
    groups = columns // (4 * width)
    for share in range(4):
        side, core = share_of(share)
        pieces = [
            weight_ref[:, (4 * g + share) * width : (4 * g + share + 1) * width]
            for g in range(groups)
        ]
        value = jnp.concatenate(pieces, axis=1)
        relation = 2 * (me_ref[CORE] ^ core) + (me_ref[SIDE] ^ side)
        for k in range(4):

            @pl.when(relation == k)
            def _(k=k, value=value):
                outs[k][...] = value


def sort_columns(me, weight, width, share_of, name):
    rows, columns = weight.shape
    return kernel_call(
        functools.partial(sort_kernel, width, share_of),
        (1,),
        [whole_spec(weight.shape)],
        [whole_spec((rows, columns // 4))] * 4,
        [shaped((rows, columns // 4), weight.dtype)] * 4,
        name,
    )(me, weight)


def quad(me_ref, refs):
    own, side, core, both = (ref[...].astype(F32) for ref in refs)
    here = me_ref[SIDE] == 0
    near = jnp.concatenate([jnp.where(here, own, side), jnp.where(here, side, own)], axis=1)
    far = jnp.concatenate([jnp.where(here, core, both), jnp.where(here, both, core)], axis=1)
    here = me_ref[CORE] == 0
    return jnp.concatenate([jnp.where(here, near, far), jnp.where(here, far, near)], axis=0)


def unit_kernel(me_ref, a_ref, b_ref, c_ref, d_ref, *rest):
    out_ref = rest[-1]
    value = quad(me_ref, (a_ref, b_ref, c_ref, d_ref)).astype(BF)
    rows, columns = value.shape
    out_ref[:rows, :columns] = value
    if len(rest) == 1:
        return
    extra = rest[0][...].astype(F32)
    half = extra.shape[1] // 2
    extra = jnp.concatenate([extra[:, :half], extra[:, half:]], axis=0).astype(BF)
    out_ref[:rows, columns:] = extra
    keep, came = rest[1][...].astype(F32), rest[2][...].astype(F32)
    here = me_ref[SIDE] == 0
    value = jnp.concatenate([jnp.where(here, keep, came), jnp.where(here, came, keep)], axis=1)
    out_ref[rows:, :] = value.astype(BF)


def make_unit(me, parts, extras, name):
    rows, columns = parts[0].shape
    high, wide = 2 * rows, 2 * columns
    if extras:
        high, wide = high + extras[1].shape[0], wide + extras[0].shape[1] // 2
    operands = list(parts) + list(extras)
    return kernel_call(
        unit_kernel,
        (1,),
        [whole_spec(v.shape) for v in operands],
        whole_spec((high, wide)),
        shaped((high, wide), BF),
        name,
    )(me, *operands)


def gather_steps(planes):
    return [0] + [s * d for d in range(1, planes // 2) for s in (-1, 1)] + [planes // 2]


def assemble_kernel(planes, rows, split, me_ref, *refs):
    pieces = len(gather_steps(planes)) + 1
    outs = refs[pieces:]
    high = refs[0].shape[0]
    for at, step in enumerate(gather_steps(planes)):
        plane = plane_of(me_ref[PLACE] + step, planes)
        if at == pieces - 2:
            value = jnp.concatenate(
                [refs[at][...].astype(F32), refs[at + 1][...].astype(F32)], axis=0
            ).astype(BF)
        else:
            value = refs[at][...]
        outs[0][pl.ds(pl.multiple_of(plane * rows, 16), rows), :] = value[:rows, :split]
        if len(outs) > 1:
            slot = lax.rem(plane, 2) * (planes // 2) + plane // 2
            extra = value[:rows, split:].astype(F32)
            extra = jnp.concatenate([extra[: rows // 2], extra[rows // 2 :]], axis=1)
            outs[1][slot] = extra.astype(BF)
            rest = high - rows
            outs[2][pl.ds(pl.multiple_of(plane * rest, 16), rest), :] = value[rows:]


def assemble(me, pieces, planes, rows, split, name):
    high, columns = pieces[0].shape
    outs = [shaped((planes * rows, split), BF)]
    if split < columns:
        outs.append(shaped((planes, rows // 2, 2 * (columns - split)), BF))
        outs.append(shaped((planes * (high - rows), columns), BF))
    return kernel_call(
        functools.partial(assemble_kernel, planes, rows, split),
        (1,),
        [whole_spec(v.shape) for v in pieces],
        [whole_spec(v.shape) for v in outs],
        outs,
        name,
    )(me, *pieces)


def mod_part_kernel(me_ref, rows_ref, weight_ref, keep_ref, send_ref):
    columns = keep_ref.shape[2]
    product = dot(rows_ref[...], weight_ref[...]).reshape(keep_ref.shape[:2] + (2 * columns,))
    here = me_ref[CORE] == 0
    left, right = product[:, :, :columns], product[:, :, columns:]
    keep_ref[...] = jnp.where(here, left, right)
    send_ref[...] = jnp.where(here, right, left).astype(BF)


def mod_part(me, rows, weight, planes):
    shape = (planes, rows.shape[0] // planes, weight.shape[1] // 2)
    return kernel_call(
        mod_part_kernel,
        (1,),
        [whole_spec(rows.shape), whole_spec(weight.shape)],
        [whole_spec(shape)] * 2,
        [shaped(shape, F32), shaped(shape, BF)],
        "mod_part",
    )(me, rows, weight)


def split_kernel(rows, columns, me_ref, own_ref, ahead_ref, behind_ref, *outs):
    height = own_ref.shape[1]
    total = own_ref[0].astype(F32) + ahead_ref[:height].astype(F32)
    total = total + behind_ref[:height].astype(F32)
    for side in range(2):
        for core in range(2):
            value = total[core * rows : (core + 1) * rows, side * columns : (side + 1) * columns]
            relation = 2 * (me_ref[CORE] ^ core) + (me_ref[SIDE] ^ side)
            for k in range(4):

                @pl.when(relation == k)
                def _(k=k, value=value):
                    outs[k][...] = value.astype(BF)

    if len(outs) == 5:
        extra = total[: 2 * rows, 2 * columns :]
        outs[4][...] = jnp.concatenate([extra[:rows], extra[rows:]], axis=1)
    if len(outs) == 6:
        low, width = outs[4].shape
        width *= 2
        value = total[2 * rows :]
        high = value.shape[0]
        tail = value[:, width:]
        step = low - high
        tail = [tail[at : at + step] for at in range(0, high, step)]
        value = jnp.concatenate([value[:, :width], jnp.concatenate(tail, axis=1)], axis=0)
        here = me_ref[SIDE] == 0
        left, right = value[:, : width // 2], value[:, width // 2 :]
        outs[4][...] = jnp.where(here, left, right).astype(BF)
        outs[5][...] = jnp.where(here, right, left).astype(BF)


def split_sum(me, blocks, ahead, behind, rows, columns, low, name):
    planes, height, wide = blocks.shape
    outs = [shaped((rows, columns), BF)] * 4
    if low:
        outs += [shaped((low, (height - 2 * rows) * wide // low // 2), BF)] * 2
    else:
        outs.append(shaped((rows, 2 * (wide - 2 * columns)), F32))
    return kernel_call(
        functools.partial(split_kernel, rows, columns),
        (1,),
        [
            pl.BlockSpec((1, height, wide), lambda i, me: (plane_of(me[PLACE], planes), 0, 0)),
            whole_spec(ahead.shape),
            whole_spec(behind.shape),
        ],
        [whole_spec(v.shape) for v in outs],
        outs,
        name,
    )(me, blocks, ahead, behind)


def unsort_kernel(width, share_of, me_ref, *refs):
    out_ref = refs[-1]
    groups = refs[0].shape[1] // width
    found = [ref[...].astype(F32) for ref in refs[:4]]
    shares = []
    for share in range(4):
        side, core = share_of(share)
        near, far = me_ref[SIDE] == side, me_ref[CORE] == core
        shares.append(
            jnp.where(
                far,
                jnp.where(near, found[0], found[1]),
                jnp.where(near, found[2], found[3]),
            )
        )
    out_ref[...] = jnp.concatenate(
        [shares[s][:, g * width : (g + 1) * width] for g in range(groups) for s in range(4)],
        axis=1,
    )


def unsort_columns(me, parts, width, share_of, name):
    rows, columns = parts[0].shape
    return kernel_call(
        functools.partial(unsort_kernel, width, share_of),
        (1,),
        [whole_spec(v.shape) for v in parts],
        whole_spec((rows, 4 * columns)),
        shaped((rows, 4 * columns), F32),
        name,
    )(me, *parts)


def attend_grads_kernel(
    planes, me_ref, modded_ref, grad_ref, mixed_ref, mixed_side_ref, a_ref, b_ref, c_ref, d_ref,
    out_ref,
):
    rows = out_ref.shape[1]
    columns = grad_ref.shape[1]
    count, width = a_ref.shape
    whole = dot(modded_ref[...], grad_ref[...], 0, 0).astype(BF)
    for plane in range(planes):
        out_ref[plane, :, :columns] = whole[plane * rows : (plane + 1) * rows]
    here = me_ref[SIDE] == 0
    blocks = [
        jnp.where(here, ref[:, : width // 2].astype(F32), ref[:, width // 2 :].astype(F32))
        for ref in (a_ref, b_ref, c_ref, d_ref)
    ]
    head = rows // 2
    half = width // 4
    for flip, ref in enumerate((mixed_ref, mixed_side_ref)):
        order = jnp.concatenate([blocks[k ^ flip] for k in range(4)], axis=0).astype(BF)
        found = dot(ref[...], order)
        for j in range(found.shape[0] // head):
            value = found[j * head : (j + 1) * head]
            value = jnp.concatenate([value[:, :half], value[:, half:]], axis=0).astype(BF)
            out_ref[2 * j + (me_ref[SIDE] ^ flip), :, columns:] = value


def attend_grads(me, modded, grad, mixed, mixed_side, attended_grads, planes):
    width = modded.shape[1]
    rows = width // planes
    out = shaped((planes, rows, grad.shape[1] + width // 4), BF)
    operands = [modded, grad, mixed, mixed_side, *attended_grads]
    return kernel_call(
        functools.partial(attend_grads_kernel, planes),
        (1,),
        [whole_spec(v.shape) for v in operands],
        whole_spec(out.shape),
        out,
        "attend_grads",
    )(me, *operands)


def ring_first_kernel(cut, me_ref, mine_ref, *refs):
    ahead_out, behind_out = refs[-2:]
    rows = mine_ref.shape[1]
    ahead_out[:cut] = mine_ref[0, :cut]
    behind_out[: rows - cut] = mine_ref[0, cut:]
    if len(refs) > 2:
        ahead_out[cut:] = refs[0][...]
        behind_out[rows - cut :] = refs[0][...]


def ring_first(me, blocks, along, cut, name):
    planes, rows, columns = blocks.shape
    more = 0 if along is None else along.shape[0]
    operands = [blocks] if along is None else [blocks, along]
    outs = [shaped((cut + more, columns), BF), shaped((rows - cut + more, columns), BF)]
    return kernel_call(
        functools.partial(ring_first_kernel, cut),
        (1,),
        [
            pl.BlockSpec(
                (1, rows, columns),
                lambda i, me: (plane_of(me[PLACE] + planes // 2, planes), 0, 0),
            ),
            *[whole_spec(v.shape) for v in operands[1:]],
        ],
        [whole_spec(v.shape) for v in outs],
        outs,
        name,
    )(me, *operands)


def ring_add_kernel(cut, me_ref, ahead_mine, behind_mine, ahead, behind, ahead_out, behind_out):
    rows = ahead_mine.shape[1]
    came = cut or rows
    ahead_out[:came] = (ahead_mine[0, :came].astype(F32) + ahead[:came].astype(F32)).astype(BF)
    if cut:
        ahead_out[cut:rows] = ahead_mine[0, cut:]
    kept = ahead_out.shape[0] - rows
    if kept:
        ahead_out[rows:] = ahead[came : came + kept]
    start = cut
    came = rows - cut
    behind_out[start:rows] = (
        behind_mine[0, start:].astype(F32) + behind[:came].astype(F32)
    ).astype(BF)
    if cut:
        behind_out[:cut] = behind_mine[0, :cut]
    if kept:
        behind_out[rows:] = behind[behind.shape[0] - kept :]


def ring_add(me, blocks, ahead, behind, step, cut, kept, name):
    planes, rows, columns = blocks.shape

    def at(sign):
        return lambda i, me: (plane_of(me[PLACE] + sign * step, planes), 0, 0)

    block = (1, rows, columns)
    out = shaped((rows + kept, columns), BF)
    return kernel_call(
        functools.partial(ring_add_kernel, cut),
        (1,),
        [
            pl.BlockSpec(block, at(1)),
            pl.BlockSpec(block, at(-1)),
            whole_spec(ahead.shape),
            whole_spec(behind.shape),
        ],
        [whole_spec(out.shape)] * 2,
        [out] * 2,
        name,
    )(me, blocks, blocks, ahead, behind)


def weight_grad_kernel(me_ref, left_ref, right_ref, out_ref):
    out_ref[...] = dot(left_ref[...], right_ref[...], 0, 0).astype(BF)


def weight_grad(me, left, right, tile, name):
    count, rows = left.shape
    columns = right.shape[1]
    return kernel_call(
        weight_grad_kernel,
        (rows // tile,),
        [pl.BlockSpec((count, tile), lambda i, *_: (0, i)), whole_spec(right.shape)],
        pl.BlockSpec((tile, columns), lambda i, *_: (i, 0)),
        shaped((rows, columns), BF),
        name,
    )(me, left, right)


def feed_grads_kernel(planes, me_ref, modded_ref, grad_ref, hidden_ref, fed_grad_ref, out_ref):
    wide = out_ref.shape[2]
    width = modded_ref.shape[1]
    rows, low = width // planes, hidden_ref.shape[1] // planes
    high = low * width // wide
    rest = wide - width
    down = dot(hidden_ref[...], fed_grad_ref[...], 0, 0)
    for plane in range(planes):
        value = down[plane * low : (plane + 1) * low]
        tail = [value[high:, at : at + rest] for at in range(0, width, rest)]
        value = jnp.concatenate([value[:high], jnp.concatenate(tail, axis=0)], axis=1)
        out_ref[plane, rows:, :] = value.astype(BF)
    up = dot(modded_ref[...], grad_ref[...], 0, 0)
    for plane in range(planes):
        out_ref[plane, :rows, :] = up[plane * rows : (plane + 1) * rows].astype(BF)


def feed_grads(me, modded, grad, hidden, fed_grad, planes):
    width, wide = modded.shape[1], grad.shape[1]
    rows = width // planes + hidden.shape[1] // planes * width // wide
    out = shaped((planes, rows, wide), BF)
    operands = [modded, grad, hidden, fed_grad]
    return kernel_call(
        functools.partial(feed_grads_kernel, planes),
        (1,),
        [whole_spec(v.shape) for v in operands],
        whole_spec(out.shape),
        out,
        "feed_grads",
    )(me, *operands)


def turned(values, first):
    quarter = values.shape[0] // 4
    ahead = pltpu.roll(values, values.shape[0] - quarter, 0)
    behind = pltpu.roll(values, quarter, 0)
    return jnp.where(first, ahead, behind)


def rms(values):
    return lax.rsqrt(jnp.mean(values * values, axis=0, keepdims=True) + 1e-06)


def scores_t(key_rot, query_rot, same, scale):
    raw = dot(key_rot, query_rot, 0, 0) * scale
    return jnp.where(same, raw, -1e30)


def softmax_t(scores):
    peak = jnp.max(scores, axis=0, keepdims=True)
    exponent = jnp.exp(scores - peak)
    return exponent / jnp.sum(exponent, axis=0, keepdims=True)


def first_mask(head, count):
    row = lax.broadcasted_iota(I32, (head, count), 0)
    return lax.rem(row, head // 2) < head // 4


def by_rows(count, work, step=STEP_ROWS):
    step = min(step, count)
    for at in range(0, count, step):
        work(slice(at, at + step))


def put_chosen(out_ref, refs, at, per):
    for k, ref in enumerate(refs):

        @pl.when(at // per == k)
        def _(ref=ref):
            out_ref[...] = ref[...]


def chosen(refs, at, per):
    value = refs[0][...]
    for k, ref in enumerate(refs[1:], 1):
        value = jnp.where(at >= k * per, ref[...], value)
    return value


def quarter_specs(shape, per, parts):
    return [
        pl.BlockSpec(shape, lambda i, *_, k=k: (jnp.clip(i - k * per, 0, per - 1), 0))
        for k in range(parts)
    ]


def join_mods_kernel(me_ref, a_ref, b_ref, c_ref, d_ref, out_ref):
    own, side, core, both = (ref[...].astype(F32) for ref in (a_ref, b_ref, c_ref, d_ref))
    here = me_ref[CORE] == 0
    near = [jnp.where(here, own, core), jnp.where(here, core, own)]
    far = [jnp.where(here, side, both), jnp.where(here, both, side)]
    here = me_ref[SIDE] == 0
    parts = [jnp.where(here, n, f) for n, f in zip(near, far)]
    parts += [jnp.where(here, f, n) for n, f in zip(near, far)]
    out_ref[...] = jnp.concatenate(parts, axis=1).astype(BF)


def join_mods(me, parts):
    items, columns = parts[0].shape
    return kernel_call(
        join_mods_kernel,
        (1,),
        [whole_spec(v.shape) for v in parts],
        whole_spec((items, 4 * columns)),
        shaped((items, 4 * columns), BF),
        "join_mods",
    )(me, *parts)


def join_out_kernel(me_ref, a_ref, b_ref, c_ref, d_ref, out_ref):
    here = me_ref[SIDE] == 0
    for other, (near, far) in enumerate(((a_ref, b_ref), (c_ref, d_ref))):
        for side in range(2):
            own, off = near[side].astype(F32), far[side].astype(F32)
            value = jnp.concatenate([jnp.where(here, own, off), jnp.where(here, off, own)], axis=1)
            out_ref[2 * side + (me_ref[CORE] ^ other)] = value.astype(BF)


def join_out(me, parts):
    _, rows, columns = parts[0].shape
    return kernel_call(
        join_out_kernel,
        (1,),
        [whole_spec(v.shape) for v in parts],
        whole_spec((4, rows, 2 * columns)),
        shaped((4, rows, 2 * columns), BF),
        "join_out",
    )(me, *parts)


def tables_kernel(dp_items, own_items, me_ref, freq_ref, *refs):
    cos_ref, sin_ref, row_ref, col_ref = refs[4:]
    head, count = freq_ref.shape
    seqs = cos_ref.shape[0] // 4
    items = own_items // seqs
    entry = lax.broadcasted_iota(I32, (head, count), 0)
    low = lax.rem(entry, head // 2) < head // 4
    for k in range(4):
        base = (me_ref[CORE] ^ (k >> 1)) * dp_items
        base += me_ref[FIRST] - me_ref[CORE] * dp_items
        base += jnp.where(me_ref[SIDE] == 0, k & 1, -(k & 1)) * own_items
        for q in range(seqs):
            at = k * seqs + q
            spots = refs[k][:2, q * count : (q + 1) * count]
            spot = jnp.where(entry < head // 2, spots[0:1], spots[1:2]).astype(F32)
            angle = spot * freq_ref[...]
            sine = jnp.sin(angle)
            cos_ref[at] = jnp.cos(angle)
            sin_ref[at] = jnp.where(low, -sine, sine)
            for ref, shape, axis in ((row_ref, (1, count), 1), (col_ref, (count, 1), 0)):
                token = lax.broadcasted_iota(I32, shape, axis)
                end = jnp.zeros((1, 1), I32)
                item = jnp.zeros(shape, I32) + (base + q * items)
                for j in range(items):
                    end = end + refs[k][2 + q : 3 + q, j : j + 1]
                    item = item + (token >= end).astype(I32)
                ref[at] = item


def make_tables(me, freq, small, seqs, dp_items, own_items):
    head, count = freq.shape
    outs = [
        shaped((seqs, head, count), F32),
        shaped((seqs, head, count), F32),
        shaped((seqs, 1, count), I32),
        shaped((seqs, count, 1), I32),
    ]
    return kernel_call(
        functools.partial(tables_kernel, dp_items, own_items),
        (1,),
        [whole_spec(v.shape) for v in (freq, *small)],
        [whole_spec(v.shape) for v in outs],
        outs,
        "tables",
    )(me, freq, *small)


def members_of(column, items):
    lane = lax.broadcasted_iota(I32, (column.shape[0], items), 1)
    return (column == lane).astype(BF)


def attend_forward_kernel(
    heads, head, me_ref, t0_ref, t1_ref, t2_ref, t3_ref, mods_ref, weight_ref, cos_ref, sin_ref,
    qg_ref, kg_ref, row_ref, col_ref, modded_ref, raw_ref, low_ref, mixed_ref, held_ref,
    tokens_ref, token_mod_ref,
):
    count, width = t0_ref.shape
    per = pl.num_programs(0) // 4
    put_chosen(tokens_ref, (t0_ref, t1_ref, t2_ref, t3_ref), pl.program_id(0), per)
    own = heads * head
    members = members_of(col_ref[0], mods_ref.shape[0])
    token_mod_ref[...] = dot(members, mods_ref[:, : 2 * width])

    def modulated(at):
        normed, _ = layer_norm(tokens_ref[at, :].astype(F32))
        modded = normed * (1.0 + token_mod_ref[at, width:]) + token_mod_ref[at, :width]
        modded_ref[at, :] = modded.astype(BF)

    by_rows(count, modulated)
    projected = dot(modded_ref[...], weight_ref[...]).T
    raw_ref[0] = projected[: 2 * own]
    values = projected[2 * own :]
    low_ref[0] = values.astype(BF)
    same = col_ref[0] == row_ref[0]
    first = first_mask(head, count)
    cosine, sine = cos_ref[0], sin_ref[0]
    scale = head ** (-0.5)

    def rotated(raw, gain):
        normed = raw * rms(raw) * gain
        return (normed * cosine + turned(normed, first) * sine).astype(BF)

    for h in range(heads):
        query_rot = rotated(projected[h * head : (h + 1) * head], qg_ref[...])
        key_rot = rotated(projected[own + h * head : own + (h + 1) * head], kg_ref[...])
        prob = softmax_t(scores_t(key_rot, query_rot, same, scale)).astype(BF)
        mixed = dot(values[h * head : (h + 1) * head].astype(BF), prob)
        held_ref[h * head : (h + 1) * head, :] = mixed
    mixed_ref[...] = held_ref[...].astype(BF)


def attend_forward(me, tokens, mods, weight, cosine, sine, qg, kg, row, col, heads):
    seqs, head, count = cosine.shape
    width = tokens[0].shape[1]
    own = heads * head
    return kernel_call(
        functools.partial(attend_forward_kernel, heads, head),
        (seqs,),
        [
            *quarter_specs((count, width), seqs // 4, 4),
            whole_spec(mods.shape),
            whole_spec(weight.shape),
            lead_spec(cosine.shape),
            lead_spec(sine.shape),
            whole_spec(qg.shape),
            whole_spec(kg.shape),
            lead_spec(row.shape),
            lead_spec(col.shape),
        ],
        [
            pl.BlockSpec((count, width), lambda i, *_: (i, 0)),
            lead_spec((seqs, 2 * own, count)),
            lead_spec((seqs, own, count)),
            pl.BlockSpec((own, count), lambda i, *_: (0, i)),
        ],
        [
            shaped((seqs * count, width), BF),
            shaped((seqs, 2 * own, count), F32),
            shaped((seqs, own, count), BF),
            shaped((own, seqs * count), BF),
        ],
        "attend_forward",
        [
            pltpu.VMEM((own, count), F32),
            pltpu.VMEM((count, width), BF),
            pltpu.VMEM((count, 2 * width), F32),
        ],
    )(me, *tokens, mods, weight, cosine, sine, qg, kg, row, col)


def attend_backward_kernel(
    heads, head, me_ref, near_ref, far_ref, out_w_ref, in_w_ref, raw_ref, low_ref, cos_ref,
    sin_ref, qg_ref, kg_ref, row_ref, col_ref, near_tokens_ref, far_tokens_ref, *rest,
):
    out_ref, m1_ref, qgg_ref, kgg_ref, sums_ref, held_ref, tokens_ref, m1_held, scaled_ref = rest[
        -9:
    ]
    own = heads * head
    half = pl.num_programs(0) // 2
    grad = chosen((near_ref, far_ref), pl.program_id(0), half)
    put_chosen(tokens_ref, (near_tokens_ref, far_tokens_ref), pl.program_id(0), half)
    count = grad.shape[0]
    mixed_grad = dot(out_w_ref[0], grad, 1, 1)
    same = col_ref[0] == row_ref[0]
    first = first_mask(head, count)
    cosine, sine = cos_ref[0], sin_ref[0]
    scale = head ** (-0.5)

    @pl.when(pl.program_id(0) == 0)
    def _():
        qgg_ref[...] = jnp.zeros_like(qgg_ref)
        kgg_ref[...] = jnp.zeros_like(kgg_ref)
        sums_ref[...] = jnp.zeros_like(sums_ref)

    def rotated(raw, gain):
        inverse = rms(raw)
        normed = raw * inverse * gain
        return inverse, (normed * cosine + turned(normed, first) * sine).astype(BF)

    def back(rot_grad, raw, inverse, gain):
        norm_grad = rot_grad * cosine + turned(rot_grad * sine, first)
        gain_grad = norm_grad * raw * inverse
        scaled = norm_grad * gain
        inner = jnp.mean(scaled * raw, axis=0, keepdims=True)
        return inverse * scaled - raw * (inverse * inverse * inverse * inner), gain_grad

    query_total = jnp.zeros((head, count), F32)
    key_total = jnp.zeros((head, count), F32)
    low = low_ref[0].astype(F32)
    for h in range(heads):
        rows = slice(h * head, (h + 1) * head)
        query_raw = raw_ref[0, h * head : (h + 1) * head]
        key_raw = raw_ref[0, own + h * head : own + (h + 1) * head]
        values = low[rows].astype(BF)
        upstream = mixed_grad[rows].astype(BF)
        query_inverse, query_rot = rotated(query_raw, qg_ref[...])
        key_inverse, key_rot = rotated(key_raw, kg_ref[...])
        prob = softmax_t(scores_t(key_rot, query_rot, same, scale))
        prob_grad = dot(values, upstream, 0, 0)
        inner = jnp.sum(prob * prob_grad, axis=0, keepdims=True)
        score_grad = (prob * (prob_grad - inner)).astype(BF)
        query_rot_grad = dot(key_rot, score_grad) * scale
        key_rot_grad = dot(query_rot, score_grad, 1, 1) * scale
        values_grad = dot(upstream, prob.astype(BF), 1, 1)
        query_grad, query_part = back(query_rot_grad, query_raw, query_inverse, qg_ref[...])
        key_grad, key_part = back(key_rot_grad, key_raw, key_inverse, kg_ref[...])
        query_total += query_part
        key_total += key_part
        held_ref[h * head : (h + 1) * head, :] = query_grad
        held_ref[own + h * head : own + (h + 1) * head, :] = key_grad
        held_ref[2 * own + h * head : 2 * own + (h + 1) * head, :] = values_grad
    qgg_ref[...] += query_total
    kgg_ref[...] += key_total
    projected_grad = held_ref[...].T.astype(BF)
    out_ref[...] = projected_grad
    m1_held[...] = dot(projected_grad, in_w_ref[...], 1, 1)

    def scaled(at):
        m1 = m1_held[at, :]
        normed, _ = layer_norm(tokens_ref[at, :].astype(F32))
        m1_ref[at, :] = m1.astype(BF)
        scaled_ref[at, :] = (m1 * normed).astype(BF)

    by_rows(count, scaled)
    members = members_of(col_ref[0], sums_ref.shape[0])
    width = m1_ref.shape[1]
    sums_ref[:, :width] += dot(members, m1_ref[...], 0, 0)
    sums_ref[:, width:] += dot(members, scaled_ref[...], 0, 0)


def attend_backward(
    me, near, far, w_out, w_in, raw, low, cosine, sine, qg, kg, row, col, tokens, items, heads,
    at, held,
):
    seqs, head, count = cosine.shape
    width = near.shape[1]
    own = heads * head
    per = seqs // 4

    def seq(i):
        return at * per + i + jnp.where(i < per, 0, per)

    def block(shape):
        return pl.BlockSpec((1,) + shape[1:], lambda i, *_: (seq(i), 0, 0))

    in_specs = [
        *quarter_specs((count, width), per, 2),
        pl.BlockSpec((1,) + w_out.shape[1:], lambda i, me: (me[CLS], 0, 0)),
        whole_spec(w_in.shape),
        block(raw.shape),
        block(low.shape),
        block(cosine.shape),
        block(sine.shape),
        whole_spec(qg.shape),
        whole_spec(kg.shape),
        block(row.shape),
        block(col.shape),
        *quarter_specs((count, width), per, 2),
    ]
    operands = [near, far, w_out, w_in, raw, low, cosine, sine, qg, kg, row, col]
    operands += [tokens[at], tokens[at + 2]]
    alias = {}
    if held is not None:
        alias = {1 + len(operands): 0}
        operands.append(held)
        in_specs.append(pl.BlockSpec(memory_space=pl.ANY))
    return kernel_call(
        functools.partial(attend_backward_kernel, heads, head),
        (2 * per,),
        in_specs,
        [
            pl.BlockSpec((count, 3 * own), lambda i, *_: (seq(i), 0)),
            pl.BlockSpec((count, width), lambda i, *_: (i, 0)),
            whole_spec((head, count)),
            whole_spec((head, count)),
            whole_spec((items, 2 * width)),
        ],
        [
            shaped((seqs * count, 3 * own), BF),
            shaped((2 * per * count, width), BF),
            shaped((head, count), F32),
            shaped((head, count), F32),
            shaped((items, 2 * width), F32),
        ],
        "attend_backward",
        [
            pltpu.VMEM((3 * own, count), F32),
            pltpu.VMEM((count, width), BF),
            pltpu.VMEM((count, width), F32),
            pltpu.VMEM((count, width), BF),
        ],
        alias,
    )(me, *operands)


def feed_forward_kernel(me_ref, *refs):
    mods_ref, col_ref, m0_ref, m1_ref, m2_ref, m3_ref, w_out_ref, w_up_ref = refs[8:16]
    modded_ref, gate_up_ref, hidden_ref, fed_grad_ref, attended_ref = refs[16:21]
    mixed_ref, tokens_ref, upstream_ref, held_ref, token_mod_ref, gate_up_held = refs[21:]
    put_chosen(tokens_ref, refs[:4], pl.program_id(0), 1)
    put_chosen(upstream_ref, refs[4:8], pl.program_id(0), 1)
    count, width = tokens_ref.shape
    own = m0_ref.shape[0]
    for k, ref in enumerate((m0_ref, m1_ref, m2_ref, m3_ref)):
        cls = 2 * (me_ref[SIDE] ^ (k & 1)) + (me_ref[CORE] ^ (k >> 1))
        mixed_ref[pl.ds(pl.multiple_of(cls * own, 16), own), :] = ref[...]
    held_ref[...] = dot(mixed_ref[...], w_out_ref[...], 0, 0)

    @pl.when(pl.program_id(0) == 0)
    def _():
        attended_ref[...] = held_ref[...]

    members = members_of(col_ref[...].reshape(-1, 1), mods_ref.shape[0])
    token_mod_ref[...] = dot(members, mods_ref[:, 2 * width :])

    def modulated(at):
        resid = tokens_ref[at, :].astype(F32) + token_mod_ref[at, :width] * held_ref[at, :]
        normed, _ = layer_norm(resid)
        scale = token_mod_ref[at, 2 * width : 3 * width]
        modded = normed * (1.0 + scale) + token_mod_ref[at, width : 2 * width]
        modded_ref[at, :] = modded.astype(BF)
        grad = token_mod_ref[at, 3 * width :] * upstream_ref[at, :].astype(F32)
        fed_grad_ref[at, :] = grad.astype(BF)

    by_rows(count, modulated)
    gate_up_held[...] = dot(modded_ref[...], w_up_ref[...])
    units = hidden_ref.shape[1]

    def activated(at):
        gate, up = gate_up_held[at, :units], gate_up_held[at, units:]
        sigma = jax.nn.sigmoid(gate)
        silu = gate * sigma
        hidden_ref[at, :] = (silu * up).astype(BF)
        gate_up_ref[at, :units] = (up * (sigma * (1.0 + gate * (1.0 - sigma)))).astype(BF)
        gate_up_ref[at, units:] = silu.astype(BF)

    by_rows(count, activated)


def feed_forward(me, tokens, upstream, mods, col, mixed, w_out, w_up):
    count, width = tokens[0].shape
    total = 4 * count
    own = mixed[0].shape[0]
    per = col.shape[0] // 4
    columns = w_up.shape[1]

    def rows(n):
        return pl.BlockSpec((count, n), lambda j, *_: (j, 0))

    def mixed_spec(k):
        return pl.BlockSpec((own, count), lambda j, *_: (0, j ^ k))

    return kernel_call(
        feed_forward_kernel,
        (4,),
        [
            *[fixed_spec((count, width))] * 8,
            fixed_spec(mods.shape),
            pl.BlockSpec((per,) + col.shape[1:], lambda j, *_: (j, 0, 0)),
            *(mixed_spec(k) for k in range(4)),
            fixed_spec(w_out.shape),
            fixed_spec(w_up.shape),
        ],
        [
            rows(width),
            rows(columns),
            rows(columns // 2),
            rows(width),
            whole_spec((count, width)),
        ],
        [
            shaped((total, width), BF),
            shaped((total, columns), BF),
            shaped((total, columns // 2), BF),
            shaped((total, width), BF),
            shaped((count, width), F32),
        ],
        "feed_forward",
        [
            pltpu.VMEM((4 * own, count), BF),
            pltpu.VMEM((count, width), BF),
            pltpu.VMEM((count, width), BF),
            pltpu.VMEM((count, width), F32),
            pltpu.VMEM((count, 4 * width), F32),
            pltpu.VMEM((count, columns), F32),
        ],
    )(me, *tokens, *upstream, mods, col, *mixed, w_out, w_up)


def feed_backward_kernel(
    me_ref, gate_up_ref, hidden_ref, fed_grad_ref, w_up_ref, w_down_ref, *rest
):
    grad_ref, m2_ref, fed_ref, held_ref = rest[-4:]
    held_ref[...] = dot(fed_grad_ref[...], w_down_ref[...], 1, 1)
    count, units = held_ref.shape

    def back(at):
        hidden_grad = held_ref[at, :]
        slope, silu = gate_up_ref[at, :units], gate_up_ref[at, units:]
        grad_ref[at, :units] = (hidden_grad * slope.astype(F32)).astype(BF)
        grad_ref[at, units:] = (hidden_grad * silu.astype(F32)).astype(BF)

    by_rows(count, back)
    m2_ref[...] = dot(grad_ref[...], w_up_ref[...], 1, 1).astype(BF)
    fed_ref[...] = dot(hidden_ref[...], w_down_ref[...]).astype(BF)


def feed_backward(me, gate_up, hidden, fed_grad, w_up, w_down, at, held):
    total, columns = gate_up.shape
    width = fed_grad.shape[1]
    count = total // 4

    def rows(n):
        return pl.BlockSpec((count, n), lambda j, *_: (2 * j + at, 0))

    out = pl.BlockSpec((count, width), lambda j, *_: (j, 0))
    in_specs = [
        rows(columns),
        rows(columns // 2),
        rows(width),
        fixed_spec(w_up.shape),
        fixed_spec(w_down.shape),
    ]
    operands = [gate_up, hidden, fed_grad, w_up, w_down]
    alias = {}
    if held is not None:
        alias = {1 + len(operands): 0}
        operands.append(held)
        in_specs.append(pl.BlockSpec(memory_space=pl.ANY))
    return kernel_call(
        feed_backward_kernel,
        (2,),
        in_specs,
        [rows(columns), out, out],
        [
            shaped((total, columns), BF),
            shaped((2 * count, width), BF),
            shaped((2 * count, width), BF),
        ],
        "feed_backward",
        [pltpu.VMEM((count, columns // 2), F32)],
        alias,
    )(me, *operands)


def own_sums(me_ref, column, sums_ref, *terms):
    lane = lax.broadcasted_iota(I32, (column.shape[0], sums_ref.shape[0]), 1)
    members = (column - me_ref[FIRST] == lane).astype(BF)
    width = terms[0].shape[1]
    for at, term in enumerate(terms):
        sums_ref[:, at * width : (at + 1) * width] = dot(members, term[...], 0, 0).astype(BF)


def resid_kernel(
    me_ref, tokens_ref, upstream_ref, mods_ref, col_ref, attended_ref, near_ref, core_ref,
    side_ref, grad_ref, out_ref, sums_ref, token_mod_ref, gate_sum_ref, shift_sum_ref,
    scale_sum_ref,
):
    count, width = tokens_ref.shape
    column = col_ref[...].reshape(-1, 1)
    members = members_of(column, mods_ref.shape[0])
    token_mod_ref[:, :width] = dot(members, mods_ref[:, 2 * width : 3 * width])
    token_mod_ref[:, width:] = dot(members, mods_ref[:, 4 * width : 5 * width])

    def back(at):
        attended = attended_ref[at, :]
        resid = tokens_ref[at, :].astype(F32) + token_mod_ref[at, :width] * attended
        normed, inverse = layer_norm(resid)
        m2 = near_ref[at, :].astype(F32) + core_ref[at, :].astype(F32)
        m2 = m2 + side_ref[at, :].astype(F32)
        shift_sum_ref[at, :] = m2.astype(BF)
        scale_sum_ref[at, :] = (m2 * normed).astype(BF)
        grad = norm_back(m2 * (1.0 + token_mod_ref[at, width:]), normed, inverse)
        grad = grad + upstream_ref[at, :].astype(F32)
        grad_ref[at, :] = grad
        out_ref[at, :] = (token_mod_ref[at, :width] * grad).astype(BF)
        gate_sum_ref[at, :] = (grad * attended).astype(BF)

    by_rows(count, back)
    own_sums(me_ref, column, sums_ref, gate_sum_ref, shift_sum_ref, scale_sum_ref)


def resid_back(me, tokens, upstream, mods, col, attended, near, core, side, items):
    count, width = tokens.shape
    block = pl.BlockSpec((count, width), lambda i, *_: (0, 0))
    return kernel_call(
        resid_kernel,
        (1,),
        [
            block,
            block,
            whole_spec(mods.shape),
            pl.BlockSpec((col.shape[0] // 4,) + col.shape[1:], lambda i, *_: (0, 0, 0)),
            block,
            block,
            block,
            block,
        ],
        [block, block, whole_spec((items, 3 * width))],
        [
            shaped((count, width), F32),
            shaped((count, width), BF),
            shaped((items, 3 * width), BF),
        ],
        "resid_back",
        [pltpu.VMEM((count, 2 * width), F32)] + [pltpu.VMEM((count, width), BF)] * 3,
    )(me, tokens, upstream, mods, col, attended, near, core, side)


def output_kernel(
    me_ref, tokens_ref, upstream_ref, mods_ref, col_ref, attended_ref, near_ref, core_ref,
    side_ref, out_ref, sums_ref, token_mod_ref, gate_sum_ref,
):
    count, width = tokens_ref.shape
    column = col_ref[...].reshape(-1, 1)
    members = members_of(column, mods_ref.shape[0])
    token_mod_ref[:, :width] = dot(members, mods_ref[:, 2 * width : 3 * width])
    token_mod_ref[:, width:] = dot(members, mods_ref[:, 5 * width :])

    def add(at):
        fed = near_ref[at, :].astype(F32) + core_ref[at, :].astype(F32)
        fed = fed + side_ref[at, :].astype(F32)
        resid = tokens_ref[at, :].astype(F32) + token_mod_ref[at, :width] * attended_ref[at, :]
        out_ref[at, :] = (resid + token_mod_ref[at, width:] * fed).astype(BF)
        gate_sum_ref[at, :] = (upstream_ref[at, :].astype(F32) * fed).astype(BF)

    by_rows(count, add)
    own_sums(me_ref, column, sums_ref, gate_sum_ref)


def output(me, tokens, upstream, mods, col, attended, near, core, side, items):
    count, width = tokens.shape
    block = pl.BlockSpec((count, width), lambda i, *_: (0, 0))
    return kernel_call(
        output_kernel,
        (1,),
        [
            block,
            block,
            whole_spec(mods.shape),
            pl.BlockSpec((col.shape[0] // 4,) + col.shape[1:], lambda i, *_: (0, 0, 0)),
            block,
            block,
            block,
            block,
        ],
        [block, whole_spec((items, width))],
        [shaped((count, width), BF), shaped((items, width), BF)],
        "output",
        [pltpu.VMEM((count, 2 * width), F32), pltpu.VMEM((count, width), BF)],
    )(me, tokens, upstream, mods, col, attended, near, core, side)


def tokens_kernel(
    me_ref, tokens_ref, mods_ref, col_ref, resid_ref, near_ref, core_ref, side_ref, out_ref,
    scale_ref,
):
    count, width = tokens_ref.shape
    members = members_of(col_ref[...].reshape(-1, 1), mods_ref.shape[0])
    scale_ref[...] = dot(members, mods_ref[:, width : 2 * width])

    def back(at):
        normed, inverse = layer_norm(tokens_ref[at, :].astype(F32))
        m1 = near_ref[at, :].astype(F32) + core_ref[at, :].astype(F32)
        m1 = (m1 + side_ref[at, :].astype(F32)) * (1.0 + scale_ref[at, :])
        out_ref[at, :] = resid_ref[at, :] + norm_back(m1, normed, inverse)

    by_rows(count, back)


def tokens_back(me, tokens, mods, col, resid_grad, near, core, side):
    count, width = tokens.shape
    block = pl.BlockSpec((count, width), lambda i, *_: (0, 0))
    return kernel_call(
        tokens_kernel,
        (1,),
        [
            block,
            whole_spec(mods.shape),
            pl.BlockSpec((col.shape[0] // 4,) + col.shape[1:], lambda i, *_: (0, 0, 0)),
            block,
            block,
            block,
            block,
        ],
        block,
        shaped((count, width), F32),
        "tokens_back",
        [pltpu.VMEM((count, width), F32)],
    )(me, tokens, mods, col, resid_grad, near, core, side)


def mod_back_kernel(planes, items, me_ref, rows_ref, weight_ref, *refs):
    count = len(gather_steps(planes)) + 1
    pieces = refs[: 2 * count]
    grad_ref, terms_ref, gains_ref, held_ref = refs[2 * count :]
    more, width = refs[0].shape
    gains = jnp.zeros((1, width), F32)
    for at, step in enumerate(gather_steps(planes)):
        plane = plane_of(me_ref[PLACE] + step, planes)
        for other in range(2):
            refs = pieces[other * count + at : other * count + at + 2]
            if at == count - 2:
                value = jnp.concatenate(
                    [ref[ref.shape[0] - more // 2 :].astype(F32) for ref in refs], axis=0
                )
            else:
                value = refs[0][refs[0].shape[0] - more :].astype(F32)
            row = (2 * plane + (me_ref[CORE] ^ other)) * items
            row = pl.ds(pl.multiple_of(row, items), items)
            for part in range(weight_ref.shape[1] // width):
                held_ref[row, part * width : (part + 1) * width] = value[
                    part * items : (part + 1) * items
                ].astype(BF)
            at_gain = held_ref.shape[1] // width * items
            gains += value[at_gain : at_gain + 1]
    grad_ref[...] = dot(rows_ref[...], held_ref[...], 0, 0)
    terms_ref[...] = dot(held_ref[...], weight_ref[...], 1, 1).astype(BF)
    gains_ref[...] = gains


def mod_back(me, rows, weight, own, other, planes, items):
    pieces = list(own) + list(other)
    outs = [shaped(weight.shape, F32), shaped(rows.shape, BF), shaped((1, own[0].shape[1]), F32)]
    return kernel_call(
        functools.partial(mod_back_kernel, planes, items),
        (1,),
        [whole_spec(v.shape) for v in (rows, weight, *pieces)],
        [whole_spec(v.shape) for v in outs],
        outs,
        "mod_back",
        [pltpu.VMEM((rows.shape[0], weight.shape[1]), BF)],
    )(me, rows, weight, *pieces)


def body(
    tokens,
    condition,
    lengths,
    positions,
    query_gain,
    key_gain,
    attend_in,
    attend_out,
    feed_in,
    feed_out,
    modulate_weight,
    cotangent,
):
    ndp, nmod = lax.axis_size("dp"), lax.axis_size("mod")
    planes = ndp // 2
    half = planes // 2
    dp, mod = lax.axis_index("dp"), lax.axis_index("mod")
    core, plane, side = dp % 2, dp // 2, mod % 2
    own_seqs, items_seq = lengths.shape
    own_count, width = tokens.shape
    count = own_count // own_seqs
    seqs = 4 * own_seqs
    head = query_gain.shape[0]
    heads = width // head // 4
    cls = 2 * side + core
    own_items = own_seqs * items_seq
    dp_items = condition.shape[0]
    ringed = nmod == 2 and attend_out.shape[0] == head
    hid = feed_out.shape[0] // 2
    place = jnp.where(plane % 2 == 0, plane // 2, planes - 1 - plane // 2)
    first_item = core * dp_items + mod * own_items
    me = jnp.stack([side, core, place, cls, first_item]).astype(I32)

    def relate(value, k):
        pairs = [
            (d * nmod + m, (d ^ (k >> 1)) * nmod + (m ^ (k & 1)))
            for d in range(ndp)
            for m in range(nmod)
        ]
        return lax.ppermute(value, ("dp", "mod"), pairs)

    def swap_core(value):
        return relate(value, 2)

    def swap_side(value):
        return relate(value, 1)

    def pick(which, pair0, pair1):
        return jnp.where(which == 0, pair0, pair1)

    def ordered(which, own, other):
        return pick(which, own, other), pick(which, other, own)

    def static_plane(ring):
        ring %= planes
        return 2 * ring if ring < half else 2 * (planes - 1 - ring) + 1

    def hop(value, step):
        pairs = [
            (2 * static_plane(r) + c, 2 * static_plane(r + step) + c)
            for r in range(planes)
            for c in range(2)
        ]
        return lax.ppermute(value, "dp", pairs)

    class Gather:
        def __init__(self, block, cut=None):
            self.pieces = [block]
            self.cut = block.shape[0] // 32 * 16 if cut is None else cut
            self.ahead = self.behind = block
            self.step = 0

        def go(self):
            self.step += 1
            if self.step == half:
                self.ahead, self.behind = self.ahead[: self.cut], self.behind[self.cut :]
            self.ahead, self.behind = hop(self.ahead, 1), hop(self.behind, -1)
            self.pieces += [self.ahead, self.behind]

    class Scatter:
        def __init__(self, blocks, name, along=None):
            self.blocks, self.name = blocks, name
            self.rows = blocks.shape[1]
            self.cut = self.rows // 32 * 16
            self.more = 0 if along is None else along.shape[0]
            self.pieces = [along]
            self.step = half
            if name:
                self.ahead, self.behind = ring_first(
                    me, blocks, along, self.cut, name + "_first"
                )
            else:
                far = self.take(half)
                self.ahead, self.behind = far[: self.cut], far[self.cut :]

        def take(self, step):
            start = (plane_of(place + step, planes), 0, 0)
            return lax.dynamic_slice(self.blocks, start, (1,) + self.blocks.shape[1:])[0]

        def go(self):
            self.hop()
            self.add()

        def hop(self):
            self.ahead, self.behind = hop(self.ahead, 1), hop(self.behind, -1)
            self.pieces += [self.ahead, self.behind]
            self.step -= 1

        def add(self):
            if self.step == 0:
                return
            cut = self.cut if self.step == half - 1 else 0
            if self.name:
                self.ahead, self.behind = ring_add(
                    me,
                    self.blocks,
                    self.ahead,
                    self.behind,
                    self.step,
                    cut,
                    self.more // 2 if self.step == 1 else self.more,
                    self.name,
                )
                return
            mine = self.take(self.step).astype(F32), self.take(-self.step).astype(F32)
            if cut:
                self.ahead = jnp.pad(self.ahead, ((0, self.rows - cut), (0, 0)))
                self.behind = jnp.pad(self.behind, ((cut, 0), (0, 0)))
            self.ahead = (mine[0] + self.ahead.astype(F32)).astype(BF)
            self.behind = (mine[1] + self.behind.astype(F32)).astype(BF)

        def last(self):
            return self.ahead, self.behind

        def result(self):
            return self.take(0).astype(F32) + self.ahead.astype(F32) + self.behind.astype(F32)

    def tie(rings, *values):
        state = [v for ring in rings for v in (ring.ahead, ring.behind)]
        out = list(lax.optimization_barrier(tuple(state) + values))
        for at, ring in enumerate(rings):
            ring.ahead, ring.behind = out[2 * at : 2 * at + 2]
        return out[2 * len(rings) :]

    def gather_whole(weight):
        return lax.all_gather(
            lax.all_gather(weight, "mod", axis=1, tiled=True), "dp", axis=0, tiled=True
        )

    def scatter_whole(padded):
        padded = lax.psum_scatter(padded.astype(BF), "mod", scatter_dimension=1, tiled=True)
        return lax.psum_scatter(padded, "dp", scatter_dimension=0, tiled=True).astype(F32)

    def stack_other_core(value):
        return jnp.stack(ordered(core, value, swap_core(value)))

    def group(value):
        other = swap_side(value)
        return [value, other, swap_core(value), swap_core(other)]

    columns_in = attend_in.shape[1]
    rows = feed_in.shape[0]
    out_slot = lambda index: lax.rem(index, 2) * half + index // 2
    cond_float = condition.astype(F32)
    silu_cond = jax.nn.silu(cond_float).astype(BF)
    mod_cols = modulate_weight.shape[1]
    small = jnp.pad(lengths, ((0, 0), (0, own_count - items_seq)))
    small = jnp.concatenate([positions, small], axis=0)
    quarter = head // 4
    entry = jnp.arange(head, dtype=I32)
    freq = jnp.power(10000.0, -(entry % quarter).astype(F32) / quarter)
    freq = jnp.broadcast_to(freq[:, None], (head, count))

    if ringed:
        silu_rows = lax.all_to_all(silu_cond, "dp", split_axis=1, concat_axis=0, tiled=True)
        silu_rows, attend_in_, feed_out_ = tie([], silu_rows, attend_in, feed_out)
        parts = sort_columns(me, attend_in_, head, lambda s: (s // 2, s % 2), "sort_in")
        keep = pick(side, feed_out_[:hid], feed_out_[hid:])
        came = swap_side(pick(side, feed_out_[hid:], feed_out_[:hid]))
        parts = [parts[0]] + [relate(parts[k], k) for k in (1, 2, 3)]
        kept, sent = mod_part(me, silu_rows, modulate_weight, planes)
        ring_a = Gather(make_unit(me, parts, [attend_out, keep, came], "unit_in"))
        kept, sent, small, tokens_ = tie([ring_a], kept, sent, small, tokens)
        ring_a.go()
        small_side = swap_side(small)
        tokens_side = swap_side(tokens_)
        ring_m = Scatter((kept + swap_core(sent).astype(F32)).astype(BF), "")
        small_side, feed_in_ = tie([ring_a, ring_m], small_side, feed_in)
        ring_a.go()
        ring_m.hop()
        small = [small, small_side, swap_core(small), swap_core(small_side)]
        parts = sort_columns(me, feed_in_, hid, lambda s: (s % 2, s // 2), "sort_up")
        tokens_side, cotangent_, *parts = tie([ring_a, ring_m], tokens_side, cotangent, *parts)
        ring_m.add()
        ring_a.go()
        ring_m.hop()
        parts = [parts[0]] + [relate(parts[k], k) for k in (1, 2, 3)]
        tokens_g = [tokens, tokens_side, swap_core(tokens), swap_core(tokens_side)]
        upstream_side = swap_side(cotangent_)
        small = tie([ring_a, ring_m], *small)
        ring_m.add()
        ring_a.go()
        ring_m.hop()
        ring_b = Gather(make_unit(me, parts, [], "unit_up"))
        tabled = make_tables(me, freq, small, seqs, dp_items, own_items)
        tabled = tie([ring_a, ring_b, ring_m], *tabled)
        ring_m.add()
        ring_b.go()
        ring_m.hop()
        ring_a.pieces[-2:] = [ring_a.ahead, ring_a.behind]
        w_in, w_out, w_down = assemble(
            me, ring_a.pieces, planes, 2 * rows, 3 * heads * head, "join_in"
        )
        w_out, w_in, upstream_side = tie([ring_b, ring_m], w_out, w_in, upstream_side)
        mods = group(ring_m.result().astype(BF))
        ring_b.go()
        w_out, *mods = tie([ring_b], w_out, *mods)
        mods = join_mods(me, mods)
        ring_b.go()
        w_out = w_out.reshape(2, half * head, width // 2)
        w_out_side = swap_side(w_out)
    else:
        silu_rows = lax.all_to_all(silu_cond, "dp", split_axis=1, concat_axis=0, tiled=True)
        partial = dot(silu_rows, modulate_weight)
        tabled = make_tables(me, freq, group(small), seqs, dp_items, own_items)
        tokens_g = group(tokens)
        upstream_g = group(cotangent)
        mods = lax.psum_scatter(partial, "dp", scatter_dimension=0, tiled=True).astype(BF)
        mods = lax.all_gather(mods, "mod", axis=1, tiled=True)
        mods = stack_other_core(mods).reshape(2 * dp_items, 6 * width)
        w_in = gather_whole(attend_in).reshape(width, 3 * heads, 4, head)
        w_in = lax.dynamic_index_in_dim(w_in, cls, 2, False).reshape(width, 3 * heads * head)
        w_out = gather_whole(attend_out).reshape(heads, 4, head, width)
        w_out = jnp.swapaxes(w_out, 0, 1).reshape(4, heads * head, width)
        share = 2 * core + side
        w_up = gather_whole(feed_in).reshape(width, 2 * planes, 4, hid)
        w_up = lax.dynamic_index_in_dim(w_up, share, 2, False).reshape(width, 2 * planes * hid)
        w_down = gather_whole(feed_out).reshape(planes, 4, hid, width)
        w_down = lax.dynamic_index_in_dim(w_down, share, 1, False).reshape(planes * hid, width)
    hidden_units = planes * hid

    cosine, sine, item_row, col = tabled
    item_col = col
    qg = jnp.broadcast_to(query_gain[:, None], (head, count))
    kg = jnp.broadcast_to(key_gain[:, None], (head, count))
    modded_one, raw, low, mixed = attend_forward(
        me, tokens_g, mods, w_in, cosine, sine, qg, kg, item_row, item_col, heads
    )
    if ringed:
        mixed, w_out_side = tie([ring_b], mixed, w_out_side)
        ring_b.go()
        mixed_side = swap_side(mixed)
        mixed_core = swap_core(mixed)
        upstream_g = [
            cotangent, upstream_side, swap_core(cotangent), swap_core(upstream_side)
        ]
        w_out = join_out(me, [w_out, w_out_side, swap_core(w_out), swap_core(w_out_side)])
        mixed_side, w_out, mixed_core, *upstream_g = tie(
            [ring_b], mixed_side, w_out, mixed_core, *upstream_g
        )
        ring_b.pieces[-2:] = [ring_b.ahead, ring_b.behind]
        (w_up,) = assemble(me, ring_b.pieces, planes, 2 * rows, ring_b.pieces[0].shape[1], "join_up")
    else:
        mixed_side = swap_side(mixed)
        mixed_core = swap_core(mixed)
    mixed_all = (mixed, mixed_side, mixed_core, swap_core(mixed_side))
    modded_two, gate_up, hidden, fed_grad, own_attended = feed_forward(
        me, tokens_g, upstream_g, mods, col, mixed_all, w_out.reshape(width, width), w_up
    )

    def two_cores(part):
        part = part.reshape(2, own_count, width)
        return (part[0].astype(F32) + swap_core(part[1]).astype(F32)).astype(BF)

    gate_up_grad, m2_far, fed_far = feed_backward(
        me, gate_up, hidden, fed_grad, w_up, w_down, 1, None
    )
    m2_far = two_cores(m2_far)
    if ringed:
        gate_up_grad, m2_far, fed_far = tie([], gate_up_grad, m2_far, fed_far)
    m2_side = swap_side(m2_far)
    gate_up_grad, m2_near, fed_near = feed_backward(
        me, gate_up, hidden, fed_grad, w_up, w_down, 0, gate_up_grad
    )
    if ringed:
        gate_up_grad, m2_near, fed_near = tie([], gate_up_grad, m2_near, fed_near)
        m2_core = swap_core(m2_near[own_count:])
        grads = feed_grads(me, modded_two, gate_up_grad, hidden, fed_grad, planes)
        ring_u = Scatter(grads, "up_add")
        fed_far = two_cores(fed_far)
        m2_side, m2_core, fed_near, fed_far = tie([ring_u], m2_side, m2_core, fed_near, fed_far)
        ring_u.hop()
    else:
        m2_core = swap_core(m2_near[own_count:])
        fed_far = two_cores(fed_far)
    resid_grad, attended_grad, early_sums = resid_back(
        me, tokens, cotangent, mods, col, own_attended, m2_near, m2_core, m2_side, own_items
    )
    side_grad = swap_side(attended_grad)
    core_grad = swap_core(attended_grad)
    shared = (
        w_out, w_in, raw, low, cosine, sine, qg, kg, item_row, item_col, tokens_g,
        2 * dp_items, heads,
    )
    projected_grad, m1_near, qg_near, kg_near, sums_near = attend_backward(
        me, attended_grad, core_grad, *shared, 0, None
    )
    if ringed:
        projected_grad, side_grad, fed_far, m1_near, fed_near = tie(
            [ring_u], projected_grad, side_grad, fed_far, m1_near, fed_near
        )
        ring_u.add()
    both_grad = swap_core(side_grad)
    fed_core = swap_core(fed_near[own_count:])
    if ringed:
        projected_grad, both_grad, fed_far = tie([ring_u], projected_grad, both_grad, fed_far)
        ring_u.hop()
    fed_side = swap_side(fed_far)
    projected_grad, m1_far, qg_far, kg_far, sums_far = attend_backward(
        me, side_grad, both_grad, *shared, 1, projected_grad
    )
    if ringed:
        projected_grad, m1_far, sums_far, fed_side, m1_near = tie(
            [ring_u], projected_grad, m1_far, sums_far, fed_side, m1_near
        )
        ring_u.add()
    gains = jnp.stack([jnp.sum(qg_near + qg_far, axis=1), jnp.sum(kg_near + kg_far, axis=1)])
    sums = sums_near + sums_far
    keep, came = sums[:dp_items], sums[dp_items:]
    sums = pick(core, keep, came) + swap_core(pick(core, came, keep))

    def as_row(values):
        top = lax.reduce_precision(values, 8, 7)
        row = jnp.concatenate([top.reshape(-1), (values - top).reshape(-1)]).astype(BF)
        return jnp.pad(row, (0, 2 * width - row.shape[0]))[None]

    def from_rows(row):
        return (row[: 2 * head] + row[2 * head : 4 * head]).reshape(2, head)

    if not ringed:
        block_out, late_sums = output(
            me, tokens, cotangent, mods, col, own_attended, fed_near, fed_core, fed_side, own_items
        )
        early = jnp.concatenate([early_sums, late_sums], axis=1)

    if ringed:
        gain_row = as_row(gains)
        found = swap_side(jnp.concatenate([sums.astype(BF), gain_row], axis=0))
        projected_grad, m1_far, m1_near = tie([ring_u], projected_grad, m1_far, m1_near)
        ring_u.hop()
        grads = attend_grads(
            me,
            modded_one,
            projected_grad,
            mixed,
            mixed_side,
            (attended_grad, side_grad, core_grad, both_grad),
            planes,
        )
        block_out, late_sums = output(
            me, tokens, cotangent, mods, col, own_attended, fed_near, fed_core, fed_side,
            own_items,
        )
        early = jnp.concatenate([early_sums, late_sums], axis=1)
        early_side = swap_side(early)
        grads, m1_far, m1_near, found, early, early_side = tie(
            [ring_u], grads, m1_far, m1_near, found, early, early_side
        )
        ring_u.add()
        sums = (sums + found[:-1].astype(F32)).astype(BF)
        gains = from_rows(jnp.sum(gain_row.astype(F32) + found[-1:].astype(F32), axis=0))
        early = jnp.concatenate(ordered(side, early, early_side), axis=0)
        parts = [
            pick(side, sums[:, :width], early[:, width : 2 * width]),
            pick(side, sums[:, width:], early[:, 2 * width : 3 * width]),
            pick(side, early[:, :width], early[:, 3 * width :]),
            as_row(gains)[:, :width],
        ]
        along = jnp.concatenate(parts, axis=0)
        along = jnp.pad(along, ((0, 64 - along.shape[0]), (0, 0)))
        ring_i = Scatter(grads, "in_add", along)
        m1_far, m1_near = tie([ring_u, ring_i], m1_far, m1_near)
        ring_u.hop()
        ring_i.hop()
        m1_far = two_cores(m1_far)
        m1_core = swap_core(m1_near[own_count:])
        m1_far, m1_core = tie([ring_u, ring_i], m1_far, m1_core)
        ring_i.add()
        ring_i.hop()
        m1_side = swap_side(m1_far)
        *up_parts, keep, came = split_sum(
            me, ring_u.blocks, *ring_u.last(), rows, planes * hid, hid, "up_split"
        )
        m1_side, came, *up_parts = tie([ring_i], m1_side, came, *up_parts)
        ring_i.add()
        ring_i.hop()
        up_parts = [up_parts[0]] + [relate(up_parts[k], k) for k in (1, 2, 3)]
        came = swap_side(came)
        tokens_grad = tokens_back(
            me, tokens, mods, col, resid_grad, m1_near, m1_core, m1_side
        )
        (tokens_grad,) = tie([ring_i], tokens_grad)
        ring_i.add()
        ring_i.hop()
        feed_in_grad = unsort_columns(
            me, up_parts, hid, lambda s: (s % 2, s // 2), "unsort_up"
        )
        feed_out_grad = jnp.concatenate(ordered(side, keep, came), axis=0).astype(F32)
        other = [swap_core(piece) for piece in ring_i.pieces[:-2]]
        feed_in_grad, feed_out_grad, *other = tie([ring_i], feed_in_grad, feed_out_grad, *other)
        ring_i.pieces[-2:] = [ring_i.ahead, ring_i.behind]
        other += [swap_core(ring_i.ahead), swap_core(ring_i.behind)]
        *parts, attend_out_grad = split_sum(
            me, ring_i.blocks, *ring_i.last(), head, columns_in // 4, 0, "in_split"
        )
        other[-2], other[-1], *parts = tie([], other[-2], other[-1], *parts)
        modulate_grad, cond_terms, gains = mod_back(
            me, silu_rows, modulate_weight, ring_i.pieces, other, planes, dp_items
        )
        gains = from_rows(gains[0])
        cond_terms, *parts = tie([], cond_terms, *parts)
        parts = [parts[0]] + [relate(parts[k], k) for k in (1, 2, 3)]
        attend_in_grad = unsort_columns(
            me, parts, head, lambda s: (s // 2, s % 2), "unsort_in"
        )
    else:
        m1_side = swap_side(two_cores(m1_far))
        m1_core = swap_core(m1_near[own_count:])

        def padded(shape, value, axis, which):
            zero = jnp.zeros(shape, value.dtype)
            return lax.dynamic_update_index_in_dim(zero, value, which, axis)

        down_grad = weight_grad(me, hidden, fed_grad, hidden_units // 2, "down_grad")
        up_grad = weight_grad(me, modded_two, gate_up_grad, width // 3, "up_grad")
        grad = down_grad.reshape(planes, hid, width)
        grad = padded((planes, 4, hid, width), grad, 1, share)
        feed_out_grad = scatter_whole(grad.reshape(4 * hidden_units, width))
        grad = up_grad.reshape(width, 2 * planes, hid)
        grad = padded((width, 2 * planes, 4, hid), grad, 2, share)
        feed_in_grad = scatter_whole(grad.reshape(width, 8 * hidden_units))
        columns = [
            pick(side, value[:, : width // 2], value[:, width // 2 :])
            for value in (attended_grad, side_grad, core_grad, both_grad)
        ]
        near_rows = dot(mixed, jnp.concatenate(columns, axis=0))
        far_rows = dot(mixed_side, jnp.concatenate([columns[k] for k in (1, 0, 3, 2)], axis=0))
        out_grad = jnp.stack(ordered(side, near_rows, far_rows)).astype(BF)
        in_grad = weight_grad(me, modded_one, projected_grad, width // 3, "in_grad")
        grad = out_grad.reshape(2, heads, head, width // 2)
        grad = jnp.swapaxes(grad, 0, 1)
        grad = padded((heads, 2, head, 2, width // 2), grad, 3, side)
        grad = padded((heads, 2, 2, head, 2, width // 2), grad, 2, core)
        attend_out_grad = scatter_whole(grad.reshape(width, width))
        grad = in_grad.reshape(width, 3 * heads, head)
        grad = padded((width, 3 * heads, 4, head), grad, 2, cls)
        attend_in_grad = scatter_whole(grad.reshape(width, 3 * width))

    if not ringed:
        tokens_grad = tokens_back(
            me, tokens, mods, col, resid_grad, m1_near, m1_core, m1_side
        )

    if not ringed:
        sums = sums + swap_side(sums)
        found = lax.dynamic_slice_in_dim(sums, mod * own_items, own_items, 0).astype(BF)
        mod_grad = jnp.concatenate([found, early], axis=1)
        mod_grad = lax.all_to_all(mod_grad, "mod", split_axis=1, concat_axis=0, tiled=True)
        mod_grad = lax.all_gather(mod_grad, "dp", axis=0, tiled=True)
        gains = lax.psum(gains, ("dp", "mod"))
        modulate_grad = dot(silu_rows, mod_grad, 0, 0)
        cond_terms = dot(mod_grad, modulate_weight, 1, 1).astype(BF)
    cond_terms = lax.all_to_all(cond_terms, "dp", split_axis=0, concat_axis=1, tiled=True)
    own_width = width // nmod
    if ringed:
        left, right = cond_terms[:, :own_width], cond_terms[:, own_width:]
        came = swap_side(pick(side, right, left))
        cond_share = pick(side, left, right).astype(F32) + came.astype(F32)
    else:
        cond_share = lax.psum_scatter(
            cond_terms, "mod", scatter_dimension=1, tiled=True
        ).astype(F32)
    cond_cols = lax.dynamic_slice_in_dim(cond_float, mod * own_width, own_width, 1)
    cond_sigma = jax.nn.sigmoid(cond_cols)
    condition_grad = cond_share * cond_sigma * (1.0 + cond_cols * (1.0 - cond_sigma))
    return (
        block_out,
        tokens_grad,
        condition_grad,
        gains[0],
        gains[1],
        attend_in_grad,
        attend_out_grad,
        feed_in_grad,
        feed_out_grad,
        modulate_grad,
    )


def solution(mesh):
    rows = P(("dp", "mod"), None)
    both = P("dp", "mod")
    return jax.shard_map(
        body,
        mesh=mesh,
        in_specs=(
            rows,
            P("dp", None),
            rows,
            P(None, ("dp", "mod")),
            P(),
            P(),
            both,
            both,
            both,
            both,
            both,
            rows,
        ),
        out_specs=(rows, rows, both, P(), P(), both, both, both, both, both),
        check_vma=False,
    )
```
